256 devices in a mesh: ctx: 32 (over x, z), tp: 8 (over y, core).
Axes of the slice: x: 4, y: 4, z: 8, core: 2. Of those that a mesh axis runs over, the one named last changes fastest.
Arguments:
- moe_input: bfloat16 [4096, 6400], P('ctx', 'tp'), may hold values from -6 to 6
- out_grad: bfloat16 [4096, 6400], P('ctx', 'tp'), may hold values from -6 to 6
- route_prob: float32 [4096, 2], P('ctx'), may hold values from 0.2 to 1
- route_ids: int32 [4096, 2], P('ctx'), may hold values from 0 to 31, as said below
- route_counts: int32 [32, 32], P('ctx'), may hold values from 0 to 16, as said below
- w_gate: bfloat16 [32, 6400, 1536], P('ctx', 'tp'), may hold values from -0.078125 to 0.078125
- w_up: bfloat16 [32, 6400, 1536], P('ctx', 'tp'), may hold values from -0.078125 to 0.078125
- w_down: bfloat16 [32, 1536, 6400], P('ctx', None, 'tp'), may hold values from -0.15625 to 0.15625
- out_weight: bfloat16 [6400, 8192], P('ctx', 'tp'), may hold values from -0.078125 to 0.078125
- ssd_input: bfloat16 [4096, 8192], P('ctx', 'tp'), may hold values from -0.19921875 to 0.19921875
- input_map: bfloat16 [4096, 1024], P('ctx', 'tp'), may hold values from -0.29882812 to 0.29882812
- output_map: bfloat16 [4096, 1024], P('ctx', 'tp'), may hold values from -0.29882812 to 0.29882812
- log_decay: float32 [4096, 128], P('ctx', 'tp'), may hold values from -2.2 to 0
Outputs:
- input_grad: bfloat16 [4096, 6400], P('ctx', 'tp')
- scan_grad: bfloat16 [4096, 8192], P('ctx', 'tp')
- in_map_grad: float32 [4096, 1024], P('ctx', 'tp')
- out_map_grad: float32 [4096, 1024], P('ctx', 'tp')
The draws below stay inside these ranges and needn't reach their ends.
Inputs may be any that keep to these rules, and one draw needn't show every extreme that they name: `route_ids`: each row names 2 different experts. Among the 128 rows of one device (rows c * 128 to (c + 1) * 128 - 1) no expert is named more than 16 times, and in the rows of every device some expert is named exactly 16 times. route_counts[c, e] is the most entries among rows c * 128 to (c + 1) * 128 - 1 of route_ids that expert e accepts; it never exceeds the number of those rows that name e.
All inputs are finite; a program needn't handle non-finite values.
Results may differ from the reference program's by a relative error of at most 0.027.
Values may be sent and summed in bfloat16 or wider, within the bound.
A program may use at most 128 MiB of HBM per device.

```python
import jax
import jax.numpy as jnp
from jax import lax

D = 6400
F = 1536
TOP = 2
H_DEV = 16
P_SIZE = 64
STATE = 128
TOK = 128
SEQUENCE_TOKENS = 4096
HEADS = 128
GROUPS = 8
EXPERTS = 32
CAP = 16
N_TP = 8


def route_table(key):
    blocks = SEQUENCE_TOKENS // TOK
    mean_load = TOK * TOP // EXPERTS
    pairs = EXPERTS // 2
    order_key, shift_key, perm_key = jax.random.split(key, 3)
    limit_key = jax.random.fold_in(key, 11)
    pick_key, level_key = jax.random.split(limit_key, 2)
    order = jax.random.permutation(order_key, EXPERTS)
    shifts = jax.random.randint(shift_key, (blocks, pairs), 0, mean_load + 1)
    shifts = shifts.at[:, 0].set(mean_load)
    counts = jnp.full((blocks, EXPERTS), mean_load, jnp.int32)
    counts = counts.at[:, order[:pairs]].add(shifts).at[:, order[pairs:]].add(-shifts)
    bounds = jnp.cumsum(counts, axis=1)
    positions = jnp.arange(TOK * TOP, dtype=jnp.int32)
    listed = jnp.sum((positions[None, :, None] >= bounds[:, None, :]).astype(jnp.int32), axis=2)
    row_orders = jax.vmap(lambda subkey: jax.random.permutation(subkey, TOK))(jax.random.split(perm_key, blocks))
    picks = row_orders[:, :, None] + TOK * jnp.arange(TOP, dtype=jnp.int32)[None, None, :]
    chosen = jnp.take_along_axis(listed, picks.reshape(blocks, TOK * TOP), axis=1)
    limited = jax.random.randint(pick_key, (blocks, EXPERTS), 0, 3) == 0
    keep_full = (jnp.arange(EXPERTS, dtype=jnp.int32)[None, :] == order[0]).astype(jnp.int32)
    limited = jnp.logical_and(limited, keep_full == 0)
    levels = jax.random.randint(level_key, (blocks, EXPERTS), 0, CAP)
    capacity = jnp.where(limited, jnp.minimum(counts, levels), counts).astype(jnp.int32)
    return (chosen.reshape(blocks * TOK, TOP), capacity)


def draw_route_ids(key, part):
    return route_table(key)[0]


def draw_route_counts(key, part):
    return route_table(key)[1]


def draw_log_decay(key, part):
    key = jax.random.fold_in(key, 7)
    key_list = jax.random.split(key, 7)
    slow_share = 0.5
    slow = jax.random.uniform(key_list[0], (HEADS,)) < slow_share
    slow_rate = jnp.exp(jax.random.uniform(key_list[1], (HEADS,), minval=jnp.log(0.1), maxval=jnp.log(0.6))) / SEQUENCE_TOKENS
    fast_rate = jnp.exp(jax.random.uniform(key_list[2], (HEADS,), minval=jnp.log(1.0 / 50.0), maxval=jnp.log(1.0 / 30.0)))
    decay_rate = jnp.where(slow, slow_rate, fast_rate)
    block_multiplier = jnp.exp(jax.random.uniform(key_list[3], (SEQUENCE_TOKENS // TOK, HEADS), minval=-0.693, maxval=0.693))
    block_multiplier = jnp.repeat(block_multiplier, TOK, axis=0)
    position_multiplier = jnp.exp(jax.random.uniform(key_list[4], (SEQUENCE_TOKENS, HEADS), minval=-0.5, maxval=0.5))
    spike_position = jax.random.randint(key_list[5], (3,), 0, SEQUENCE_TOKENS)
    nesting_level = jax.random.uniform(key_list[6], (3, HEADS), minval=0.223, maxval=0.693)
    match_count = (jnp.arange(SEQUENCE_TOKENS)[:, None] == spike_position[None, :]).astype(jnp.float32)
    spike_amount = jnp.sum(match_count[:, :, None] * nesting_level[None, :, :], axis=1)
    return -(decay_rate[None, :] * block_multiplier * position_multiplier) - spike_amount


def shard_levels(stream_key, dims, cuts, low, largest):
    def one(axis_at, blocks):
        draws = jax.random.uniform(jax.random.fold_in(jax.random.fold_in(stream_key, 6), axis_at), (blocks,), jnp.float32, low / len(cuts), largest / len(cuts))
        return jnp.repeat(jnp.exp(draws), dims[axis_at] // blocks).reshape((-1,) + (1,) * (len(dims) - axis_at - 1))

    level = one(*cuts[0])
    for cut in cuts[1:]:
        level = level * one(*cut)
    return level


def noise(stream_key, dims, scale, bound, pieces=(), kind=jnp.bfloat16):
    drawn = scale * jax.random.normal(stream_key, dims, jnp.float32)
    if pieces:
        drawn = drawn * shard_levels(stream_key, dims, pieces, -0.22, 0.18)
    return jnp.clip(drawn, -bound, bound).astype(kind)


def setup_inputs(seed: int = 0) -> dict:
    streams_of = jax.random.split(jax.random.key(seed), 14)
    moe_input = noise(streams_of[0], (SEQUENCE_TOKENS, D), 1.0, 6.0, ((0, 32), (1, 8)))
    out_grad = noise(streams_of[1], (SEQUENCE_TOKENS, D), 1.0, 6.0, ((0, 32), (1, 8)))
    route_prob = jnp.clip(0.2 + 0.8 * jax.random.uniform(streams_of[2], (SEQUENCE_TOKENS, TOP), jnp.float32) ** shard_levels(streams_of[2], (SEQUENCE_TOKENS, TOP), ((0, 32),), -0.2, 0.2), 0.2, 1.0)
    route_ids = draw_route_ids(jax.random.fold_in(streams_of[13], 71), 0)
    route_counts = draw_route_counts(jax.random.fold_in(streams_of[13], 71), 0)
    w_gate = noise(streams_of[5], (EXPERTS, D, F), D ** -0.5, 0.078125, ((0, 32), (1, 8)))
    w_up = noise(streams_of[6], (EXPERTS, D, F), D ** -0.5, 0.078125, ((0, 32), (1, 8)))
    w_down = noise(streams_of[7], (EXPERTS, F, D), F ** -0.5, 0.15625, ((0, 32), (2, 8)))
    out_weight = noise(streams_of[8], (D, HEADS * P_SIZE), D ** -0.5, 0.078125, ((0, 32), (1, 8)))
    ssd_input = noise(streams_of[9], (SEQUENCE_TOKENS, HEADS * P_SIZE), 0.03, 0.19921875, ((0, 32), (1, 8)))
    input_map = noise(streams_of[10], (SEQUENCE_TOKENS, GROUPS * STATE), 0.05, 0.29882812, ((0, 32), (1, 8)))
    output_map = noise(streams_of[11], (SEQUENCE_TOKENS, GROUPS * STATE), 0.05, 0.29882812, ((0, 32), (1, 8)))
    log_decay = draw_log_decay(jax.random.fold_in(streams_of[13], 71), 0)
    return dict(moe_input=moe_input, out_grad=out_grad, route_prob=route_prob, route_ids=route_ids, route_counts=route_counts, w_gate=w_gate, w_up=w_up, w_down=w_down, out_weight=out_weight, ssd_input=ssd_input, input_map=input_map, output_map=output_map, log_decay=log_decay)


highest = lax.Precision.HIGHEST


def swiglu_back(pre_gate, pre_up, back):
    sigma = jax.nn.sigmoid(pre_gate)
    gate_grad = back * pre_up * sigma * (1.0 + pre_gate * (1.0 - sigma))
    up_grad = back * pre_gate * sigma
    return gate_grad.astype(jnp.bfloat16), up_grad.astype(jnp.bfloat16)


def block_sum(left, right):
    width = D // N_TP
    total = jnp.zeros((left.shape[0], right.shape[1]), jnp.float32)
    for part in range(N_TP):
        piece = jnp.dot(left[:, part * width:(part + 1) * width], right[part * width:(part + 1) * width], preferred_element_type=jnp.float32)
        total = total + lax.optimization_barrier(piece.astype(jnp.bfloat16)).astype(jnp.float32)
    return total


def decay_kernel(running):
    count = running.shape[0]
    later = (jnp.arange(count)[:, None] >= jnp.arange(count)[None, :])[None, :, :]
    spread = running.T[:, :, None] - running.T[:, None, :]
    return jnp.where(later, jnp.exp(jnp.where(later, spread, 0.0)), 0.0)


def local_terms(inputs, grads, in_map, out_map, running):
    kernel = decay_kernel(running)
    inner = jnp.einsum("thp,shp->hts", grads, inputs, precision=highest)
    weighted = kernel * inner
    affinity = jnp.einsum("tn,sn->ts", out_map, in_map, precision=highest)
    scan_part = jnp.einsum("hts,ts,thp->shp", kernel, affinity, grads, precision=highest)
    in_part = jnp.einsum("hts,tn->sn", weighted, out_map, precision=highest)
    out_part = jnp.einsum("hts,sn->tn", weighted, in_map, precision=highest)
    return scan_part, in_part, out_part


def group_grads(operands):
    inputs, grads, in_map, out_map, decay = operands
    blocks = SEQUENCE_TOKENS // TOK
    heads = decay.shape[1]
    inputs_b = inputs.reshape(blocks, TOK, heads, P_SIZE)
    grads_b = grads.reshape(blocks, TOK, heads, P_SIZE)
    in_b = in_map.reshape(blocks, TOK, STATE)
    out_b = out_map.reshape(blocks, TOK, STATE)
    running = jnp.cumsum(decay.reshape(blocks, TOK, heads), axis=1)
    totals = running[:, -1]
    zero_state = jnp.zeros((heads, P_SIZE, STATE), jnp.float32)

    def forward_step(state_before, block):
        grads_k, inputs_k, in_k, run_k, total_k = block
        out_inter = jnp.einsum("th,thp,hpn->tn", jnp.exp(run_k), grads_k, state_before, precision=highest)
        tail = jnp.exp(total_k[None, :] - run_k)
        state_local = jnp.einsum("sh,shp,sn->hpn", tail, inputs_k, in_k, precision=highest)
        return jnp.exp(total_k)[:, None, None] * state_before + state_local, out_inter

    def backward_step(grad_after, block):
        grads_k, inputs_k, in_k, out_k, run_k, total_k = block
        tail = jnp.exp(total_k[None, :] - run_k)
        in_inter = jnp.einsum("sh,shp,hpn->sn", tail, inputs_k, grad_after, precision=highest)
        scan_inter = jnp.einsum("sh,hpn,sn->shp", tail, grad_after, in_k, precision=highest)
        grad_local = jnp.einsum("th,thp,tn->hpn", jnp.exp(run_k), grads_k, out_k, precision=highest)
        return grad_local + jnp.exp(total_k)[:, None, None] * grad_after, (scan_inter, in_inter)

    _, out_inter = lax.scan(forward_step, zero_state, (grads_b, inputs_b, in_b, running, totals))
    _, (scan_inter, in_inter) = lax.scan(backward_step, zero_state, (grads_b, inputs_b, in_b, out_b, running, totals), reverse=True)
    scan_intra, in_intra, out_intra = jax.vmap(local_terms)(inputs_b, grads_b, in_b, out_b, running)
    return ((scan_intra + scan_inter).reshape(SEQUENCE_TOKENS, heads, P_SIZE), (in_intra + in_inter).reshape(SEQUENCE_TOKENS, STATE), (out_intra + out_inter).reshape(SEQUENCE_TOKENS, STATE))


def reference(moe_input, out_grad, route_prob, route_ids, route_counts, w_gate, w_up, w_down, out_weight, ssd_input, input_map, output_map, log_decay):
    entries = TOK * TOP
    blocks = SEQUENCE_TOKENS // TOK
    flat_ids = route_ids.reshape(blocks, entries)
    member = (flat_ids[:, :, None] == jnp.arange(EXPERTS, dtype=jnp.int32)[None, None, :]).astype(jnp.int32)
    entry_rank = jnp.sum((jnp.cumsum(member, axis=1) - member) * member, axis=2)
    allowed = jnp.sum(member * route_counts[:, None, :], axis=2)
    block_index = jnp.arange(blocks, dtype=jnp.int32)[:, None]
    slots_total = EXPERTS * blocks * CAP
    slot_index = jnp.where(entry_rank < allowed, (flat_ids * blocks + block_index) * CAP + entry_rank, slots_total).reshape(-1).astype(jnp.int32)
    token_index = jnp.repeat(jnp.arange(SEQUENCE_TOKENS, dtype=jnp.int32), TOP)
    slot_token = jnp.full((slots_total + 1,), SEQUENCE_TOKENS, jnp.int32).at[slot_index].set(token_index)[:slots_total]
    slot_prob = jnp.zeros((slots_total + 1,), jnp.float32).at[slot_index].set(route_prob.reshape(-1))[:slots_total]
    padded_rows = jnp.concatenate([moe_input, jnp.zeros((1, D), jnp.bfloat16)], axis=0)
    padded_grads = jnp.concatenate([out_grad, jnp.zeros((1, D), jnp.bfloat16)], axis=0)

    def expert_step(total, operands):
        tokens, probs, gate_w, up_w, down_w = operands
        rows = padded_rows[tokens]
        scaled = (probs[:, None] * padded_grads[tokens].astype(jnp.float32)).astype(jnp.bfloat16)
        pre_gate = block_sum(rows, gate_w)
        pre_up = block_sum(rows, up_w)
        back = block_sum(scaled, down_w.T)
        gate_grad, up_grad = swiglu_back(pre_gate, pre_up, back)
        entry_grad = (jnp.dot(gate_grad, gate_w.T, preferred_element_type=jnp.float32) + jnp.dot(up_grad, up_w.T, preferred_element_type=jnp.float32)).astype(jnp.bfloat16)
        return total.at[tokens].add(entry_grad.astype(jnp.float32)), None

    summed, _ = lax.scan(expert_step, jnp.zeros((SEQUENCE_TOKENS + 1, D), jnp.float32), (slot_token.reshape(EXPERTS, -1), slot_prob.reshape(EXPERTS, -1), w_gate, w_up, w_down))
    input_grad = (out_grad.astype(jnp.float32) + summed[:SEQUENCE_TOKENS]).astype(jnp.bfloat16)
    head_grad = jnp.dot(input_grad, out_weight, preferred_element_type=jnp.float32).astype(jnp.bfloat16)
    inputs = ssd_input.astype(jnp.float32).reshape(SEQUENCE_TOKENS, GROUPS, H_DEV, P_SIZE).transpose(1, 0, 2, 3)
    grads = head_grad.astype(jnp.float32).reshape(SEQUENCE_TOKENS, GROUPS, H_DEV, P_SIZE).transpose(1, 0, 2, 3)
    in_maps = input_map.astype(jnp.float32).reshape(SEQUENCE_TOKENS, GROUPS, STATE).transpose(1, 0, 2)
    out_maps = output_map.astype(jnp.float32).reshape(SEQUENCE_TOKENS, GROUPS, STATE).transpose(1, 0, 2)
    decays = log_decay.reshape(SEQUENCE_TOKENS, GROUPS, H_DEV).transpose(1, 0, 2)
    scan_all, in_all, out_all = lax.map(group_grads, (inputs, grads, in_maps, out_maps, decays))
    scan_grad = scan_all.transpose(1, 0, 2, 3).reshape(SEQUENCE_TOKENS, HEADS * P_SIZE).astype(jnp.bfloat16)
    in_map_grad = in_all.transpose(1, 0, 2).reshape(SEQUENCE_TOKENS, GROUPS * STATE)
    out_map_grad = out_all.transpose(1, 0, 2).reshape(SEQUENCE_TOKENS, GROUPS * STATE)
    return (input_grad, scan_grad, in_map_grad, out_map_grad)
```

```python
import functools

import jax
import jax.numpy as jnp
from jax import lax
from jax.experimental import pallas as pl
from jax.experimental.pallas import tpu as pltpu
from jax.sharding import PartitionSpec as P

MESH = pl.DeviceIdType.MESH
HIGHEST = lax.Precision.HIGHEST
bf16, f32, i32 = jnp.bfloat16, jnp.float32, jnp.int32
VMEM = pl.BlockSpec(memory_space=pltpu.VMEM)
ANY = pl.BlockSpec(memory_space=pl.ANY)
DMA = pltpu.SemaphoreType.DMA


def mm(a, b, ca=1, cb=0, precision=None):
    return lax.dot_general(
        a, b, (((ca,), (cb,)), ((), ())), precision=precision, preferred_element_type=f32
    )


def remote(src, dst, send, recv, axis, place):
    return pltpu.make_async_remote_copy(
        src_ref=src,
        dst_ref=dst,
        send_sem=send,
        recv_sem=recv,
        device_id={axis: place},
        device_id_type=MESH,
    )


def hello_ctx(n, me):
    barrier = pltpu.get_barrier_semaphore()

    def one(i, _):
        pl.semaphore_signal(
            barrier, inc=1, device_id={"ctx": lax.rem(me + i, n)}, device_id_type=MESH
        )
        return 0

    lax.fori_loop(1, n, one, 0)


def hello_tp(places):
    barrier = pltpu.get_barrier_semaphore()
    for place in places:
        pl.semaphore_signal(barrier, inc=1, device_id={"tp": place}, device_id_type=MESH)


def exchange(n, me, src, dst, send, recv, act):
    def one(i, _):
        to = lax.rem(me + i, n)
        back = lax.rem(me - i + n, n)
        if act == "start":
            remote(src.at[to], dst.at[me], send.at[i], recv.at[i], "ctx", to).start()
        else:
            copy = remote(src.at[to], dst.at[back], send.at[i], recv.at[i], "ctx", to)
            copy.wait_recv()
            copy.wait_send()
        return 0

    lax.fori_loop(1, n, one, 0)


def spread(columns, total):
    heads = columns.shape[1]
    size = total // heads
    put = lax.broadcasted_iota(i32, (heads, total), 1) // size == lax.broadcasted_iota(
        i32, (heads, total), 0
    )
    return mm(columns, put.astype(f32), precision=HIGHEST)


def scan_states(n, me, loc, out, totals, rows_per_head, backward):
    head = me * loc.shape[1] // rows_per_head
    lane = lax.broadcasted_iota(i32, totals.shape, 2)
    decay = jnp.exp(jnp.sum(jnp.where(lane == head, totals[...], 0.0), axis=2, keepdims=True))
    state = jnp.zeros(loc.shape[1:], f32)
    order = range(n - 1, -1, -1) if backward else range(n)
    for c in order:
        out[c] = state.astype(bf16)
        state = decay[c, 0:1, :] * state + loc[c].astype(f32)


def dispatch_kernel(
    n,
    x_ref,
    g_ref,
    ids_ref,
    prob_ref,
    counts_ref,
    u_ref,
    b_ref,
    c_ref,
    ld_ref,
    rows_ref,
    grads_ref,
    pick_ref,
    er_ref,
    tail_ref,
    ut_ref,
    decay_ref,
    mix_ref,
    before_ref,
    tot_ref,
    send_x,
    send_g,
    st_send,
    st_recv,
    back_send,
    tot_send,
    sem_x,
    sem_g,
    sem_s,
    sem_t,
    sem_b,
):
    me = lax.axis_index("ctx")
    hello_ctx(n, me)
    tok = x_ref.shape[0]
    experts = counts_ref.shape[1]
    cap = rows_ref.shape[1]
    slots = experts * cap

    ids = ids_ref[...]
    names = lax.broadcasted_iota(i32, (tok, experts), 1)
    m0 = ids[:, 0:1] == names
    m1 = ids[:, 1:2] == names
    member = jnp.where(m0, 1.0, 0.0) + jnp.where(m1, 1.0, 0.0)
    t_row = lax.broadcasted_iota(i32, (tok, tok), 0)
    t_col = lax.broadcasted_iota(i32, (tok, tok), 1)
    rank = mm(jnp.where(t_row > t_col, 1.0, 0.0).astype(bf16), member.astype(bf16))
    slot = jnp.where(
        rank < counts_ref[...].astype(f32), rank + (names * cap).astype(f32), -1.0
    )
    place = lax.broadcasted_iota(i32, (tok, slots), 1).astype(f32)
    p0 = jnp.where(place == jnp.sum(jnp.where(m0, slot, 0.0), 1, keepdims=True), 1.0, 0.0)
    p1 = jnp.where(place == jnp.sum(jnp.where(m1, slot, 0.0), 1, keepdims=True), 1.0, 0.0)
    both = (p0 + p1).astype(bf16)
    pick_ref[...] = both
    send_x[...] = mm(both, x_ref[...], 0, 0).astype(bf16).reshape(send_x.shape)
    grad = g_ref[...].astype(f32)
    prob = prob_ref[...]
    scaled = jnp.concatenate(
        [(prob[:, 0:1] * grad).astype(bf16), (prob[:, 1:2] * grad).astype(bf16)], axis=0
    )
    pair = jnp.concatenate([p0.astype(bf16), p1.astype(bf16)], axis=0)

    pl.semaphore_wait(pltpu.get_barrier_semaphore(), n - 1)
    exchange(n, me, send_x, rows_ref, sem_x.at[0], sem_x.at[1], "start")
    send_g[...] = mm(pair, scaled, 0, 0).astype(bf16).reshape(send_g.shape)
    exchange(n, me, send_g, grads_ref, sem_g.at[0], sem_g.at[1], "start")
    rows_ref[me] = send_x[me]
    grads_ref[me] = send_g[me]

    heads = ld_ref.shape[1]
    width = u_ref.shape[1]
    log = ld_ref[...]
    upto = jnp.where(t_row >= t_col, 1.0, 0.0)
    run = mm(upto, log, precision=HIGHEST)
    run_t = mm(log, upto, 0, 1, precision=HIGHEST)
    total = run[tok - 1 : tok, :]
    tail_x = spread(jnp.exp(total - run), width)
    tail_ref[...] = tail_x
    ut = (u_ref[...].astype(f32) * tail_x).astype(bf16)
    ut_ref[...] = ut
    st_send[...] = mm(ut, b_ref[...], 0, 0).astype(bf16).reshape(st_send.shape)
    tot_send[...] = jnp.concatenate(
        [
            jnp.broadcast_to(total, (tot_send.shape[0], heads)),
            jnp.zeros((tot_send.shape[0], tot_send.shape[1] - heads), f32),
        ],
        axis=1,
    )

    def totals(act):
        def one(i, _):
            to = lax.rem(me + i, n)
            back = lax.rem(me - i + n, n)
            if act == "start":
                remote(
                    tot_send, tot_ref.at[me], sem_t.at[0, i], sem_t.at[1, i], "ctx", to
                ).start()
            else:
                copy = remote(
                    tot_send, tot_ref.at[back], sem_t.at[0, i], sem_t.at[1, i], "ctx", to
                )
                copy.wait_recv()
                copy.wait_send()
            return 0

        lax.fori_loop(1, n, one, 0)

    totals("start")
    exchange(n, me, st_send, st_recv, sem_s.at[0], sem_s.at[1], "start")
    st_recv[me] = st_send[me]
    tot_ref[me] = tot_send[...]

    er_ref[...] = spread(jnp.exp(run), width)
    affinity = mm(c_ref[...], b_ref[...], 1, 1)
    for h in range(heads):
        gap = run[:, h : h + 1] - run_t[h : h + 1, :]
        decay = jnp.where(t_row >= t_col, jnp.exp(jnp.where(t_row >= t_col, gap, 0.0)), 0.0)
        decay_ref[h] = decay.astype(bf16)
        mix_ref[h] = (decay * affinity).astype(bf16)

    totals("wait")
    exchange(n, me, st_send, st_recv, sem_s.at[0], sem_s.at[1], "wait")
    scan_states(n, me, st_recv, back_send, tot_ref, width // heads, False)
    exchange(n, me, back_send, before_ref, sem_b.at[0], sem_b.at[1], "start")
    before_ref[me] = back_send[me]
    exchange(n, me, send_x, rows_ref, sem_x.at[0], sem_x.at[1], "wait")
    exchange(n, me, send_g, grads_ref, sem_g.at[0], sem_g.at[1], "wait")
    exchange(n, me, back_send, before_ref, sem_b.at[0], sem_b.at[1], "wait")


def dispatch(moe_input, out_grad, ids, prob, counts, ssd_input, in_map, out_map, log_decay):
    n = lax.axis_size("ctx")
    tok, cols = moe_input.shape
    experts = counts.shape[1]
    cap = 2 * tok * ids.shape[1] // experts
    heads = log_decay.shape[1]
    width = ssd_input.shape[1]
    state = in_map.shape[1]
    part = width // n
    block = jax.ShapeDtypeStruct((n, cap, cols), bf16)
    wide = jax.ShapeDtypeStruct((tok, width), f32)
    square = jax.ShapeDtypeStruct((heads, tok, tok), bf16)
    return pl.pallas_call(
        functools.partial(dispatch_kernel, n),
        out_shape=(
            block,
            block,
            jax.ShapeDtypeStruct((tok, experts * cap), bf16),
            wide,
            wide,
            jax.ShapeDtypeStruct((tok, width), bf16),
            square,
            square,
            jax.ShapeDtypeStruct((n, part, state), bf16),
            jax.ShapeDtypeStruct((n, 8, 128), f32),
        ),
        in_specs=[VMEM] * 9,
        out_specs=[VMEM] * 10,
        scratch_shapes=[
            pltpu.VMEM((n, cap, cols), bf16),
            pltpu.VMEM((n, cap, cols), bf16),
            pltpu.VMEM((n, part, state), bf16),
            pltpu.VMEM((n, part, state), bf16),
            pltpu.VMEM((n, part, state), bf16),
            pltpu.VMEM((8, 128), f32),
            DMA((2, n)),
            DMA((2, n)),
            DMA((2, n)),
            DMA((2, n)),
            DMA((2, n)),
        ],
        compiler_params=pltpu.CompilerParams(
            collective_id=0, has_side_effects=True, vmem_limit_bytes=48 * 2**20
        ),
        name="dispatch",
    )(moe_input, out_grad, ids, prob, counts, ssd_input, in_map, out_map, log_decay)


def expert_kernel(
    n,
    n_tp,
    x_ref,
    g_ref,
    pick_ref,
    og_ref,
    wg_hbm,
    wu_hbm,
    wd_hbm,
    out_ref,
    wg,
    wu,
    wd,
    psend,
    precv,
    q,
    ain,
    bin_,
    cin,
    csend,
    gall,
    eg,
    ret,
    wsem,
    psem,
    ringsem,
    gsem,
    rsem,
):
    me = lax.axis_index("ctx")
    t = lax.axis_index("tp")
    ny = n_tp // 2
    y, k = t // 2, lax.rem(t, 2)
    sib = y * 2 + (1 - k)
    y_up, y_dn, y_op = lax.rem(y + 1, ny), lax.rem(y + ny - 1, ny), lax.rem(y + 2, ny)
    up, dn = y_up * 2 + k, y_dn * 2 + k
    loads = [
        pltpu.make_async_copy(src, dst, wsem.at[i])
        for i, (src, dst) in enumerate(((wg_hbm, wg), (wu_hbm, wu), (wd_hbm, wd)))
    ]
    for load in loads:
        load.start()
    hello_ctx(n, me)
    hello_tp((sib, up, dn))

    half = x_ref.shape[0] // 2
    cap = ret.shape[1]
    hidden = wg.shape[1]
    chunk = half // ny
    edge = chunk // 2
    mine, other = k * half, (1 - k) * half

    def product(p, base):
        if p == 0:
            return mm(x_ref[pl.ds(base, half), :], wg[...]).astype(bf16)
        if p == 1:
            return mm(x_ref[pl.ds(base, half), :], wu[...]).astype(bf16)
        return mm(g_ref[pl.ds(base, half), :], wd[...], 1, 1).astype(bf16)

    pair = []
    for p in range(3):
        loads[p].wait()
        psend[p] = product(p, other)
        if p == 0:
            pl.semaphore_wait(pltpu.get_barrier_semaphore(), n - 1 + 3)
        copy = remote(psend.at[p], precv.at[p], psem.at[0, p], psem.at[1, p], "tp", sib)
        copy.start()
        pair.append(copy)
    for p in range(3):
        q[p] = product(p, mine)
    for p in range(3):
        pair[p].wait_recv()

    def rows(place, lo, size):
        return pl.ds(pl.multiple_of(place * chunk + lo, 16), size)

    def join(place):
        at = rows(place, 0, chunk)
        q[:, at, :] = (q[:, at, :].astype(f32) + precv[:, at, :].astype(f32)).astype(bf16)

    def ring(i, src, dst, place):
        copy = remote(src, dst, ringsem.at[0, i], ringsem.at[1, i], "tp", place)
        copy.start()
        return copy

    join(y_op)
    a_up = ring(0, q.at[:, rows(y_op, 0, edge), :], ain.at[0], up)
    a_dn = ring(1, q.at[:, rows(y_op, edge, edge), :], ain.at[1], dn)
    join(y_up)
    b_up = ring(2, q.at[:, rows(y_up, edge, edge), :], bin_.at[0], up)
    join(y_dn)
    b_dn = ring(3, q.at[:, rows(y_dn, 0, edge), :], bin_.at[1], dn)
    join(y)
    a_up.wait_recv()
    csend[0] = (q[:, rows(y_up, 0, edge), :].astype(f32) + ain[0].astype(f32)).astype(bf16)
    c_up = ring(4, csend.at[0], cin.at[0], up)
    a_dn.wait_recv()
    csend[1] = (q[:, rows(y_dn, edge, edge), :].astype(f32) + ain[1].astype(f32)).astype(bf16)
    c_dn = ring(5, csend.at[1], cin.at[1], dn)
    b_up.wait_recv()
    b_dn.wait_recv()
    c_up.wait_recv()
    c_dn.wait_recv()

    start = mine + y * chunk
    for e in range(2):
        total = (
            q[:, rows(y, e * edge, edge), :].astype(f32)
            + cin[e].astype(f32)
            + bin_[1 - e].astype(f32)
        )
        gate, upv, back = total[0], total[1], total[2]
        sigma = 1.0 / (1.0 + jnp.exp(-gate))
        at = pl.ds(pl.multiple_of(start + e * edge, 16), edge)
        gall[at, 0:hidden] = (back * upv * sigma * (1.0 + gate * (1.0 - sigma))).astype(bf16)
        gall[at, hidden : 2 * hidden] = (back * gate * sigma).astype(bf16)

    def share(i, base, place, lo, size, to):
        at = gall.at[pl.ds(pl.multiple_of(base + place * chunk + lo, 16), size), :]
        copy = remote(at, at, gsem.at[0, i], gsem.at[1, i], "tp", to)
        copy.start()
        return copy

    def arrived(i, base, place, lo, size):
        at = gall.at[pl.ds(pl.multiple_of(base + place * chunk + lo, 16), size), :]
        remote(at, at, gsem.at[0, i], gsem.at[1, i], "tp", sib).wait_recv()

    sent = [
        share(0, mine, y, 0, chunk, up),
        share(1, mine, y, 0, chunk, dn),
        share(2, mine, y, 0, chunk, sib),
    ]
    arrived(0, mine, y_dn, 0, chunk)
    sent.append(share(3, mine, y_dn, 0, edge, up))
    sent.append(share(5, mine, y_dn, 0, chunk, sib))
    arrived(1, mine, y_up, 0, chunk)
    sent.append(share(4, mine, y_up, edge, edge, dn))
    sent.append(share(6, mine, y_up, 0, chunk, sib))
    arrived(3, mine, y_op, 0, edge)
    arrived(4, mine, y_op, edge, edge)
    sent.append(share(7, mine, y_op, 0, chunk, sib))

    def back_product(base):
        at = pl.ds(pl.multiple_of(base, 16), half)
        grad = mm(gall[at, 0:hidden], wg[...], 1, 1) + mm(
            gall[at, hidden : 2 * hidden], wu[...], 1, 1
        )
        return grad.astype(bf16).reshape(n // 2, cap, grad.shape[1])

    def give(first):
        def one(i, _):
            to = first + lax.rem(me + i, n // 2)

            @pl.when(to != me)
            def _():
                remote(eg.at[to], ret.at[me], rsem.at[0, to], rsem.at[1, me], "ctx", to).start()

            return 0

        lax.fori_loop(0, n // 2, one, 0)

    first, second = k * (n // 2), (1 - k) * (n // 2)
    eg[pl.ds(first, n // 2)] = back_product(mine)
    give(first)
    arrived(2, other, y, 0, chunk)
    arrived(5, other, y_dn, 0, chunk)
    arrived(6, other, y_up, 0, chunk)
    arrived(7, other, y_op, 0, chunk)
    eg[pl.ds(second, n // 2)] = back_product(other)
    give(second)
    ret[me] = eg[me]

    for copy in pair + [a_up, a_dn, b_up, b_dn, c_up, c_dn] + sent:
        copy.wait_send()

    def finish(i, _):
        it = lax.rem(me + i, n)
        copy = remote(eg.at[it], ret.at[it], rsem.at[0, it], rsem.at[1, it], "ctx", it)
        copy.wait_send()
        copy.wait_recv()
        return 0

    lax.fori_loop(1, n, finish, 0)
    entries = ret[...].reshape(n * cap, ret.shape[2])
    out_ref[...] = (og_ref[...].astype(f32) + mm(pick_ref[...], entries)).astype(bf16)


def experts(rows, grads, pick, out_grad, w_gate, w_up, w_down):
    n = lax.axis_size("ctx")
    n_tp = lax.axis_size("tp")
    _, cap, cols = rows.shape
    hidden = w_gate.shape[1]
    total = n * cap
    half = total // 2
    edge = half // (n_tp // 2) // 2
    flat = (total, cols)
    return pl.pallas_call(
        functools.partial(expert_kernel, n, n_tp),
        out_shape=jax.ShapeDtypeStruct(out_grad.shape, bf16),
        in_specs=[VMEM] * 4 + [ANY] * 3,
        out_specs=VMEM,
        scratch_shapes=[
            pltpu.VMEM(w_gate.shape, bf16),
            pltpu.VMEM(w_up.shape, bf16),
            pltpu.VMEM(w_down.shape, bf16),
            pltpu.VMEM((3, half, hidden), bf16),
            pltpu.VMEM((3, half, hidden), bf16),
            pltpu.VMEM((3, half, hidden), bf16),
            pltpu.VMEM((2, 3, edge, hidden), bf16),
            pltpu.VMEM((2, 3, edge, hidden), bf16),
            pltpu.VMEM((2, 3, edge, hidden), bf16),
            pltpu.VMEM((2, 3, edge, hidden), bf16),
            pltpu.VMEM((total, 2 * hidden), bf16),
            pltpu.VMEM((n, cap, cols), bf16),
            pltpu.VMEM((n, cap, cols), bf16),
            DMA((3,)),
            DMA((2, 3)),
            DMA((2, 6)),
            DMA((2, 8)),
            DMA((2, n)),
        ],
        compiler_params=pltpu.CompilerParams(
            collective_id=1, has_side_effects=True, vmem_limit_bytes=56 * 2**20
        ),
        name="experts",
    )(rows.reshape(flat), grads.reshape(flat), pick, out_grad, w_gate, w_up, w_down)


def head_kernel(
    n,
    n_tp,
    ig_ref,
    u_ref,
    b_ref,
    c_ref,
    er_ref,
    tail_ref,
    ut_ref,
    decay_ref,
    mix_ref,
    before_ref,
    tot_ref,
    w_hbm,
    scan_ref,
    in_ref,
    out_ref,
    w,
    gat,
    acc,
    intra,
    st_send,
    st_recv,
    back_send,
    after,
    wsem,
    gsem,
    sem_s,
    sem_b,
):
    me = lax.axis_index("ctx")
    t = lax.axis_index("tp")
    ny = n_tp // 2
    y, k = t // 2, lax.rem(t, 2)
    sib = y * 2 + (1 - k)
    y_up, y_dn, y_op = lax.rem(y + 1, ny), lax.rem(y + ny - 1, ny), lax.rem(y + 2, ny)
    up, dn = y_up * 2 + k, y_dn * 2 + k
    op = y_op * 2 + k
    tok, cols = ig_ref.shape
    loads = []
    for part in range(n_tp):
        load = pltpu.make_async_copy(
            w_hbm.at[pl.ds(part * cols, cols), :], w.at[part], wsem.at[part]
        )
        load.start()
        loads.append(load)
    hello_ctx(n, me)
    hello_tp((sib, up, dn))
    gat[t] = ig_ref[...]
    pl.semaphore_wait(pltpu.get_barrier_semaphore(), n - 1 + 3)

    def share(i, place, lo, size, to):
        at = gat.at[place, pl.ds(lo, size), :]
        copy = remote(at, at, gsem.at[0, i], gsem.at[1, i], "tp", to)
        copy.start()
        return copy

    def arrived(i, place, lo, size):
        at = gat.at[place, pl.ds(lo, size), :]
        remote(at, at, gsem.at[0, i], gsem.at[1, i], "tp", sib).wait_recv()

    edge = tok // 2
    sent = [share(0, t, 0, tok, up), share(1, t, 0, tok, dn), share(2, t, 0, tok, sib)]
    for load in loads:
        load.wait()

    def add(place):
        acc[...] += mm(gat[place], w[place])

    acc[...] = mm(gat[t], w[t])
    arrived(2, sib, 0, tok)
    add(sib)
    arrived(0, dn, 0, tok)
    sent.append(share(3, dn, 0, edge, up))
    sent.append(share(5, dn, 0, tok, sib))
    arrived(1, up, 0, tok)
    sent.append(share(4, up, edge, edge, dn))
    sent.append(share(6, up, 0, tok, sib))
    add(dn)
    add(up)
    arrived(3, op, 0, edge)
    arrived(4, op, edge, edge)
    sent.append(share(7, op, 0, tok, sib))
    add(op)
    sdn, sup, sop = y_dn * 2 + (1 - k), y_up * 2 + (1 - k), y_op * 2 + (1 - k)
    arrived(5, sdn, 0, tok)
    add(sdn)
    arrived(6, sup, 0, tok)
    add(sup)
    arrived(7, sop, 0, tok)
    add(sop)

    grad = acc[...].astype(bf16)
    ge = (grad.astype(f32) * er_ref[...]).astype(bf16)
    st_send[...] = mm(ge, c_ref[...], 0, 0).astype(bf16).reshape(st_send.shape)
    exchange(n, me, st_send, st_recv, sem_s.at[0], sem_s.at[1], "start")
    st_recv[me] = st_send[me]

    heads = decay_ref.shape[0]
    size = grad.shape[1] // heads
    weights = jnp.zeros((tok, tok), f32)
    for h in range(heads):
        gh = grad[:, h * size : (h + 1) * size]
        uh = u_ref[:, h * size : (h + 1) * size]
        weights = weights + decay_ref[h].astype(f32) * mm(gh, uh, 1, 1)
        intra[:, h * size : (h + 1) * size] = mm(mix_ref[h], gh, 0, 0)
    weights = weights.astype(bf16)
    state = b_ref.shape[1]
    out_ref[...] = mm(weights, b_ref[...]) + mm(ge, before_ref[...].reshape(-1, state))

    exchange(n, me, st_send, st_recv, sem_s.at[0], sem_s.at[1], "wait")
    scan_states(n, me, st_recv, back_send, tot_ref, size, True)
    exchange(n, me, back_send, after, sem_b.at[0], sem_b.at[1], "start")
    after[me] = back_send[me]
    in_part = mm(weights, c_ref[...], 0, 0)
    for copy in sent:
        copy.wait_send()
    exchange(n, me, back_send, after, sem_b.at[0], sem_b.at[1], "wait")
    later = after[...].reshape(-1, state)
    in_ref[...] = in_part + mm(ut_ref[...], later)
    scan_ref[...] = (intra[...] + tail_ref[...] * mm(b_ref[...], later, 1, 1)).astype(bf16)


def head_part(input_grad, ssd_input, in_map, out_map, prepared, weight):
    n = lax.axis_size("ctx")
    n_tp = lax.axis_size("tp")
    tok, cols = input_grad.shape
    width = ssd_input.shape[1]
    state = in_map.shape[1]
    part = width // n
    small = jax.ShapeDtypeStruct((tok, state), f32)
    return pl.pallas_call(
        functools.partial(head_kernel, n, n_tp),
        out_shape=(jax.ShapeDtypeStruct((tok, width), bf16), small, small),
        in_specs=[VMEM] * 11 + [ANY],
        out_specs=[VMEM] * 3,
        scratch_shapes=[
            pltpu.VMEM((n_tp, cols, width), bf16),
            pltpu.VMEM((n_tp, tok, cols), bf16),
            pltpu.VMEM((tok, width), f32),
            pltpu.VMEM((tok, width), f32),
            pltpu.VMEM((n, part, state), bf16),
            pltpu.VMEM((n, part, state), bf16),
            pltpu.VMEM((n, part, state), bf16),
            pltpu.VMEM((n, part, state), bf16),
            DMA((n_tp,)),
            DMA((2, 8)),
            DMA((2, n)),
            DMA((2, n)),
        ],
        compiler_params=pltpu.CompilerParams(
            collective_id=2, has_side_effects=True, vmem_limit_bytes=48 * 2**20
        ),
        name="heads",
    )(input_grad, ssd_input, in_map, out_map, *prepared, weight)


def body(
    moe_input,
    out_grad,
    route_prob,
    route_ids,
    route_counts,
    w_gate,
    w_up,
    w_down,
    out_weight,
    ssd_input,
    input_map,
    output_map,
    log_decay,
):
    weight = lax.all_gather(out_weight, "ctx", axis=0, tiled=True)
    rows, grads, pick, *prepared = dispatch(
        moe_input,
        out_grad,
        route_ids,
        route_prob,
        route_counts,
        ssd_input,
        input_map,
        output_map,
        log_decay,
    )
    input_grad = experts(rows, grads, pick, out_grad, w_gate[0], w_up[0], w_down[0])
    scan_grad, in_map_grad, out_map_grad = head_part(
        input_grad, ssd_input, input_map, output_map, prepared, weight
    )
    return (input_grad, scan_grad, in_map_grad, out_map_grad)


def solution(mesh):
    in_specs = (
        P("ctx", "tp"),
        P("ctx", "tp"),
        P("ctx", None),
        P("ctx", None),
        P("ctx", None),
        P("ctx", "tp", None),
        P("ctx", "tp", None),
        P("ctx", None, "tp"),
        P("ctx", "tp"),
        P("ctx", "tp"),
        P("ctx", "tp"),
        P("ctx", "tp"),
        P("ctx", "tp"),
    )
    out_specs = (P("ctx", "tp"), P("ctx", "tp"), P("ctx", "tp"), P("ctx", "tp"))
    return jax.shard_map(body, mesh=mesh, in_specs=in_specs, out_specs=out_specs, check_vma=False)
```

```python
import functools

import jax
import jax.numpy as jnp
from jax import lax
from jax.experimental import pallas as pl
from jax.experimental.pallas import tpu as pltpu
from jax.sharding import PartitionSpec as P

MESH = pl.DeviceIdType.MESH
HIGHEST = lax.Precision.HIGHEST
bf16, f32, i32 = jnp.bfloat16, jnp.float32, jnp.int32
VMEM = pl.BlockSpec(memory_space=pltpu.VMEM)
ANY = pl.BlockSpec(memory_space=pl.ANY)
DMA = pltpu.SemaphoreType.DMA


def mm(a, b, ca=1, cb=0, precision=None):
    return lax.dot_general(
        a, b, (((ca,), (cb,)), ((), ())), precision=precision, preferred_element_type=f32
    )


def remote(src, dst, send, recv, axis, place):
    return pltpu.make_async_remote_copy(
        src_ref=src,
        dst_ref=dst,
        send_sem=send,
        recv_sem=recv,
        device_id={axis: place},
        device_id_type=MESH,
    )


def hello_ctx(n, me):
    barrier = pltpu.get_barrier_semaphore()

    def one(i, _):
        pl.semaphore_signal(
            barrier, inc=1, device_id={"ctx": lax.rem(me + i, n)}, device_id_type=MESH
        )
        return 0

    lax.fori_loop(1, n, one, 0)


def hello_tp(places):
    barrier = pltpu.get_barrier_semaphore()
    for place in places:
        pl.semaphore_signal(barrier, inc=1, device_id={"tp": place}, device_id_type=MESH)


def exchange(n, me, src, dst, send, recv, act):
    def one(i, _):
        to = lax.rem(me + i, n)
        back = lax.rem(me - i + n, n)
        if act == "start":
            remote(src.at[to], dst.at[me], send.at[i], recv.at[i], "ctx", to).start()
        else:
            copy = remote(src.at[to], dst.at[back], send.at[i], recv.at[i], "ctx", to)
            copy.wait_recv()
            copy.wait_send()
        return 0

    lax.fori_loop(1, n, one, 0)


def spread(columns, total):
    heads = columns.shape[1]
    size = total // heads
    put = lax.broadcasted_iota(i32, (heads, total), 1) // size == lax.broadcasted_iota(
        i32, (heads, total), 0
    )
    return mm(columns, put.astype(f32), precision=HIGHEST)


def scan_states(n, me, loc, out, totals, rows_per_head, backward):
    head = me * loc.shape[1] // rows_per_head
    lane = lax.broadcasted_iota(i32, totals.shape, 2)
    decay = jnp.exp(jnp.sum(jnp.where(lane == head, totals[...], 0.0), axis=2, keepdims=True))
    state = jnp.zeros(loc.shape[1:], f32)
    order = range(n - 1, -1, -1) if backward else range(n)
    for c in order:
        out[c] = state.astype(bf16)
        state = decay[c, 0:1, :] * state + loc[c].astype(f32)


def layer_kernel(
    nx,
    nz,
    ny,
    x_ref,
    g_ref,
    ids_ref,
    prob_ref,
    counts_ref,
    u_ref,
    b_ref,
    c_ref,
    ld_ref,
    wg_hbm,
    wu_hbm,
    wd_hbm,
    w_hbm,
    out_ref,
    scan_ref,
    in_ref,
    out_map_ref,
    er_ref,
    tail_ref,
    ut_ref,
    decay_ref,
    mix_ref,
    before_ref,
    tot_ref,
    wg,
    wu,
    wd,
    send,
    inbuf,
    part,
    precv,
    rsum,
    gall,
    eg,
    ret,
    pick,
    st_send,
    st_recv,
    back_send,
    tot_send,
    w,
    ya,
    xa,
    hsend,
    hrecv,
    intra,
    gst_send,
    gst_recv,
    gback_send,
    after,
    wsem,
    isem,
    psem,
    ssem,
    gsem,
    fsem,
    rsem,
    sem_s,
    sem_t,
    sem_b,
    usem,
    dsem,
    ysem,
    xsem,
    hfsem,
    hsem,
    gsem_s,
    gsem_b,
):
    n = nx * nz
    me = lax.axis_index("ctx")
    x, z = me // nz, lax.rem(me, nz)
    t = lax.axis_index("tp")
    y, k = t // 2, lax.rem(t, 2)
    sib = y * 2 + (1 - k)
    y_up, y_dn, y_op = lax.rem(y + 1, ny), lax.rem(y + ny - 1, ny), lax.rem(y + 2, ny)
    up, dn, op = y_up * 2 + k, y_dn * 2 + k, y_op * 2 + k

    def ahead(dx, dz):
        return lax.rem(x + dx, nx) * nz + lax.rem(z + dz, nz)

    def behind(dx, dz):
        return lax.rem(x - dx + nx, nx) * nz + lax.rem(z - dz + nz, nz)

    cols, tok = x_ref.shape
    hidden = wg.shape[1]
    cut = wd_hbm.shape[0] // 128 * 128
    loads = [
        pltpu.make_async_copy(wg_hbm, wg.at[pl.ds(0, cols)], wsem.at[0]),
        pltpu.make_async_copy(wu_hbm, wu.at[pl.ds(0, cols)], wsem.at[1]),
        pltpu.make_async_copy(wd_hbm.at[pl.ds(0, cut)], wd.at[pl.ds(0, cut)], wsem.at[2]),
        pltpu.make_async_copy(
            wd_hbm.at[pl.ds(cut, cols - cut)], wd.at[pl.ds(cols, cols - cut)], wsem.at[3]
        ),
    ]
    own_w = pltpu.make_async_copy(w_hbm, w.at[z], wsem.at[4])
    own_w.start()
    for load in loads:
        load.start()
    hello_ctx(n, me)
    hello_tp((sib, up, dn, op))

    experts = counts_ref.shape[1]
    cap = inbuf.shape[2]
    slots = experts * cap
    rest = cols - cut
    full = cut + 128
    ids = ids_ref[...]
    names = lax.broadcasted_iota(i32, (experts, tok), 0)
    m0 = ids[0:1, :] == names
    m1 = ids[1:2, :] == names
    member = jnp.where(m0, 1.0, 0.0) + jnp.where(m1, 1.0, 0.0)
    t_row = lax.broadcasted_iota(i32, (tok, tok), 0)
    t_col = lax.broadcasted_iota(i32, (tok, tok), 1)
    rank = mm(member.astype(bf16), jnp.where(t_row < t_col, 1.0, 0.0).astype(bf16))
    e_row = lax.broadcasted_iota(i32, (experts, experts), 0)
    e_col = lax.broadcasted_iota(i32, (experts, experts), 1)
    limit = jnp.sum(
        jnp.where(e_row == e_col, counts_ref[...].astype(f32), 0.0), axis=1, keepdims=True
    )
    slot = jnp.where(rank < limit, rank + (names * cap).astype(f32), -1.0)
    place = lax.broadcasted_iota(i32, (slots, tok), 0).astype(f32)
    p0 = jnp.where(place == jnp.sum(jnp.where(m0, slot, 0.0), 0, keepdims=True), 1.0, 0.0)
    p1 = jnp.where(place == jnp.sum(jnp.where(m1, slot, 0.0), 0, keepdims=True), 1.0, 0.0)
    both = (p0 + p1).astype(bf16)
    pick[...] = both

    pl.semaphore_wait(pltpu.get_barrier_semaphore(), n - 1 + 4)
    mid = w.shape[2] // 2
    last_hop = nz // 2 - 1

    def w_copy(j, upward):
        if upward:
            block, to, sem = lax.rem(z - j + nz, nz), ahead(0, 1), usem
        else:
            block, to, sem = lax.rem(z + j, nz), behind(0, 1), dsem
        if j < last_hop:
            at = w.at[block]
        else:
            at = w.at[block, :, pl.ds(0 if upward else mid, mid)]
        return remote(at, at, sem.at[0, j], sem.at[1, j], "ctx", to)

    def w_landed(j):
        for upward, sem in ((True, usem), (False, dsem)):
            block = lax.rem(z - j - 1 + nz, nz) if upward else lax.rem(z + j + 1, nz)
            if j < last_hop:
                at = w.at[block]
            else:
                at = w.at[block, :, pl.ds(0 if upward else mid, mid)]
            remote(at, at, sem.at[0, j], sem.at[1, j], "ctx", ahead(0, 1)).wait_recv()

    def w_hop(j):
        if j:
            w_landed(j - 1)
        w_copy(j, True).start()
        w_copy(j, False).start()

    own_w.wait()
    w_hop(0)
    grad = g_ref[...].astype(f32)
    prob = prob_ref[...]
    scaled = jnp.concatenate(
        [(prob[0:1, :] * grad).astype(bf16), (prob[1:2, :] * grad).astype(bf16)], axis=1
    )
    pair = jnp.concatenate([p0.astype(bf16), p1.astype(bf16)], axis=1)
    sel_x = mm(both, x_ref[...], 1, 1)
    sel_g = mm(pair, scaled, 1, 1)
    send[:, :, 0:cut] = sel_x[:, 0:cut].astype(bf16).reshape(experts, cap, cut)
    send[:, :, cut : 2 * cut] = sel_g[:, 0:cut].astype(bf16).reshape(experts, cap, cut)
    last = jnp.concatenate(
        [sel_x[:, cut:], sel_g[:, cut:], jnp.zeros((slots, 128 - 2 * rest), f32)], axis=1
    )
    send[:, :, 2 * cut :] = last.astype(bf16).reshape(experts, cap, 128)

    def post(i, _):
        dx, dz = i // nz, lax.rem(i, nz)
        to = ahead(dx, dz)
        remote(
            send.at[to], inbuf.at[dx, dz], isem.at[0, i], isem.at[1, i], "ctx", to
        ).start()
        return 0

    lax.fori_loop(1, 2 * nz, post, 0)
    inbuf[0, 0] = send[me]

    heads = ld_ref.shape[0]
    width = u_ref.shape[1]
    log = ld_ref[...]
    upto = jnp.where(t_row >= t_col, 1.0, 0.0)
    run = mm(upto, log, 1, 1, precision=HIGHEST)
    run_t = mm(log, upto, 1, 1, precision=HIGHEST)
    total = run[tok - 1 : tok, :]
    tail_x = spread(jnp.exp(total - run), width)
    tail_ref[...] = tail_x
    ut = (u_ref[...].astype(f32) * tail_x).astype(bf16)
    ut_ref[...] = ut
    st_send[...] = mm(ut, b_ref[...], 0, 0).astype(bf16).reshape(st_send.shape)
    tot_send[...] = jnp.concatenate(
        [
            jnp.broadcast_to(total, (tot_send.shape[0], heads)),
            jnp.zeros((tot_send.shape[0], tot_send.shape[1] - heads), f32),
        ],
        axis=1,
    )

    def totals(act):
        def one(i, _):
            to = lax.rem(me + i, n)
            back = lax.rem(me - i + n, n)
            if act == "start":
                remote(
                    tot_send, tot_ref.at[me], sem_t.at[0, i], sem_t.at[1, i], "ctx", to
                ).start()
            else:
                copy = remote(
                    tot_send, tot_ref.at[back], sem_t.at[0, i], sem_t.at[1, i], "ctx", to
                )
                copy.wait_recv()
                copy.wait_send()
            return 0

        lax.fori_loop(1, n, one, 0)


    wg[pl.ds(cols, 128 - rest), :] = jnp.zeros((128 - rest, hidden), bf16)
    wu[pl.ds(cols, 128 - rest), :] = jnp.zeros((128 - rest, hidden), bf16)
    wd[pl.ds(cut, rest), :] = jnp.zeros((rest, hidden), bf16)
    wd[pl.ds(cols + rest, 128 - 2 * rest), :] = jnp.zeros((128 - 2 * rest, hidden), bf16)
    for load in loads:
        load.wait()

    er_ref[...] = spread(jnp.exp(run), width)
    affinity = mm(c_ref[...], b_ref[...], 1, 1)
    for h in range(heads):
        gap = run[:, h : h + 1] - run_t[h : h + 1, :]
        decay = jnp.where(t_row >= t_col, jnp.exp(jnp.where(t_row >= t_col, gap, 0.0)), 0.0)
        decay_ref[h] = decay.astype(bf16)
        mix_ref[h] = (decay * affinity).astype(bf16)

    half = nz // 2 * cap
    mine, other = pl.multiple_of(k * half, cap), pl.multiple_of((1 - k) * half, cap)

    def pair_copy(s, p):
        return remote(
            part.at[s, p, pl.ds(other, half)],
            precv.at[s, p],
            psem.at[0, s, p],
            psem.at[1, s, p],
            "tp",
            sib,
        )

    def sum_copy(s, i):
        to, dz = ((up, y_up), (dn, y_dn), (op, y_op))[i]
        return remote(
            part.at[s, :, pl.ds(pl.multiple_of(mine + dz * cap, cap), cap)],
            rsum.at[s, i],
            ssem.at[0, s, i],
            ssem.at[1, s, i],
            "tp",
            to,
        )

    def grads_at(s, core, dz):
        return gall.at[s, pl.ds(pl.multiple_of(core * half + dz * cap, cap), cap)]

    froms = (y_dn, y_up, y_op)

    def grad_copy(s, i, dz):
        at = grads_at(s, k, dz)
        return remote(at, at, gsem.at[0, s, i], gsem.at[1, s, i], "tp", (up, dn, op)[i])

    def fwd_copy(s, i, core, dz):
        at = grads_at(s, core, dz)
        return remote(at, at, fsem.at[0, s, i], fsem.at[1, s, i], "tp", sib)

    def first(s):
        def one(i, _):
            @pl.when(s * nz + i > 0)
            def _():
                remote(
                    send.at[ahead(s, i)],
                    inbuf.at[s, i],
                    isem.at[0, s * nz + i],
                    isem.at[1, s * nz + i],
                    "ctx",
                    ahead(s, i),
                ).wait_recv()

            return 0

        lax.fori_loop(0, nz, one, 0)
        rows = inbuf[s].reshape(nz * cap, 2 * cut + 128)
        lasts = rows[:, 2 * cut :]
        for p, w in enumerate((wg, wu, wd)):
            lo = 0 if p < 2 else cut
            got = mm(rows[:, lo : lo + cut], w[0:cut, :]) + mm(lasts, w[cut:full, :])
            part[s, p] = got.astype(bf16)
            pair_copy(s, p).start()

    def second(s):
        for p in range(3):
            pair_copy(s, p).wait_recv()
            at = pl.ds(mine, half)
            part[s, p, at] = (part[s, p, at].astype(f32) + precv[s, p].astype(f32)).astype(bf16)
        for i in range(3):
            sum_copy(s, i).start()

    def third(s):
        total = part[s, :, pl.ds(pl.multiple_of(mine + y * cap, cap), cap)].astype(f32)
        for i in range(3):
            sum_copy(s, i).wait_recv()
            total = total + rsum[s, i].astype(f32)
        gate, upv, back = total[0], total[1], total[2]
        sigma = 1.0 / (1.0 + jnp.exp(-gate))
        at = pl.ds(pl.multiple_of(mine + y * cap, cap), cap)
        gall[s, at, 0:hidden] = (back * upv * sigma * (1.0 + gate * (1.0 - sigma))).astype(bf16)
        gall[s, at, hidden : 2 * hidden] = (back * gate * sigma).astype(bf16)
        for i in range(3):
            grad_copy(s, i, y).start()
        fwd_copy(s, 3, k, y).start()

    def fourth(s):
        for i in range(3):
            grad_copy(s, i, froms[i]).wait_recv()
            fwd_copy(s, i, k, froms[i]).start()

    def fifth(s):
        for i in range(3):
            fwd_copy(s, i, 1 - k, froms[i]).wait_recv()
        fwd_copy(s, 3, 1 - k, y).wait_recv()
        grad = mm(gall[s, :, 0:hidden], wg[0:cols, :], 1, 1) + mm(
            gall[s, :, hidden : 2 * hidden], wu[0:cols, :], 1, 1
        )
        eg[s] = grad.astype(bf16).reshape(nz, cap, cols)

        def one(i, _):
            @pl.when(s * nz + i > 0)
            def _():
                back_copy(s, i).start()

            return 0

        lax.fori_loop(0, nz, one, 0)

    def back_copy(s, i):
        return remote(
            eg.at[s, i],
            ret.at[me],
            rsem.at[0, s * nz + i],
            rsem.at[1, s * nz + i],
            "ctx",
            behind(s, i),
        )

    def stage(s, _):
        first(s)

        @pl.when(s + 2 < nx)
        def _():
            lax.fori_loop((s + 2) * nz, (s + 3) * nz, post, 0)

        second(s)

        @pl.when(s > 0)
        def _():
            fourth(s - 1)
            fifth(s - 1)

        third(s)
        return 0

    lax.fori_loop(0, nx, stage, 0)
    totals("start")
    exchange(n, me, st_send, st_recv, sem_s.at[0], sem_s.at[1], "start")
    st_recv[me] = st_send[me]
    tot_ref[me] = tot_send[...]
    fourth(nx - 1)
    w_hop(1)
    fifth(nx - 1)
    w_hop(2)
    ret[me] = eg[0, 0]

    def finish(i, _):
        dx, dz = i // nz, lax.rem(i, nz)
        it = ahead(dx, dz)
        remote(eg.at[dx, dz], ret.at[it], rsem.at[0, i], rsem.at[1, i], "ctx", it).wait_recv()
        return 0

    lax.fori_loop(1, n, finish, 0)
    entries = ret[...].reshape(slots, cols)
    input_grad = g_ref[...].astype(f32) + mm(entries, pick[...], 0, 0)
    ya[y] = input_grad.reshape(nz // 2, cols // (nz // 2), tok).astype(bf16)

    def y_copy(i, chunk):
        return remote(
            ya.at[chunk], ya.at[chunk], ysem.at[0, i], ysem.at[1, i], "tp", (up, dn, op)[i]
        )

    def x_copy(chunk, source):
        return remote(
            ya.at[chunk],
            xa.at[source, k],
            xsem.at[0, chunk],
            xsem.at[1, source],
            "ctx",
            chunk * nz + z,
        )

    def f_copy(source, core):
        at = xa.at[source, core]
        return remote(at, at, hfsem.at[0, source], hfsem.at[1, source], "tp", sib)

    def pass_on(chunk):
        @pl.when(chunk != x)
        def _():
            x_copy(chunk, x).start()

        @pl.when(chunk == x)
        def _():
            xa[x, k] = ya[chunk]
            f_copy(x, k).start()

    for i in range(3):
        y_copy(i, y).start()
    pass_on(y)
    out_ref[...] = input_grad.astype(bf16)
    w_hop(3)
    for i in range(3):
        y_copy(i, froms[i]).wait_recv()
        pass_on(froms[i])

    totals("wait")
    exchange(n, me, st_send, st_recv, sem_s.at[0], sem_s.at[1], "wait")
    size = width // heads
    scan_states(n, me, st_recv, back_send, tot_ref, size, False)
    exchange(n, me, back_send, before_ref, sem_b.at[0], sem_b.at[1], "start")
    before_ref[me] = back_send[me]

    def x_at(d):
        return lax.rem(x + d, nx)

    def product(source):
        total = jnp.zeros((tok, width), f32)
        for b in range(nz):
            total = total + mm(xa[source, b // (nz // 2), b % (nz // 2)], w[b], 0, 0)
        return total

    def h_copy(d):
        return remote(
            hsend.at[d - 1],
            hrecv.at[d - 1],
            hsem.at[0, d - 1],
            hsem.at[1, d - 1],
            "ctx",
            x_at(d) * nz + z,
        )

    order = [1, nx - 1] + list(range(2, nx - 1))
    for d in order:
        source = x_at(d)
        x_copy(x, source).wait_recv()
        f_copy(source, k).start()
    w_landed(3)
    for d in order:
        source = x_at(d)
        f_copy(source, 1 - k).wait_recv()
        hsend[d - 1] = product(source).astype(bf16)
        h_copy(d).start()
    f_copy(x, 1 - k).wait_recv()
    whole = product(x)
    for d in order:
        h_copy(d).wait_recv()
        whole = whole + hrecv[d - 1].astype(f32)

    grad = whole.astype(bf16)
    ge = (grad.astype(f32) * er_ref[...]).astype(bf16)
    gst_send[...] = mm(ge, c_ref[...], 0, 0).astype(bf16).reshape(gst_send.shape)
    exchange(n, me, gst_send, gst_recv, gsem_s.at[0], gsem_s.at[1], "start")
    gst_recv[me] = gst_send[me]

    weights = jnp.zeros((tok, tok), f32)
    for h in range(heads):
        gh = grad[:, h * size : (h + 1) * size]
        uh = u_ref[:, h * size : (h + 1) * size]
        weights = weights + decay_ref[h].astype(f32) * mm(gh, uh, 1, 1)
        intra[:, h * size : (h + 1) * size] = mm(mix_ref[h], gh, 0, 0)
    weights = weights.astype(bf16)
    state = b_ref.shape[1]

    exchange(n, me, gst_send, gst_recv, gsem_s.at[0], gsem_s.at[1], "wait")
    scan_states(n, me, gst_recv, gback_send, tot_ref, size, True)
    exchange(n, me, gback_send, after, gsem_b.at[0], gsem_b.at[1], "start")
    after[me] = gback_send[me]

    exchange(n, me, back_send, before_ref, sem_b.at[0], sem_b.at[1], "wait")
    out_map_ref[...] = mm(weights, b_ref[...]) + mm(ge, before_ref[...].reshape(-1, state))
    in_part = mm(weights, c_ref[...], 0, 0)

    def settle(s, _):
        for p in range(3):
            pair_copy(s, p).wait_send()
        for i in range(3):
            sum_copy(s, i).wait_send()
            grad_copy(s, i, y).wait_send()
            fwd_copy(s, i, k, froms[i]).wait_send()
        fwd_copy(s, 3, k, y).wait_send()
        return 0

    lax.fori_loop(0, nx, settle, 0)

    def sent(i, _):
        dx, dz = i // nz, lax.rem(i, nz)
        it = ahead(dx, dz)
        remote(
            send.at[it], inbuf.at[dx, dz], isem.at[0, i], isem.at[1, i], "ctx", it
        ).wait_send()
        remote(eg.at[dx, dz], ret.at[it], rsem.at[0, i], rsem.at[1, i], "ctx", it).wait_send()
        return 0

    lax.fori_loop(1, n, sent, 0)
    for j in range(nz // 2):
        w_copy(j, True).wait_send()
        w_copy(j, False).wait_send()
    for i in range(3):
        y_copy(i, y).wait_send()
    for d in order:
        x_copy(x_at(d), x).wait_send()
        h_copy(d).wait_send()
    for d in range(nx):
        f_copy(x_at(d), k).wait_send()

    exchange(n, me, gback_send, after, gsem_b.at[0], gsem_b.at[1], "wait")
    later = after[...].reshape(-1, state)
    in_ref[...] = in_part + mm(ut_ref[...], later)
    scan_ref[...] = (intra[...] + tail_ref[...] * mm(b_ref[...], later, 1, 1)).astype(bf16)


def layer(
    sizes, moe_t, grad_t, ids_t, prob_t, counts, ssd_input, in_map, out_map, log_t, wg, wu, wd, w
):
    nx, nz, ny = sizes
    n = nx * nz
    cols, tok = moe_t.shape
    experts = counts.shape[1]
    cap = 2 * tok * ids_t.shape[0] // experts
    heads = log_t.shape[0]
    width = ssd_input.shape[1]
    state = in_map.shape[1]
    hidden = wg.shape[1]
    part = width // n
    cut = cols // 128 * 128
    full = cut + 128
    rows = nz * cap
    small = jax.ShapeDtypeStruct((tok, state), f32)
    states = pltpu.VMEM((n, part, state), bf16)
    pairs = DMA((2, n))
    return pl.pallas_call(
        functools.partial(layer_kernel, nx, nz, ny),
        out_shape=(
            jax.ShapeDtypeStruct((cols, tok), bf16),
            jax.ShapeDtypeStruct((tok, width), bf16),
            small,
            small,
        ),
        in_specs=[VMEM] * 9 + [ANY] * 4,
        out_specs=[VMEM] * 4,
        scratch_shapes=[
            pltpu.VMEM((tok, width), f32),
            pltpu.VMEM((tok, width), f32),
            pltpu.VMEM((tok, width), bf16),
            pltpu.VMEM((heads, tok, tok), bf16),
            pltpu.VMEM((heads, tok, tok), bf16),
            states,
            pltpu.VMEM((n, 8, 128), f32),
            pltpu.VMEM((full, hidden), bf16),
            pltpu.VMEM((full, hidden), bf16),
            pltpu.VMEM((full, hidden), bf16),
            pltpu.VMEM((n, cap, 2 * cut + 128), bf16),
            pltpu.VMEM((nx, nz, cap, 2 * cut + 128), bf16),
            pltpu.VMEM((nx, 3, rows, hidden), bf16),
            pltpu.VMEM((nx, 3, rows // 2, hidden), bf16),
            pltpu.VMEM((nx, 3, 3, cap, hidden), bf16),
            pltpu.VMEM((nx, rows, 2 * hidden), bf16),
            pltpu.VMEM((nx, nz, cap, cols), bf16),
            pltpu.VMEM((n, cap, cols), bf16),
            pltpu.VMEM((experts * cap, tok), bf16),
            states,
            states,
            states,
            pltpu.VMEM((8, 128), f32),
            pltpu.VMEM((nz, w.shape[0], width), bf16),
            pltpu.VMEM((ny, nz // 2, w.shape[0], tok), bf16),
            pltpu.VMEM((nx, 2, nz // 2, w.shape[0], tok), bf16),
            pltpu.VMEM((nx - 1, tok, width), bf16),
            pltpu.VMEM((nx - 1, tok, width), bf16),
            pltpu.VMEM((tok, width), f32),
            states,
            states,
            states,
            states,
            DMA((5,)),
            pairs,
            DMA((2, nx, 3)),
            DMA((2, nx, 3)),
            DMA((2, nx, 3)),
            DMA((2, nx, 4)),
            pairs,
            pairs,
            pairs,
            pairs,
            DMA((2, nz // 2)),
            DMA((2, nz // 2)),
            DMA((2, 3)),
            DMA((2, nx)),
            DMA((2, nx)),
            DMA((2, nx - 1)),
            pairs,
            pairs,
        ],
        compiler_params=pltpu.CompilerParams(
            collective_id=0, has_side_effects=True, vmem_limit_bytes=46 * 2**20
        ),
        name="layer",
    )(moe_t, grad_t, ids_t, prob_t, counts, ssd_input, in_map, out_map, log_t, wg, wu, wd, w)


def body(
    moe_input,
    out_grad,
    route_prob,
    route_ids,
    route_counts,
    w_gate,
    w_up,
    w_down,
    out_weight,
    ssd_input,
    input_map,
    output_map,
    log_decay,
):
    n = lax.axis_size("ctx")
    ny = lax.axis_size("tp") // 2
    nx = ny
    nz = n // nx
    grad_t, scan_grad, in_map_grad, out_map_grad = layer(
        (nx, nz, ny),
        moe_input.T,
        out_grad.T,
        route_ids.T,
        route_prob.T,
        route_counts,
        ssd_input,
        input_map,
        output_map,
        log_decay.T,
        w_gate[0],
        w_up[0],
        w_down[0].T,
        out_weight,
    )
    return (grad_t.T, scan_grad, in_map_grad, out_map_grad)


def solution(mesh):
    in_specs = (
        P("ctx", "tp"),
        P("ctx", "tp"),
        P("ctx", None),
        P("ctx", None),
        P("ctx", None),
        P("ctx", "tp", None),
        P("ctx", "tp", None),
        P("ctx", None, "tp"),
        P("ctx", "tp"),
        P("ctx", "tp"),
        P("ctx", "tp"),
        P("ctx", "tp"),
        P("ctx", "tp"),
    )
    out_specs = (P("ctx", "tp"), P("ctx", "tp"), P("ctx", "tp"), P("ctx", "tp"))
    return jax.shard_map(body, mesh=mesh, in_specs=in_specs, out_specs=out_specs, check_vma=False)
```

```python
import functools

import jax
import jax.numpy as jnp
from jax import lax
from jax.experimental import pallas as pl
from jax.experimental.pallas import tpu as pltpu
from jax.sharding import PartitionSpec as P

MESH = pl.DeviceIdType.MESH
HIGHEST = lax.Precision.HIGHEST
bf16, f32, i32 = jnp.bfloat16, jnp.float32, jnp.int32
VMEM = pl.BlockSpec(memory_space=pltpu.VMEM)
HBM = pl.BlockSpec(memory_space=pltpu.HBM)
DMA = pltpu.SemaphoreType.DMA


def mm(a, b, ca=1, cb=0, precision=None):
    return lax.dot_general(
        a, b, (((ca,), (cb,)), ((), ())), precision=precision, preferred_element_type=f32
    )


def remote(src, dst, send, recv, axis, place):
    return pltpu.make_async_remote_copy(
        src_ref=src,
        dst_ref=dst,
        send_sem=send,
        recv_sem=recv,
        device_id={axis: place},
        device_id_type=MESH,
    )


def hello_ctx(n, me):
    barrier = pltpu.get_barrier_semaphore()

    def one(i, _):
        pl.semaphore_signal(
            barrier, inc=1, device_id={"ctx": lax.rem(me + i, n)}, device_id_type=MESH
        )
        return 0

    lax.fori_loop(1, n, one, 0)


def hello_tp(places):
    barrier = pltpu.get_barrier_semaphore()
    for place in places:
        pl.semaphore_signal(barrier, inc=1, device_id={"tp": place}, device_id_type=MESH)


def exchange(n, me, src, dst, send, recv, act):
    def one(i, _):
        to = lax.rem(me + i, n)
        back = lax.rem(me - i + n, n)
        if act == "start":
            remote(src.at[to], dst.at[me], send.at[i], recv.at[i], "ctx", to).start()
        else:
            copy = remote(src.at[to], dst.at[back], send.at[i], recv.at[i], "ctx", to)
            copy.wait_recv()
            copy.wait_send()
        return 0

    lax.fori_loop(1, n, one, 0)


def spread(columns, total):
    heads = columns.shape[1]
    size = total // heads
    put = lax.broadcasted_iota(i32, (heads, total), 1) // size == lax.broadcasted_iota(
        i32, (heads, total), 0
    )
    return mm(columns, put.astype(f32), precision=HIGHEST)


def scan_states(n, me, loc, out, totals, rows_per_head, first_head, backward):
    head = first_head + me * loc.shape[1] // rows_per_head
    lane = lax.broadcasted_iota(i32, totals.shape, 2)
    decay = jnp.exp(jnp.sum(jnp.where(lane == head, totals[...], 0.0), axis=2, keepdims=True))
    state = jnp.zeros(loc.shape[1:], f32)
    order = range(n - 1, -1, -1) if backward else range(n)
    for c in order:
        out[c] = state.astype(bf16)
        state = decay[c, 0:1, :] * state + loc[c].astype(f32)


def layer_kernel(
    nx,
    nz,
    ny,
    x_hbm,
    g_hbm,
    ids_hbm,
    prob_hbm,
    counts_hbm,
    u_hbm,
    b_hbm,
    c_hbm,
    ld_hbm,
    wg_hbm,
    wu_hbm,
    wd_hbm,
    w_hbm,
    out_ref,
    scan_ref,
    in_ref,
    out_map_ref,
    x_ref,
    g_ref,
    ids_ref,
    prob_ref,
    counts_ref,
    u_ref,
    b_ref,
    c_ref,
    ld_ref,
    er_ref,
    tail_ref,
    ut_ref,
    decay_ref,
    mix_ref,
    before_ref,
    tot_ref,
    wg,
    wu,
    wd,
    send,
    inbuf,
    part,
    precv,
    rsum,
    gall,
    eg,
    ret,
    pick,
    st_send,
    st_recv,
    back_send,
    tot_send,
    w,
    ya,
    xa,
    hsend,
    hrecv,
    intra,
    gst_send,
    gst_recv,
    gback_send,
    after,
    wsem,
    isem,
    psem,
    ssem,
    gsem,
    fsem,
    rsem,
    sem_s,
    sem_t,
    sem_b,
    usem,
    dsem,
    ysem,
    xsem,
    hfsem,
    hsem,
    gsem_s,
    gsem_b,
    lsem,
):
    n = nx * nz
    me = lax.axis_index("ctx")
    x, z = me // nz, lax.rem(me, nz)
    t = lax.axis_index("tp")
    y, k = t // 2, lax.rem(t, 2)
    sib = y * 2 + (1 - k)
    y_up, y_dn, y_op = lax.rem(y + 1, ny), lax.rem(y + ny - 1, ny), lax.rem(y + 2, ny)
    up, dn = y_up * 2 + k, y_dn * 2 + k

    def ahead(dx, dz):
        return lax.rem(x + dx, nx) * nz + lax.rem(z + dz, nz)

    def behind(dx, dz):
        return lax.rem(x - dx + nx, nx) * nz + lax.rem(z - dz + nz, nz)

    def offset(s, i):
        j = i // nx
        dz = jnp.where(j == 0, s + 1, jnp.where(s == nz // 2 - 1, 0, nz - 1 - s))
        return lax.rem(i, nx), dz

    def target(s, i):
        return ahead(*offset(s, i))

    def origin(s, i):
        return behind(*offset(s, i))

    per = 2 * nx
    stages = nz // 2
    own = (stages - 1, nx)

    cols, tok = x_hbm.shape
    hidden = wg.shape[1]
    cut = wd_hbm.shape[0] // 128 * 128
    loads = [
        pltpu.make_async_copy(wg_hbm, wg.at[pl.ds(0, cols)], wsem.at[0]),
        pltpu.make_async_copy(wu_hbm, wu.at[pl.ds(0, cols)], wsem.at[1]),
        pltpu.make_async_copy(wd_hbm.at[pl.ds(0, cut)], wd.at[pl.ds(0, cut)], wsem.at[2]),
        pltpu.make_async_copy(
            wd_hbm.at[pl.ds(cut, cols - cut)], wd.at[pl.ds(cols, cols - cut)], wsem.at[3]
        ),
    ]
    small = [
        pltpu.make_async_copy(src, dst, lsem.at[i])
        for i, (src, dst) in enumerate(
            (
                (ids_hbm, ids_ref),
                (counts_hbm, counts_ref),
                (x_hbm, x_ref),
                (g_hbm, g_ref),
                (prob_hbm, prob_ref),
                (ld_hbm, ld_ref),
                (u_hbm, u_ref),
                (b_hbm, b_ref),
                (c_hbm, c_ref),
            )
        )
    ]
    for load in small:
        load.start()
    own_w = pltpu.make_async_copy(w_hbm, w.at[z], wsem.at[4])
    own_w.start()
    for load in loads:
        load.start()
    hello_ctx(n, me)
    hello_tp((sib, up, dn))
    for load in small[0:2]:
        load.wait()

    experts = counts_ref.shape[1]
    cap = inbuf.shape[2]
    slots = experts * cap
    rest = cols - cut
    full = cut + 128
    ids = ids_ref[...]
    names = lax.broadcasted_iota(i32, (experts, tok), 0)
    m0 = ids[0:1, :] == names
    m1 = ids[1:2, :] == names
    member = jnp.where(m0, 1.0, 0.0) + jnp.where(m1, 1.0, 0.0)
    t_row = lax.broadcasted_iota(i32, (tok, tok), 0)
    t_col = lax.broadcasted_iota(i32, (tok, tok), 1)
    rank = mm(member.astype(bf16), jnp.where(t_row < t_col, 1.0, 0.0).astype(bf16))
    e_row = lax.broadcasted_iota(i32, (experts, experts), 0)
    e_col = lax.broadcasted_iota(i32, (experts, experts), 1)
    limit = jnp.sum(
        jnp.where(e_row == e_col, counts_ref[...].astype(f32), 0.0), axis=1, keepdims=True
    )
    slot = jnp.where(rank < limit, rank + (names * cap).astype(f32), -1.0)
    place = lax.broadcasted_iota(i32, (slots, tok), 0).astype(f32)
    p0 = jnp.where(place == jnp.sum(jnp.where(m0, slot, 0.0), 0, keepdims=True), 1.0, 0.0)
    p1 = jnp.where(place == jnp.sum(jnp.where(m1, slot, 0.0), 0, keepdims=True), 1.0, 0.0)
    both = (p0 + p1).astype(bf16)
    pick[...] = both

    pl.semaphore_wait(pltpu.get_barrier_semaphore(), n - 1 + 3)
    mid = w.shape[2] // 2
    last_hop = nz // 2 - 1

    def w_copy(j, upward):
        if upward:
            block, to, sem = lax.rem(z - j + nz, nz), ahead(0, 1), usem
        else:
            block, to, sem = lax.rem(z + j, nz), behind(0, 1), dsem
        if j < last_hop:
            at = w.at[block]
        else:
            at = w.at[block, :, pl.ds(0 if upward else mid, mid)]
        return remote(at, at, sem.at[0, j], sem.at[1, j], "ctx", to)

    def w_landed(j):
        for upward, sem in ((True, usem), (False, dsem)):
            block = lax.rem(z - j - 1 + nz, nz) if upward else lax.rem(z + j + 1, nz)
            if j < last_hop:
                at = w.at[block]
            else:
                at = w.at[block, :, pl.ds(0 if upward else mid, mid)]
            remote(at, at, sem.at[0, j], sem.at[1, j], "ctx", ahead(0, 1)).wait_recv()

    def w_hop(j):
        if j:
            w_landed(j - 1)
        w_copy(j, True).start()
        w_copy(j, False).start()

    for load in small[2:]:
        load.wait()
    grad = g_ref[...].astype(f32)
    prob = prob_ref[...]
    scaled = jnp.concatenate(
        [(prob[0:1, :] * grad).astype(bf16), (prob[1:2, :] * grad).astype(bf16)], axis=1
    )
    pair = jnp.concatenate([p0.astype(bf16), p1.astype(bf16)], axis=1)
    sel_x = mm(both, x_ref[...], 1, 1)
    sel_g = mm(pair, scaled, 1, 1)
    send[:, :, 0:cut] = sel_x[:, 0:cut].astype(bf16).reshape(experts, cap, cut)
    send[:, :, cut : 2 * cut] = sel_g[:, 0:cut].astype(bf16).reshape(experts, cap, cut)
    last = jnp.concatenate(
        [sel_x[:, cut:], sel_g[:, cut:], jnp.zeros((slots, 128 - 2 * rest), f32)], axis=1
    )
    send[:, :, 2 * cut :] = last.astype(bf16).reshape(experts, cap, 128)

    def in_copy(s, j):
        to = target(s, j)
        at = s * per + j
        return remote(
            send.at[to], inbuf.at[s, j], isem.at[0, at], isem.at[1, at], "ctx", to
        )

    def post(i, _):
        s, j = i // per, lax.rem(i, per)

        @pl.when(i != own[0] * per + own[1])
        def _():
            in_copy(s, j).start()

        return 0

    lax.fori_loop(0, per, post, 0)
    inbuf[own] = send[me]

    heads = ld_ref.shape[0]
    width = u_ref.shape[1]
    log = ld_ref[...]
    upto = jnp.where(t_row >= t_col, 1.0, 0.0)
    run = mm(upto, log, 1, 1, precision=HIGHEST)
    run_t = mm(log, upto, 1, 1, precision=HIGHEST)
    total = run[tok - 1 : tok, :]
    tail_x = spread(jnp.exp(total - run), width)
    tail_ref[...] = tail_x
    ut = (u_ref[...].astype(f32) * tail_x).astype(bf16)
    ut_ref[...] = ut
    st_send[...] = mm(ut, b_ref[...], 0, 0).astype(bf16).reshape(st_send.shape)
    tot_send[...] = jnp.concatenate(
        [
            jnp.broadcast_to(total, (tot_send.shape[0], heads)),
            jnp.zeros((tot_send.shape[0], tot_send.shape[1] - heads), f32),
        ],
        axis=1,
    )

    def totals(act):
        def one(i, _):
            to = lax.rem(me + i, n)
            back = lax.rem(me - i + n, n)
            if act == "start":
                remote(
                    tot_send, tot_ref.at[me], sem_t.at[0, i], sem_t.at[1, i], "ctx", to
                ).start()
            else:
                copy = remote(
                    tot_send, tot_ref.at[back], sem_t.at[0, i], sem_t.at[1, i], "ctx", to
                )
                copy.wait_recv()
                copy.wait_send()
            return 0

        lax.fori_loop(1, n, one, 0)


    wg[pl.ds(cols, 128 - rest), :] = jnp.zeros((128 - rest, hidden), bf16)
    wu[pl.ds(cols, 128 - rest), :] = jnp.zeros((128 - rest, hidden), bf16)
    wd[pl.ds(cut, rest), :] = jnp.zeros((rest, hidden), bf16)
    wd[pl.ds(cols + rest, 128 - 2 * rest), :] = jnp.zeros((128 - 2 * rest, hidden), bf16)
    for load in loads:
        load.wait()

    er_ref[...] = spread(jnp.exp(run), width)
    affinity = mm(c_ref[...], b_ref[...], 1, 1)
    for h in range(heads):
        gap = run[:, h : h + 1] - run_t[h : h + 1, :]
        decay = jnp.where(t_row >= t_col, jnp.exp(jnp.where(t_row >= t_col, gap, 0.0)), 0.0)
        decay_ref[h] = decay.astype(bf16)
        mix_ref[h] = (decay * affinity).astype(bf16)

    half = per // 2 * cap
    mine, other = pl.multiple_of(k * half, cap), pl.multiple_of((1 - k) * half, cap)

    def pair_copy(s, p):
        return remote(
            part.at[s, p, pl.ds(other, half)],
            precv.at[s, p],
            psem.at[0, s, p],
            psem.at[1, s, p],
            "tp",
            sib,
        )

    side = hidden // 2
    lows, highs = pl.ds(0, side), pl.ds(side, side)

    def chunk(dz):
        return pl.ds(pl.multiple_of(mine + dz * cap, cap), cap)

    def sum_copy(s, i):
        src = (
            part.at[s, :, chunk(y_op), lows],
            part.at[s, :, chunk(y_op), highs],
            part.at[s, :, chunk(y_up), highs],
            part.at[s, :, chunk(y_dn), lows],
            rsum.at[s, 6],
            rsum.at[s, 7],
        )[i]
        return remote(
            src, rsum.at[s, i], ssem.at[0, s, i], ssem.at[1, s, i], "tp", (up, dn)[i % 2]
        )

    def grads_at(s, core, dz):
        return gall.at[s, pl.ds(pl.multiple_of(core * half + dz * cap, cap), cap)]

    froms = (y_dn, y_up, y_op)

    def grad_copy(s, i, dz):
        at = gall.at[s, chunk(dz)]
        if i >= 2:
            at = gall.at[s, chunk(dz), pl.ds((i - 2) * hidden, hidden)]
        return remote(at, at, gsem.at[0, s, i], gsem.at[1, s, i], "tp", (up, dn)[i % 2])

    def fwd_copy(s, i, core, dz):
        at = grads_at(s, core, dz)
        return remote(at, at, fsem.at[0, s, i], fsem.at[1, s, i], "tp", sib)

    def first(s):
        def one(i, _):
            @pl.when(jnp.logical_and(i == per // 2, jnp.logical_and(s != 1, s + 1 < stages)))
            def _():
                lax.fori_loop((s + 1) * per, (s + 2) * per, post, 0)

            @pl.when(s * per + i != own[0] * per + own[1])
            def _():
                in_copy(s, i).wait_recv()

            return 0

        lax.fori_loop(0, per, one, 0)
        rows = inbuf[s].reshape(per * cap, 2 * cut + 128)
        lasts = rows[:, 2 * cut :]
        for p, w in enumerate((wg, wu, wd)):
            lo = 0 if p < 2 else cut
            got = mm(rows[:, lo : lo + cut], w[0:cut, :]) + mm(lasts, w[cut:full, :])
            part[s, p] = got.astype(bf16)
            pair_copy(s, p).start()

    def second(s):
        for p in range(3):
            pair_copy(s, p).wait_recv()
            at = pl.ds(mine, half)
            part[s, p, at] = (part[s, p, at].astype(f32) + precv[s, p].astype(f32)).astype(bf16)
        for i in range(4):
            sum_copy(s, i).start()

    def relay(s):
        for i, (dz, at) in enumerate(((y_up, lows), (y_dn, highs))):
            sum_copy(s, i).wait_recv()
            rsum[s, 6 + i] = (
                part[s, :, chunk(dz), at].astype(f32) + rsum[s, i].astype(f32)
            ).astype(bf16)
            sum_copy(s, 4 + i).start()

    def third(s):
        for i in range(2, 6):
            sum_copy(s, i).wait_recv()
        for e, at, near, far in ((0, lows, 3, 4), (1, highs, 2, 5)):
            total = (
                part[s, :, chunk(y), at].astype(f32)
                + rsum[s, near].astype(f32)
                + rsum[s, far].astype(f32)
            )
            gate, upv, back = total[0], total[1], total[2]
            sigma = 1.0 / (1.0 + jnp.exp(-gate))
            lo, hi = pl.ds(e * side, side), pl.ds(hidden + e * side, side)
            gall[s, chunk(y), lo] = (back * upv * sigma * (1.0 + gate * (1.0 - sigma))).astype(bf16)
            gall[s, chunk(y), hi] = (back * gate * sigma).astype(bf16)
        for i in range(2):
            grad_copy(s, i, y).start()
        fwd_copy(s, 3, k, y).start()

    def fourth(s):
        for i in range(2):
            grad_copy(s, i, froms[i]).wait_recv()
            grad_copy(s, 2 + i, froms[i]).start()
            fwd_copy(s, i, k, froms[i]).start()

    def gathered(s):
        for i in range(2):
            grad_copy(s, 2 + i, y_op).wait_recv()
        fwd_copy(s, 2, k, y_op).start()

    def fifth(s):
        for i in range(3):
            fwd_copy(s, i, 1 - k, froms[i]).wait_recv()
        fwd_copy(s, 3, 1 - k, y).wait_recv()
        grad = mm(gall[s, :, 0:hidden], wg[0:cols, :], 1, 1) + mm(
            gall[s, :, hidden : 2 * hidden], wu[0:cols, :], 1, 1
        )
        eg[s] = grad.astype(bf16).reshape(per, cap, cols)

        def one(i, _):
            @pl.when(s * per + i != own[0] * per + own[1])
            def _():
                back_copy(s, i).start()

            return 0

        lax.fori_loop(0, per, one, 0)

    def back_copy(s, i):
        at = s * per + i
        return remote(
            eg.at[s, i], ret.at[me], rsem.at[0, at], rsem.at[1, at], "ctx", origin(s, i)
        )

    def back_landed(s, i):
        at, it = s * per + i, target(s, i)
        return remote(eg.at[s, i], ret.at[it], rsem.at[0, at], rsem.at[1, at], "ctx", it)

    def stage(s, _):
        second(s)

        @pl.when(s > 0)
        def _():
            fourth(s - 1)

        @pl.when(s > 1)
        def _():
            fifth(s - 2)

        relay(s)

        @pl.when(s == 0)
        def _():
            lax.fori_loop(2 * per, 3 * per, post, 0)

        @pl.when(s > 0)
        def _():
            gathered(s - 1)

        @pl.when(s + 1 < stages)
        def _():
            first(s + 1)

        @pl.when(s == stages - 2)
        def _():
            w_hop(0)

        @pl.when(s == stages - 1)
        def _():
            fifth(s - 1)

        third(s)
        return 0

    own_w.wait()
    first(0)
    lax.fori_loop(0, stages, stage, 0)
    fourth(stages - 1)
    w_hop(1)
    gathered(stages - 1)
    fifth(stages - 1)
    ret[me] = eg[own]

    def each(act):
        def one(i, _):
            @pl.when(i != own[0] * per + own[1])
            def _():
                act(i // per, lax.rem(i, per))

            return 0

        lax.fori_loop(0, n, one, 0)

    each(lambda a, b: back_landed(a, b).wait_recv())
    w_hop(2)
    entries = ret[...].reshape(slots, cols)
    input_grad = g_ref[...].astype(f32) + mm(entries, pick[...], 0, 0)
    ya[y] = input_grad.reshape(nz // 2, cols // (nz // 2), tok).astype(bf16)

    def y_copy(i, dz):
        at = ya.at[dz]
        if i >= 2:
            at = ya.at[dz, pl.ds((i - 2) * (nz // 4), nz // 4)]
        return remote(at, at, ysem.at[0, i], ysem.at[1, i], "tp", (up, dn)[i % 2])

    def x_copy(place, source):
        return remote(
            ya.at[place],
            xa.at[source, k],
            xsem.at[0, place],
            xsem.at[1, source],
            "ctx",
            place * nz + z,
        )

    def f_copy(source, core):
        at = xa.at[source, core]
        return remote(at, at, hfsem.at[0, source], hfsem.at[1, source], "tp", sib)

    def pass_on(place):
        @pl.when(place != x)
        def _():
            x_copy(place, x).start()

        @pl.when(place == x)
        def _():
            xa[x, k] = ya[place]
            f_copy(x, k).start()

    for i in range(2):
        y_copy(i, y).start()
    pass_on(y)
    out_ref[...] = input_grad.astype(bf16)
    for i in range(2):
        y_copy(i, froms[i]).wait_recv()
        y_copy(2 + i, froms[i]).start()
        pass_on(froms[i])
    for i in range(2):
        y_copy(2 + i, y_op).wait_recv()
    pass_on(y_op)

    def x_at(d):
        return lax.rem(x + d, nx)

    wide = width // 2
    quarter = wide // 2

    def product(source, hf):
        total = jnp.zeros((tok, wide), f32)
        for b in range(nz):
            part_x = xa[source, b // (nz // 2), b % (nz // 2)]
            total = total + mm(part_x, w[b, :, pl.ds(hf * wide, wide)], 0, 0)
        return total

    x_up, x_dn, x_op = x_at(1), x_at(nx - 1), x_at(2)
    def quart(hf, q):
        return pl.ds(hf * wide + q * quarter, quarter)

    def h_copy(hf, i):
        src, q = ((0, 0), (0, 1), (1, 1), (2, 0), (1, 0), (2, 1))[i]
        return remote(
            hsend.at[src, :, quart(hf, q)],
            hrecv.at[hf, i],
            hsem.at[0, hf, i],
            hsem.at[1, hf, i],
            "ctx",
            (x_up, x_dn)[i % 2] * nz + z,
        )

    order = [2, 1, nx - 1]
    w_hop(3)
    for d in order:
        source = x_at(d)
        x_copy(x, source).wait_recv()
        f_copy(source, k).start()
    totals("start")
    exchange(n, me, st_send, st_recv, sem_s.at[0], sem_s.at[1], "start")
    st_recv[me] = st_send[me]
    tot_ref[me] = tot_send[...]
    size = width // heads
    w_landed(3)
    for hf in range(2):
        for i, d in enumerate(order):
            source = x_at(d)
            if hf == 0:
                f_copy(source, 1 - k).wait_recv()
            hsend[i, :, pl.ds(hf * wide, wide)] = product(source, hf).astype(bf16)
            if i == 0:
                h_copy(hf, 0).start()
                h_copy(hf, 1).start()
            else:
                h_copy(hf, 1 + i).start()

    def h_relay(hf):
        for i in range(2):
            h_copy(hf, i).wait_recv()
            at = quart(hf, i)
            hsend[1 + i, :, at] = (
                hsend[1 + i, :, at].astype(f32) + hrecv[hf, i].astype(f32)
            ).astype(bf16)
            h_copy(hf, 4 + i).start()

    h_relay(0)
    f_copy(x, 1 - k).wait_recv()
    wholes = [product(x, 0), product(x, 1)]
    h_relay(1)
    totals("wait")
    exchange(n, me, st_send, st_recv, sem_s.at[0], sem_s.at[1], "wait")
    scan_states(n, me, st_recv, back_send, tot_ref, size, 0, False)
    exchange(n, me, back_send, before_ref, sem_b.at[0], sem_b.at[1], "start")
    before_ref[me] = back_send[me]

    weights = jnp.zeros((tok, tok), f32)
    some = heads // 2
    weighted = []
    for hf in range(2):
        for i in range(2, 6):
            h_copy(hf, i).wait_recv()
        grad = (
            wholes[hf]
            + jnp.concatenate(
                [
                    hrecv[hf, 4].astype(f32) + hrecv[hf, 3].astype(f32),
                    hrecv[hf, 2].astype(f32) + hrecv[hf, 5].astype(f32),
                ],
                axis=1,
            )
        ).astype(bf16)
        ge = (grad.astype(f32) * er_ref[:, hf * wide : (hf + 1) * wide]).astype(bf16)
        weighted.append(ge)
        gst_send[hf] = mm(ge, c_ref[...], 0, 0).astype(bf16).reshape(gst_send.shape[1:])
        exchange(
            n, me, gst_send.at[hf], gst_recv.at[hf], gsem_s.at[0, hf], gsem_s.at[1, hf], "start"
        )
        gst_recv[hf, me] = gst_send[hf, me]
        for j in range(some):
            h = hf * some + j
            gh = grad[:, j * size : (j + 1) * size]
            uh = u_ref[:, h * size : (h + 1) * size]
            weights = weights + decay_ref[h].astype(f32) * mm(gh, uh, 1, 1)
            intra[:, h * size : (h + 1) * size] = mm(mix_ref[h], gh, 0, 0)
    weights = weights.astype(bf16)
    state = b_ref.shape[1]

    for hf in range(2):
        exchange(
            n, me, gst_send.at[hf], gst_recv.at[hf], gsem_s.at[0, hf], gsem_s.at[1, hf], "wait"
        )
        scan_states(
            n, me, gst_recv.at[hf], gback_send.at[hf], tot_ref, size, hf * some, True
        )
        exchange(
            n, me, gback_send.at[hf], after.at[hf], gsem_b.at[0, hf], gsem_b.at[1, hf], "start"
        )
        after[hf, me] = gback_send[hf, me]

    exchange(n, me, back_send, before_ref, sem_b.at[0], sem_b.at[1], "wait")
    before = before_ref[...].reshape(-1, state)
    out_map_ref[...] = (
        mm(weights, b_ref[...])
        + mm(weighted[0], before[0 : some * size])
        + mm(weighted[1], before[some * size :])
    )
    in_part = mm(weights, c_ref[...], 0, 0)

    def settle(s, _):
        for p in range(3):
            pair_copy(s, p).wait_send()
        for i in range(6):
            sum_copy(s, i).wait_send()
        for i in range(4):
            grad_copy(s, i, y).wait_send()
        for i in range(3):
            fwd_copy(s, i, k, froms[i]).wait_send()
        fwd_copy(s, 3, k, y).wait_send()
        return 0

    lax.fori_loop(0, stages, settle, 0)

    each(lambda a, b: in_copy(a, b).wait_send())
    each(lambda a, b: back_copy(a, b).wait_send())
    for j in range(nz // 2):
        w_copy(j, True).wait_send()
        w_copy(j, False).wait_send()
    for i in range(4):
        y_copy(i, y).wait_send()
    for d in order:
        x_copy(x_at(d), x).wait_send()
    for hf in range(2):
        for i in range(6):
            h_copy(hf, i).wait_send()
    for d in range(nx):
        f_copy(x_at(d), k).wait_send()

    for hf in range(2):
        exchange(
            n, me, gback_send.at[hf], after.at[hf], gsem_b.at[0, hf], gsem_b.at[1, hf], "wait"
        )
        later = after[hf].reshape(-1, state)
        at = pl.ds(hf * wide, wide)
        in_part = in_part + mm(ut_ref[:, at], later)
        scan_ref[:, at] = (
            intra[:, at] + tail_ref[:, at] * mm(b_ref[...], later, 1, 1)
        ).astype(bf16)
    in_ref[...] = in_part


def layer(
    sizes, moe_t, grad_t, ids_t, prob_t, counts, ssd_input, in_map, out_map, log_t, wg, wu, wd, w
):
    nx, nz, ny = sizes
    n = nx * nz
    cols, tok = moe_t.shape
    experts = counts.shape[1]
    cap = 2 * tok * ids_t.shape[0] // experts
    heads = log_t.shape[0]
    width = ssd_input.shape[1]
    state = in_map.shape[1]
    hidden = wg.shape[1]
    part = width // n
    cut = cols // 128 * 128
    full = cut + 128
    per, stages = 2 * nx, nz // 2
    rows = per * cap
    small = jax.ShapeDtypeStruct((tok, state), f32)
    halves = pltpu.VMEM((2, n, part // 2, state), bf16)
    states = pltpu.VMEM((n, part, state), bf16)
    pairs = DMA((2, n))
    return pl.pallas_call(
        functools.partial(layer_kernel, nx, nz, ny),
        out_shape=(
            jax.ShapeDtypeStruct((cols, tok), bf16),
            jax.ShapeDtypeStruct((tok, width), bf16),
            small,
            small,
        ),
        in_specs=[HBM] * 13,
        out_specs=[VMEM] * 4,
        scratch_shapes=[
            pltpu.VMEM((cols, tok), bf16),
            pltpu.VMEM((cols, tok), bf16),
            pltpu.VMEM(ids_t.shape, i32),
            pltpu.VMEM(prob_t.shape, f32),
            pltpu.VMEM(counts.shape, i32),
            pltpu.VMEM((tok, width), bf16),
            pltpu.VMEM((tok, state), bf16),
            pltpu.VMEM((tok, state), bf16),
            pltpu.VMEM(log_t.shape, f32),
            pltpu.VMEM((tok, width), f32),
            pltpu.VMEM((tok, width), f32),
            pltpu.VMEM((tok, width), bf16),
            pltpu.VMEM((heads, tok, tok), bf16),
            pltpu.VMEM((heads, tok, tok), bf16),
            states,
            pltpu.VMEM((n, 8, 128), f32),
            pltpu.VMEM((full, hidden), bf16),
            pltpu.VMEM((full, hidden), bf16),
            pltpu.VMEM((full, hidden), bf16),
            pltpu.VMEM((n, cap, 2 * cut + 128), bf16),
            pltpu.VMEM((stages, per, cap, 2 * cut + 128), bf16),
            pltpu.VMEM((stages, 3, rows, hidden), bf16),
            pltpu.VMEM((stages, 3, rows // 2, hidden), bf16),
            pltpu.VMEM((stages, 8, 3, cap, hidden // 2), bf16),
            pltpu.VMEM((stages, rows, 2 * hidden), bf16),
            pltpu.VMEM((stages, per, cap, cols), bf16),
            pltpu.VMEM((n, cap, cols), bf16),
            pltpu.VMEM((experts * cap, tok), bf16),
            states,
            states,
            states,
            pltpu.VMEM((8, 128), f32),
            pltpu.VMEM((nz, w.shape[0], width), bf16),
            pltpu.VMEM((ny, nz // 2, w.shape[0], tok), bf16),
            pltpu.VMEM((nx, 2, nz // 2, w.shape[0], tok), bf16),
            pltpu.VMEM((3, tok, width), bf16),
            pltpu.VMEM((2, 6, tok, width // 4), bf16),
            pltpu.VMEM((tok, width), f32),
            halves,
            halves,
            halves,
            halves,
            DMA((5,)),
            pairs,
            DMA((2, stages, 3)),
            DMA((2, stages, 6)),
            DMA((2, stages, 4)),
            DMA((2, stages, 4)),
            pairs,
            pairs,
            pairs,
            pairs,
            DMA((2, nz // 2)),
            DMA((2, nz // 2)),
            DMA((2, 4)),
            DMA((2, nx)),
            DMA((2, nx)),
            DMA((2, 2, 6)),
            DMA((2, 2, n)),
            DMA((2, 2, n)),
            DMA((9,)),
        ],
        compiler_params=pltpu.CompilerParams(
            collective_id=0, has_side_effects=True, vmem_limit_bytes=56 * 2**20
        ),
        name="layer",
    )(moe_t, grad_t, ids_t, prob_t, counts, ssd_input, in_map, out_map, log_t, wg, wu, wd, w)


def body(
    moe_input,
    out_grad,
    route_prob,
    route_ids,
    route_counts,
    w_gate,
    w_up,
    w_down,
    out_weight,
    ssd_input,
    input_map,
    output_map,
    log_decay,
):
    n = lax.axis_size("ctx")
    ny = lax.axis_size("tp") // 2
    nx = ny
    nz = n // nx
    grad_t, scan_grad, in_map_grad, out_map_grad = layer(
        (nx, nz, ny),
        moe_input.T,
        out_grad.T,
        route_ids.T,
        route_prob.T,
        route_counts,
        ssd_input,
        input_map,
        output_map,
        log_decay.T,
        w_gate[0],
        w_up[0],
        w_down[0].T,
        out_weight,
    )
    return (grad_t.T, scan_grad, in_map_grad, out_map_grad)


def solution(mesh):
    in_specs = (
        P("ctx", "tp"),
        P("ctx", "tp"),
        P("ctx", None),
        P("ctx", None),
        P("ctx", None),
        P("ctx", "tp", None),
        P("ctx", "tp", None),
        P("ctx", None, "tp"),
        P("ctx", "tp"),
        P("ctx", "tp"),
        P("ctx", "tp"),
        P("ctx", "tp"),
        P("ctx", "tp"),
    )
    out_specs = (P("ctx", "tp"), P("ctx", "tp"), P("ctx", "tp"), P("ctx", "tp"))
    return jax.shard_map(body, mesh=mesh, in_specs=in_specs, out_specs=out_specs, check_vma=False)
```

```python
import functools

import jax
import jax.numpy as jnp
from jax import lax
from jax.experimental import pallas as pl
from jax.experimental.pallas import tpu as pltpu
from jax.sharding import PartitionSpec as P

MESH = pl.DeviceIdType.MESH
HIGHEST = lax.Precision.HIGHEST
bf16, f32, i32 = jnp.bfloat16, jnp.float32, jnp.int32
VMEM = pl.BlockSpec(memory_space=pltpu.VMEM)
HBM = pl.BlockSpec(memory_space=pltpu.HBM)
DMA = pltpu.SemaphoreType.DMA


def mm(a, b, ca=1, cb=0, precision=None):
    return lax.dot_general(
        a, b, (((ca,), (cb,)), ((), ())), precision=precision, preferred_element_type=f32
    )


def remote(src, dst, send, recv, axis, place):
    return pltpu.make_async_remote_copy(
        src_ref=src,
        dst_ref=dst,
        send_sem=send,
        recv_sem=recv,
        device_id={axis: place},
        device_id_type=MESH,
    )


def hello_ctx(n, me):
    barrier = pltpu.get_barrier_semaphore()

    def one(i, _):
        pl.semaphore_signal(
            barrier, inc=1, device_id={"ctx": lax.rem(me + i, n)}, device_id_type=MESH
        )
        return 0

    lax.fori_loop(1, n, one, 0)


def hello_tp(places):
    barrier = pltpu.get_barrier_semaphore()
    for place in places:
        pl.semaphore_signal(barrier, inc=1, device_id={"tp": place}, device_id_type=MESH)


def exchange(n, me, src, dst, sems, act):
    if act == "wait":
        copy = remote(
            src.at[pl.ds(0, n - 1)],
            dst.at[pl.ds(0, n - 1)],
            sems.at[0],
            sems.at[1],
            "ctx",
            lax.rem(me + 1, n),
        )
        copy.wait_recv()
        copy.wait_send()
        return

    def one(i, _):
        to = lax.rem(me + i, n)
        remote(src.at[to], dst.at[me], sems.at[0], sems.at[1], "ctx", to).start()
        return 0

    lax.fori_loop(1, n, one, 0)


def spread(columns, total):
    heads = columns.shape[1]
    size = total // heads
    put = lax.broadcasted_iota(i32, (heads, total), 1) // size == lax.broadcasted_iota(
        i32, (heads, total), 0
    )
    return mm(columns, put.astype(f32), precision=HIGHEST)


def scan_states(n, me, loc, out, totals, rows_per_head, first_head, backward):
    head = first_head + me * loc.shape[1] // rows_per_head
    lane = lax.broadcasted_iota(i32, totals.shape, 2)
    decay = jnp.exp(jnp.sum(jnp.where(lane == head, totals[...], 0.0), axis=2, keepdims=True))
    state = jnp.zeros(loc.shape[1:], f32)
    order = range(n - 1, -1, -1) if backward else range(n)
    for c in order:
        out[c] = state.astype(bf16)
        state = decay[c, 0:1, :] * state + loc[c].astype(f32)


def layer_kernel(
    nx,
    nz,
    ny,
    x_hbm,
    g_hbm,
    ids_hbm,
    prob_hbm,
    counts_hbm,
    u_hbm,
    b_hbm,
    c_hbm,
    ld_hbm,
    wg_hbm,
    wu_hbm,
    wd_hbm,
    w_hbm,
    out_ref,
    scan_ref,
    in_ref,
    out_map_ref,
    x_ref,
    g_ref,
    ids_ref,
    prob_ref,
    counts_ref,
    u_ref,
    b_ref,
    c_ref,
    ld_ref,
    er_ref,
    tail_ref,
    ut_ref,
    decay_ref,
    mix_ref,
    before_ref,
    tot_ref,
    wg,
    wu,
    wd,
    send,
    inbuf,
    part,
    precv,
    rsum,
    gall,
    eg,
    ret,
    pick,
    st_send,
    st_recv,
    back_send,
    tot_send,
    w,
    ya,
    xa,
    hsend,
    hrecv,
    intra,
    gst_send,
    gst_recv,
    gback_send,
    after,
    wsem,
    isem,
    psem,
    ssem,
    gsem,
    fsem,
    rsem,
    sem_s,
    sem_t,
    sem_b,
    usem,
    dsem,
    ysem,
    xsem,
    hfsem,
    hsem,
    gsem_s,
    gsem_b,
    lsem,
):
    n = nx * nz
    me = lax.axis_index("ctx")
    x, z = me // nz, lax.rem(me, nz)
    t = lax.axis_index("tp")
    y, k = t // 2, lax.rem(t, 2)
    sib = y * 2 + (1 - k)
    y_up, y_dn, y_op = lax.rem(y + 1, ny), lax.rem(y + ny - 1, ny), lax.rem(y + 2, ny)
    up, dn = y_up * 2 + k, y_dn * 2 + k

    def ahead(dx, dz):
        return lax.rem(x + dx, nx) * nz + lax.rem(z + dz, nz)

    def behind(dx, dz):
        return lax.rem(x - dx + nx, nx) * nz + lax.rem(z - dz + nz, nz)

    def offset(s, i):
        j = i // nx
        dz = jnp.where(j == 0, s + 1, jnp.where(s == nz // 2 - 1, 0, nz - 1 - s))
        return lax.rem(i, nx), dz

    def target(s, i):
        return ahead(*offset(s, i))

    def origin(s, i):
        return behind(*offset(s, i))

    per = 2 * nx
    stages = nz // 2
    own = (stages - 1, nx)

    cols, tok = x_hbm.shape
    hidden = wg.shape[1]
    cut = wd_hbm.shape[0] // 128 * 128
    loads = [
        pltpu.make_async_copy(wg_hbm, wg.at[pl.ds(0, cols)], wsem.at[0]),
        pltpu.make_async_copy(wu_hbm, wu.at[pl.ds(0, cols)], wsem.at[1]),
        pltpu.make_async_copy(wd_hbm.at[pl.ds(0, cut)], wd.at[pl.ds(0, cut)], wsem.at[2]),
        pltpu.make_async_copy(
            wd_hbm.at[pl.ds(cut, cols - cut)], wd.at[pl.ds(cols, cols - cut)], wsem.at[3]
        ),
    ]
    small = [
        pltpu.make_async_copy(src, dst, lsem.at[i])
        for i, (src, dst) in enumerate(
            (
                (ids_hbm, ids_ref),
                (counts_hbm, counts_ref),
                (x_hbm, x_ref),
                (g_hbm, g_ref),
                (prob_hbm, prob_ref),
                (ld_hbm, ld_ref),
                (u_hbm, u_ref),
                (b_hbm, b_ref),
                (c_hbm, c_ref),
            )
        )
    ]
    for load in small:
        load.start()
    own_w = pltpu.make_async_copy(w_hbm, w.at[z], wsem.at[4])
    own_w.start()
    for load in loads:
        load.start()
    hello_ctx(n, me)
    hello_tp((sib, up, dn))
    for load in small[0:2]:
        load.wait()

    experts = counts_ref.shape[1]
    cap = inbuf.shape[2]
    slots = experts * cap
    rest = cols - cut
    full = cut + 128
    ids = ids_ref[...]
    names = lax.broadcasted_iota(i32, (experts, tok), 0)
    m0 = ids[0:1, :] == names
    m1 = ids[1:2, :] == names
    member = jnp.where(m0, 1.0, 0.0) + jnp.where(m1, 1.0, 0.0)
    t_row = lax.broadcasted_iota(i32, (tok, tok), 0)
    t_col = lax.broadcasted_iota(i32, (tok, tok), 1)
    rank = mm(member.astype(bf16), jnp.where(t_row < t_col, 1.0, 0.0).astype(bf16))
    e_row = lax.broadcasted_iota(i32, (experts, experts), 0)
    e_col = lax.broadcasted_iota(i32, (experts, experts), 1)
    limit = jnp.sum(
        jnp.where(e_row == e_col, counts_ref[...].astype(f32), 0.0), axis=1, keepdims=True
    )
    slot = jnp.where(rank < limit, rank + (names * cap).astype(f32), -1.0)
    place = lax.broadcasted_iota(i32, (slots, tok), 0).astype(f32)
    p0 = jnp.where(place == jnp.sum(jnp.where(m0, slot, 0.0), 0, keepdims=True), 1.0, 0.0)
    p1 = jnp.where(place == jnp.sum(jnp.where(m1, slot, 0.0), 0, keepdims=True), 1.0, 0.0)
    both = (p0 + p1).astype(bf16)
    pick[...] = both

    pl.semaphore_wait(pltpu.get_barrier_semaphore(), n - 1 + 3)
    mid = w.shape[2] // 2
    last_hop = nz // 2 - 1

    def w_part(hf, j, block, upward):
        if j < last_hop:
            return w.at[block, :, pl.ds(hf * mid, mid)]
        return w.at[block, :, pl.ds(hf * mid + (0 if upward else mid // 2), mid // 2)]

    def w_copy(hf, j, upward):
        if upward:
            block, to, sem = lax.rem(z - j + nz, nz), ahead(0, 1), usem
        else:
            block, to, sem = lax.rem(z + j, nz), behind(0, 1), dsem
        at = w_part(hf, j, block, upward)
        return remote(at, at, sem.at[0, hf, j], sem.at[1, hf, j], "ctx", to)

    def w_landed(hf, j):
        for upward, sem in ((True, usem), (False, dsem)):
            block = lax.rem(z - j - 1 + nz, nz) if upward else lax.rem(z + j + 1, nz)
            at = w_part(hf, j, block, upward)
            remote(at, at, sem.at[0, hf, j], sem.at[1, hf, j], "ctx", ahead(0, 1)).wait_recv()

    def w_hop(hf, j):
        if j:
            w_landed(hf, j - 1)
        w_copy(hf, j, True).start()
        w_copy(hf, j, False).start()

    for load in small[2:]:
        load.wait()
    grad = g_ref[...].astype(f32)
    prob = prob_ref[...]
    scaled = jnp.concatenate(
        [(prob[0:1, :] * grad).astype(bf16), (prob[1:2, :] * grad).astype(bf16)], axis=1
    )
    pair = jnp.concatenate([p0.astype(bf16), p1.astype(bf16)], axis=1)
    sel_x = mm(both, x_ref[...], 1, 1)
    sel_g = mm(pair, scaled, 1, 1)
    send[:, :, 0:cut] = sel_x[:, 0:cut].astype(bf16).reshape(experts, cap, cut)
    send[:, :, cut : 2 * cut] = sel_g[:, 0:cut].astype(bf16).reshape(experts, cap, cut)
    last = jnp.concatenate(
        [sel_x[:, cut:], sel_g[:, cut:], jnp.zeros((slots, 128 - 2 * rest), f32)], axis=1
    )
    send[:, :, 2 * cut :] = last.astype(bf16).reshape(experts, cap, 128)

    def in_copy(s, j):
        to = target(s, j)
        at = 2 * s + j // (per // 2)
        return remote(send.at[to], inbuf.at[s, j], isem.at[2 * stages], isem.at[at], "ctx", to)

    def post(i, _):
        s, j = i // per, lax.rem(i, per)

        @pl.when(i != own[0] * per + own[1])
        def _():
            in_copy(s, j).start()

        return 0

    lax.fori_loop(0, per, post, 0)
    inbuf[own] = send[me]

    heads = ld_ref.shape[0]
    width = u_ref.shape[1]
    log = ld_ref[...]
    upto = jnp.where(t_row >= t_col, 1.0, 0.0)
    run = mm(upto, log, 1, 1, precision=HIGHEST)
    run_t = mm(log, upto, 1, 1, precision=HIGHEST)
    total = run[tok - 1 : tok, :]
    tail_x = spread(jnp.exp(total - run), width)
    tail_ref[...] = tail_x
    ut = (u_ref[...].astype(f32) * tail_x).astype(bf16)
    ut_ref[...] = ut
    st_send[...] = mm(ut, b_ref[...], 0, 0).astype(bf16).reshape(st_send.shape)
    tot_send[...] = jnp.broadcast_to(
        jnp.concatenate([total, jnp.zeros((1, tot_send.shape[2] - heads), f32)], axis=1)[None],
        tot_send.shape,
    )
    exchange(n, me, tot_send, tot_ref, sem_t, "start")
    tot_ref[me] = tot_send[me]

    wg[pl.ds(cols, 128 - rest), :] = jnp.zeros((128 - rest, hidden), bf16)
    wu[pl.ds(cols, 128 - rest), :] = jnp.zeros((128 - rest, hidden), bf16)
    wd[pl.ds(cut, rest), :] = jnp.zeros((rest, hidden), bf16)
    wd[pl.ds(cols + rest, 128 - 2 * rest), :] = jnp.zeros((128 - 2 * rest, hidden), bf16)
    for load in loads:
        load.wait()

    er_ref[...] = spread(jnp.exp(run), width)
    affinity = mm(c_ref[...], b_ref[...], 1, 1)
    for h in range(heads):
        gap = run[:, h : h + 1] - run_t[h : h + 1, :]
        decay = jnp.where(t_row >= t_col, jnp.exp(jnp.where(t_row >= t_col, gap, 0.0)), 0.0)
        decay_ref[h] = decay.astype(bf16)
        mix_ref[h] = (decay * affinity).astype(bf16)

    half = per // 2 * cap
    mine, other = pl.multiple_of(k * half, cap), pl.multiple_of((1 - k) * half, cap)

    def pair_copy(s, p):
        return remote(
            part.at[s, p, pl.ds(other, half)],
            precv.at[s, p],
            psem.at[0, s, p],
            psem.at[1, s, p],
            "tp",
            sib,
        )

    side = hidden // 2
    lows, highs = pl.ds(0, side), pl.ds(side, side)

    def chunk(dz):
        return pl.ds(pl.multiple_of(mine + dz * cap, cap), cap)

    def sum_copy(s, i):
        src = (
            part.at[s, :, chunk(y_op), lows],
            part.at[s, :, chunk(y_op), highs],
            part.at[s, :, chunk(y_up), highs],
            part.at[s, :, chunk(y_dn), lows],
            rsum.at[s, 6],
            rsum.at[s, 7],
        )[i]
        return remote(
            src, rsum.at[s, i], ssem.at[0, s, i], ssem.at[1, s, i], "tp", (up, dn)[i % 2]
        )

    def grads_at(s, core, dz):
        return gall.at[s, pl.ds(pl.multiple_of(core * half + dz * cap, cap), cap)]

    froms = (y_dn, y_up, y_op)

    def grad_copy(s, i, dz):
        at = gall.at[s, chunk(dz)]
        if i >= 2:
            at = gall.at[s, chunk(dz), pl.ds((i - 2) * hidden, hidden)]
        return remote(at, at, gsem.at[0, s, i], gsem.at[1, s, i], "tp", (up, dn)[i % 2])

    def fwd_copy(s, i, core, dz):
        at = grads_at(s, core, dz)
        return remote(at, at, fsem.at[0, s, i], fsem.at[1, s, i], "tp", sib)

    def landed(s, part_at, lo, count):
        remote(
            send.at[pl.ds(0, count)],
            inbuf.at[s, pl.ds(lo, count)],
            isem.at[2 * stages],
            isem.at[2 * s + part_at],
            "ctx",
            ahead(0, 1),
        ).wait_recv()

    def first(s):
        landed(s, 0, 0, nx)

        @pl.when(jnp.logical_and(s != 1, s + 1 < stages))
        def _():
            lax.fori_loop((s + 1) * per, (s + 2) * per, post, 0)

        @pl.when(s < stages - 1)
        def _():
            landed(s, 1, nx, nx)

        @pl.when(s == stages - 1)
        def _():
            landed(s, 1, nx + 1, nx - 1)

        rows = inbuf[s].reshape(per * cap, 2 * cut + 128)
        lasts = rows[:, 2 * cut :]
        for p, w in enumerate((wg, wu, wd)):
            lo = 0 if p < 2 else cut
            got = mm(rows[:, lo : lo + cut], w[0:cut, :]) + mm(lasts, w[cut:full, :])
            part[s, p] = got.astype(bf16)
            pair_copy(s, p).start()

    def second(s):
        for p in range(3):
            pair_copy(s, p).wait_recv()
            at = pl.ds(mine, half)
            part[s, p, at] = (part[s, p, at].astype(f32) + precv[s, p].astype(f32)).astype(bf16)
        for i in range(4):
            sum_copy(s, i).start()

    def relay(s):
        for i, (dz, at) in enumerate(((y_up, lows), (y_dn, highs))):
            sum_copy(s, i).wait_recv()
            rsum[s, 6 + i] = (
                part[s, :, chunk(dz), at].astype(f32) + rsum[s, i].astype(f32)
            ).astype(bf16)
            sum_copy(s, 4 + i).start()

    def third(s):
        for i in range(2, 6):
            sum_copy(s, i).wait_recv()
        for e, at, near, far in ((0, lows, 3, 4), (1, highs, 2, 5)):
            total = (
                part[s, :, chunk(y), at].astype(f32)
                + rsum[s, near].astype(f32)
                + rsum[s, far].astype(f32)
            )
            gate, upv, back = total[0], total[1], total[2]
            sigma = 1.0 / (1.0 + jnp.exp(-gate))
            lo, hi = pl.ds(e * side, side), pl.ds(hidden + e * side, side)
            gall[s, chunk(y), lo] = (back * upv * sigma * (1.0 + gate * (1.0 - sigma))).astype(bf16)
            gall[s, chunk(y), hi] = (back * gate * sigma).astype(bf16)
        for i in range(2):
            grad_copy(s, i, y).start()
        fwd_copy(s, 3, k, y).start()

    def fourth(s):
        for i in range(2):
            grad_copy(s, i, froms[i]).wait_recv()
            grad_copy(s, 2 + i, froms[i]).start()
            fwd_copy(s, i, k, froms[i]).start()

    def gathered(s):
        for i in range(2):
            grad_copy(s, 2 + i, y_op).wait_recv()
        fwd_copy(s, 2, k, y_op).start()

    def fifth(s):
        for i in range(3):
            fwd_copy(s, i, 1 - k, froms[i]).wait_recv()
        fwd_copy(s, 3, 1 - k, y).wait_recv()
        grad = mm(gall[s, :, 0:hidden], wg[0:cols, :], 1, 1) + mm(
            gall[s, :, hidden : 2 * hidden], wu[0:cols, :], 1, 1
        )
        eg[s] = grad.astype(bf16).reshape(per, cap, cols)

        def one(i, _):
            @pl.when(s * per + i != own[0] * per + own[1])
            def _():
                back_copy(s, i).start()

            return 0

        lax.fori_loop(0, per, one, 0)

    def back_copy(s, i):
        return remote(eg.at[s, i], ret.at[me], rsem.at[0], rsem.at[1], "ctx", origin(s, i))

    def stage(s, _):
        second(s)

        @pl.when(s > 0)
        def _():
            fourth(s - 1)

        @pl.when(s > 1)
        def _():
            fifth(s - 2)

        relay(s)

        @pl.when(s == 0)
        def _():
            lax.fori_loop(2 * per, 3 * per, post, 0)

        @pl.when(s > 0)
        def _():
            gathered(s - 1)

        @pl.when(s + 1 < stages)
        def _():
            first(s + 1)

        @pl.when(s == stages - 2)
        def _():
            w_hop(0, 0)

        @pl.when(s == stages - 1)
        def _():
            fifth(s - 1)
            w_hop(0, 1)

        third(s)
        return 0

    own_w.wait()
    first(0)
    lax.fori_loop(0, stages, stage, 0)
    fourth(stages - 1)
    gathered(stages - 1)
    fifth(stages - 1)
    w_hop(0, 2)
    w_hop(1, 0)
    ret[me] = eg[own]

    others = pl.ds(0, n - 1)
    returned = remote(
        ret.at[others], ret.at[others], rsem.at[0], rsem.at[1], "ctx", ahead(0, 1)
    )
    returned.wait_recv()
    entries = ret[...].reshape(slots, cols)
    input_grad = g_ref[...].astype(f32) + mm(entries, pick[...], 0, 0)
    ya[y] = input_grad.reshape(nz // 2, cols // (nz // 2), tok).astype(bf16)

    def y_copy(i, dz):
        at = ya.at[dz]
        if i >= 2:
            at = ya.at[dz, pl.ds((i - 2) * (nz // 4), nz // 4)]
        return remote(at, at, ysem.at[0, i], ysem.at[1, i], "tp", (up, dn)[i % 2])

    def x_copy(place, source):
        return remote(
            ya.at[place],
            xa.at[source, k],
            xsem.at[0, place],
            xsem.at[1, source],
            "ctx",
            place * nz + z,
        )

    def f_copy(source, core):
        at = xa.at[source, core]
        return remote(at, at, hfsem.at[0, source], hfsem.at[1, source], "tp", sib)

    def pass_on(place):
        @pl.when(place != x)
        def _():
            x_copy(place, x).start()

        @pl.when(place == x)
        def _():
            xa[x, k] = ya[place]
            f_copy(x, k).start()

    for i in range(2):
        y_copy(i, y).start()
    pass_on(y)
    out_ref[...] = input_grad.astype(bf16)
    for i in range(2):
        y_copy(i, froms[i]).wait_recv()
        y_copy(2 + i, froms[i]).start()
        pass_on(froms[i])
    w_hop(0, 3)
    w_hop(1, 1)
    for i in range(2):
        y_copy(2 + i, y_op).wait_recv()
    pass_on(y_op)

    def x_at(d):
        return lax.rem(x + d, nx)

    wide = width // 2
    quarter = wide // 2

    def product(source, hf):
        total = jnp.zeros((tok, wide), f32)
        for b in range(nz):
            part_x = xa[source, b // (nz // 2), b % (nz // 2)]
            total = total + mm(part_x, w[b, :, pl.ds(hf * wide, wide)], 0, 0)
        return total

    x_up, x_dn, x_op = x_at(1), x_at(nx - 1), x_at(2)
    def quart(hf, q):
        return pl.ds(hf * wide + q * quarter, quarter)

    def h_copy(hf, i):
        src, q = ((0, 0), (0, 1), (1, 1), (2, 0), (1, 0), (2, 1))[i]
        return remote(
            hsend.at[src, :, quart(hf, q)],
            hrecv.at[hf, i],
            hsem.at[0, hf, i],
            hsem.at[1, hf, i],
            "ctx",
            (x_up, x_dn)[i % 2] * nz + z,
        )

    order = [2, 1, nx - 1]
    w_hop(1, 2)
    for d in order:
        source = x_at(d)
        x_copy(x, source).wait_recv()
        f_copy(source, k).start()
    size = width // heads

    def h_send(hf):
        w_landed(hf, 3)
        for i, d in enumerate(order):
            source = x_at(d)
            if hf == 0:
                f_copy(source, 1 - k).wait_recv()
            hsend[i, :, pl.ds(hf * wide, wide)] = product(source, hf).astype(bf16)
            if i == 0:
                h_copy(hf, 0).start()
                h_copy(hf, 1).start()
            else:
                h_copy(hf, 1 + i).start()

    def h_relay(hf):
        for i in range(2):
            h_copy(hf, i).wait_recv()
            at = quart(hf, i)
            hsend[1 + i, :, at] = (
                hsend[1 + i, :, at].astype(f32) + hrecv[hf, i].astype(f32)
            ).astype(bf16)
            h_copy(hf, 4 + i).start()

    h_send(0)
    w_hop(1, 3)
    exchange(n, me, st_send, st_recv, sem_s, "start")
    st_recv[me] = st_send[me]
    h_relay(0)
    f_copy(x, 1 - k).wait_recv()
    wholes = [product(x, 0)]
    h_send(1)

    weights = jnp.zeros((tok, tok), f32)
    some = heads // 2
    weighted = []
    for hf in range(2):
        for i in range(2, 6):
            h_copy(hf, i).wait_recv()
        grad = (
            wholes[hf]
            + jnp.concatenate(
                [
                    hrecv[hf, 4].astype(f32) + hrecv[hf, 3].astype(f32),
                    hrecv[hf, 2].astype(f32) + hrecv[hf, 5].astype(f32),
                ],
                axis=1,
            )
        ).astype(bf16)
        ge = (grad.astype(f32) * er_ref[:, hf * wide : (hf + 1) * wide]).astype(bf16)
        weighted.append(ge)
        gst_send[hf] = mm(ge, c_ref[...], 0, 0).astype(bf16).reshape(gst_send.shape[1:])
        exchange(n, me, gst_send.at[hf], gst_recv.at[hf], gsem_s.at[hf], "start")
        gst_recv[hf, me] = gst_send[hf, me]
        if hf == 0:
            h_relay(1)
            wholes.append(product(x, 1))
        for j in range(some):
            h = hf * some + j
            gh = grad[:, j * size : (j + 1) * size]
            uh = u_ref[:, h * size : (h + 1) * size]
            weights = weights + decay_ref[h].astype(f32) * mm(gh, uh, 1, 1)
            intra[:, h * size : (h + 1) * size] = mm(mix_ref[h], gh, 0, 0)
    exchange(n, me, tot_send, tot_ref, sem_t, "wait")
    exchange(n, me, st_send, st_recv, sem_s, "wait")
    scan_states(n, me, st_recv, back_send, tot_ref, size, 0, False)
    exchange(n, me, back_send, before_ref, sem_b, "start")
    before_ref[me] = back_send[me]

    weights = weights.astype(bf16)
    state = b_ref.shape[1]

    for hf in range(2):
        exchange(n, me, gst_send.at[hf], gst_recv.at[hf], gsem_s.at[hf], "wait")
        scan_states(
            n, me, gst_recv.at[hf], gback_send.at[hf], tot_ref, size, hf * some, True
        )
        exchange(n, me, gback_send.at[hf], after.at[hf], gsem_b.at[hf], "start")
        after[hf, me] = gback_send[hf, me]

    exchange(n, me, back_send, before_ref, sem_b, "wait")
    before = before_ref[...].reshape(-1, state)
    out_map_ref[...] = (
        mm(weights, b_ref[...])
        + mm(weighted[0], before[0 : some * size])
        + mm(weighted[1], before[some * size :])
    )
    in_part = mm(weights, c_ref[...], 0, 0)

    def settle(s, _):
        for p in range(3):
            pair_copy(s, p).wait_send()
        for i in range(6):
            sum_copy(s, i).wait_send()
        for i in range(4):
            grad_copy(s, i, y).wait_send()
        for i in range(3):
            fwd_copy(s, i, k, froms[i]).wait_send()
        fwd_copy(s, 3, k, y).wait_send()
        return 0

    lax.fori_loop(0, stages, settle, 0)

    remote(
        send.at[others],
        send.at[others],
        isem.at[2 * stages],
        isem.at[0],
        "ctx",
        ahead(0, 1),
    ).wait_send()
    returned.wait_send()
    for hf in range(2):
        for j in range(nz // 2):
            w_copy(hf, j, True).wait_send()
            w_copy(hf, j, False).wait_send()
    for i in range(4):
        y_copy(i, y).wait_send()
    for d in order:
        x_copy(x_at(d), x).wait_send()
    for hf in range(2):
        for i in range(6):
            h_copy(hf, i).wait_send()
    for d in range(nx):
        f_copy(x_at(d), k).wait_send()

    for hf in range(2):
        exchange(n, me, gback_send.at[hf], after.at[hf], gsem_b.at[hf], "wait")
        later = after[hf].reshape(-1, state)
        at = pl.ds(hf * wide, wide)
        in_part = in_part + mm(ut_ref[:, at], later)
        scan_ref[:, at] = (
            intra[:, at] + tail_ref[:, at] * mm(b_ref[...], later, 1, 1)
        ).astype(bf16)
    in_ref[...] = in_part


def layer(
    sizes, moe_t, grad_t, ids_t, prob_t, counts, ssd_input, in_map, out_map, log_t, wg, wu, wd, w
):
    nx, nz, ny = sizes
    n = nx * nz
    cols, tok = moe_t.shape
    experts = counts.shape[1]
    cap = 2 * tok * ids_t.shape[0] // experts
    heads = log_t.shape[0]
    width = ssd_input.shape[1]
    state = in_map.shape[1]
    hidden = wg.shape[1]
    part = width // n
    cut = cols // 128 * 128
    full = cut + 128
    per, stages = 2 * nx, nz // 2
    rows = per * cap
    small = jax.ShapeDtypeStruct((tok, state), f32)
    halves = pltpu.VMEM((2, n, part // 2, state), bf16)
    states = pltpu.VMEM((n, part, state), bf16)
    pair = DMA((2,))
    return pl.pallas_call(
        functools.partial(layer_kernel, nx, nz, ny),
        out_shape=(
            jax.ShapeDtypeStruct((cols, tok), bf16),
            jax.ShapeDtypeStruct((tok, width), bf16),
            small,
            small,
        ),
        in_specs=[HBM] * 13,
        out_specs=[VMEM] * 4,
        scratch_shapes=[
            pltpu.VMEM((cols, tok), bf16),
            pltpu.VMEM((cols, tok), bf16),
            pltpu.VMEM(ids_t.shape, i32),
            pltpu.VMEM(prob_t.shape, f32),
            pltpu.VMEM(counts.shape, i32),
            pltpu.VMEM((tok, width), bf16),
            pltpu.VMEM((tok, state), bf16),
            pltpu.VMEM((tok, state), bf16),
            pltpu.VMEM(log_t.shape, f32),
            pltpu.VMEM((tok, width), f32),
            pltpu.VMEM((tok, width), f32),
            pltpu.VMEM((tok, width), bf16),
            pltpu.VMEM((heads, tok, tok), bf16),
            pltpu.VMEM((heads, tok, tok), bf16),
            states,
            pltpu.VMEM((n, 1, 128), f32),
            pltpu.VMEM((full, hidden), bf16),
            pltpu.VMEM((full, hidden), bf16),
            pltpu.VMEM((full, hidden), bf16),
            pltpu.VMEM((n, cap, 2 * cut + 128), bf16),
            pltpu.VMEM((stages, per, cap, 2 * cut + 128), bf16),
            pltpu.VMEM((stages, 3, rows, hidden), bf16),
            pltpu.VMEM((stages, 3, rows // 2, hidden), bf16),
            pltpu.VMEM((stages, 8, 3, cap, hidden // 2), bf16),
            pltpu.VMEM((stages, rows, 2 * hidden), bf16),
            pltpu.VMEM((stages, per, cap, cols), bf16),
            pltpu.VMEM((n, cap, cols), bf16),
            pltpu.VMEM((experts * cap, tok), bf16),
            states,
            states,
            states,
            pltpu.VMEM((n, 1, 128), f32),
            pltpu.VMEM((nz, w.shape[0], width), bf16),
            pltpu.VMEM((ny, nz // 2, w.shape[0], tok), bf16),
            pltpu.VMEM((nx, 2, nz // 2, w.shape[0], tok), bf16),
            pltpu.VMEM((3, tok, width), bf16),
            pltpu.VMEM((2, 6, tok, width // 4), bf16),
            pltpu.VMEM((tok, width), f32),
            halves,
            halves,
            halves,
            halves,
            DMA((5,)),
            DMA((2 * stages + 1,)),
            DMA((2, stages, 3)),
            DMA((2, stages, 6)),
            DMA((2, stages, 4)),
            DMA((2, stages, 4)),
            pair,
            pair,
            pair,
            pair,
            DMA((2, 2, nz // 2)),
            DMA((2, 2, nz // 2)),
            DMA((2, 4)),
            DMA((2, nx)),
            DMA((2, nx)),
            DMA((2, 2, 6)),
            DMA((2, 2)),
            DMA((2, 2)),
            DMA((9,)),
        ],
        compiler_params=pltpu.CompilerParams(
            collective_id=0, has_side_effects=True, vmem_limit_bytes=56 * 2**20
        ),
        name="layer",
    )(moe_t, grad_t, ids_t, prob_t, counts, ssd_input, in_map, out_map, log_t, wg, wu, wd, w)


def keep_kernel(*refs):
    count = (len(refs) - 1) // 3
    given, kept, held, sems = refs[:count], refs[count : 2 * count], refs[2 * count : -1], refs[-1]
    loads = [pltpu.make_async_copy(a, b, sems.at[0, i]) for i, (a, b) in enumerate(zip(given, held))]
    stores = [pltpu.make_async_copy(a, b, sems.at[1, i]) for i, (a, b) in enumerate(zip(held, kept))]
    for load in loads:
        load.start()
    for load, store in zip(loads, stores):
        load.wait()
        store.start()
    for store in stores:
        store.wait()


def keep(arrays):
    return pl.pallas_call(
        keep_kernel,
        out_shape=tuple(jax.ShapeDtypeStruct(a.shape, a.dtype) for a in arrays),
        in_specs=[HBM] * len(arrays),
        out_specs=[HBM] * len(arrays),
        scratch_shapes=[pltpu.VMEM(a.shape, a.dtype) for a in arrays] + [DMA((2, len(arrays)))],
        compiler_params=pltpu.CompilerParams(vmem_limit_bytes=60 * 2**20),
        name="keep",
    )(*arrays)


def body(
    moe_input,
    out_grad,
    route_prob,
    route_ids,
    route_counts,
    w_gate,
    w_up,
    w_down,
    out_weight,
    ssd_input,
    input_map,
    output_map,
    log_decay,
):
    n = lax.axis_size("ctx")
    ny = lax.axis_size("tp") // 2
    nx = ny
    nz = n // nx
    outs = layer(
        (nx, nz, ny),
        moe_input.T,
        out_grad.T,
        route_ids.T,
        route_prob.T,
        route_counts,
        ssd_input,
        input_map,
        output_map,
        log_decay.T,
        w_gate[0],
        w_up[0],
        w_down[0].T,
        out_weight,
    )
    grad_t, scan_grad, in_map_grad, out_map_grad = keep(outs)
    return (grad_t.T, scan_grad, in_map_grad, out_map_grad)


def solution(mesh):
    in_specs = (
        P("ctx", "tp"),
        P("ctx", "tp"),
        P("ctx", None),
        P("ctx", None),
        P("ctx", None),
        P("ctx", "tp", None),
        P("ctx", "tp", None),
        P("ctx", None, "tp"),
        P("ctx", "tp"),
        P("ctx", "tp"),
        P("ctx", "tp"),
        P("ctx", "tp"),
        P("ctx", "tp"),
    )
    out_specs = (P("ctx", "tp"), P("ctx", "tp"), P("ctx", "tp"), P("ctx", "tp"))
    return jax.shard_map(body, mesh=mesh, in_specs=in_specs, out_specs=out_specs, check_vma=False)
```

```python
import functools

import jax
import jax.numpy as jnp
from jax import lax
from jax.experimental import pallas as pl
from jax.experimental.pallas import tpu as pltpu
from jax.sharding import PartitionSpec as P

MESH = pl.DeviceIdType.MESH
HIGHEST = lax.Precision.HIGHEST
bf16, f32, i32 = jnp.bfloat16, jnp.float32, jnp.int32
VMEM = pl.BlockSpec(memory_space=pltpu.VMEM)
HBM = pl.BlockSpec(memory_space=pltpu.HBM)
DMA = pltpu.SemaphoreType.DMA


def mm(a, b, ca=1, cb=0, precision=None):
    return lax.dot_general(
        a, b, (((ca,), (cb,)), ((), ())), precision=precision, preferred_element_type=f32
    )


def remote(src, dst, send, recv, axis, place):
    return pltpu.make_async_remote_copy(
        src_ref=src,
        dst_ref=dst,
        send_sem=send,
        recv_sem=recv,
        device_id={axis: place},
        device_id_type=MESH,
    )


def hello_ctx(n, me):
    barrier = pltpu.get_barrier_semaphore()

    def one(i, _):
        pl.semaphore_signal(
            barrier, inc=1, device_id={"ctx": lax.rem(me + i, n)}, device_id_type=MESH
        )
        return 0

    lax.fori_loop(1, n, one, 0)


def hello_tp(places):
    barrier = pltpu.get_barrier_semaphore()
    for place in places:
        pl.semaphore_signal(barrier, inc=1, device_id={"tp": place}, device_id_type=MESH)


def exchange(n, me, src, dst, sems, act):
    if act == "wait":
        copy = remote(
            src.at[pl.ds(0, n - 1)],
            dst.at[pl.ds(0, n - 1)],
            sems.at[0],
            sems.at[1],
            "ctx",
            lax.rem(me + 1, n),
        )
        copy.wait_recv()
        copy.wait_send()
        return

    def one(i, _):
        to = lax.rem(me + i, n)
        remote(src.at[to], dst.at[me], sems.at[0], sems.at[1], "ctx", to).start()
        return 0

    lax.fori_loop(1, n, one, 0)


def spread(columns, total):
    heads = columns.shape[1]
    size = total // heads
    put = lax.broadcasted_iota(i32, (heads, total), 1) // size == lax.broadcasted_iota(
        i32, (heads, total), 0
    )
    return mm(columns, put.astype(f32), precision=HIGHEST)


def scan_states(n, me, loc, out, totals, rows_per_head, first_head, backward):
    head = first_head + me * loc.shape[1] // rows_per_head
    lane = lax.broadcasted_iota(i32, totals.shape, 2)
    decay = jnp.exp(jnp.sum(jnp.where(lane == head, totals[...], 0.0), axis=2, keepdims=True))
    state = jnp.zeros(loc.shape[1:], f32)
    order = range(n - 1, -1, -1) if backward else range(n)
    for c in order:
        out[c] = state.astype(bf16)
        state = decay[c, 0:1, :] * state + loc[c].astype(f32)


def layer_kernel(
    nx,
    nz,
    ny,
    x_hbm,
    g_hbm,
    ids_hbm,
    prob_hbm,
    counts_hbm,
    u_hbm,
    b_hbm,
    c_hbm,
    ld_hbm,
    wg_hbm,
    wu_hbm,
    wd_hbm,
    w_hbm,
    out_ref,
    scan_ref,
    in_ref,
    out_map_ref,
    x_ref,
    g_ref,
    ids_ref,
    prob_ref,
    counts_ref,
    u_ref,
    b_ref,
    c_ref,
    ld_ref,
    er_ref,
    tail_ref,
    ut_ref,
    decay_ref,
    mix_ref,
    before_ref,
    tot_ref,
    wg,
    wu,
    wd,
    send,
    inbuf,
    part,
    precv,
    rsum,
    gall,
    eg,
    ret,
    pick,
    st_send,
    st_recv,
    back_send,
    tot_send,
    w,
    ya,
    xa,
    hsend,
    hrecv,
    intra,
    gst_send,
    gst_recv,
    gback_send,
    after,
    wsem,
    isem,
    psem,
    ssem,
    gsem,
    fsem,
    rsem,
    sem_s,
    sem_t,
    sem_b,
    usem,
    dsem,
    ysem,
    xsem,
    hfsem,
    hsem,
    gsem_s,
    gsem_b,
    lsem,
):
    n = nx * nz
    me = lax.axis_index("ctx")
    x, z = me // nz, lax.rem(me, nz)
    t = lax.axis_index("tp")
    y, k = t // 2, lax.rem(t, 2)
    sib = y * 2 + (1 - k)
    y_up, y_dn, y_op = lax.rem(y + 1, ny), lax.rem(y + ny - 1, ny), lax.rem(y + 2, ny)
    up, dn = y_up * 2 + k, y_dn * 2 + k

    def ahead(dx, dz):
        return lax.rem(x + dx, nx) * nz + lax.rem(z + dz, nz)

    def behind(dx, dz):
        return lax.rem(x - dx + nx, nx) * nz + lax.rem(z - dz + nz, nz)

    def offset(s, i):
        j = i // nx
        dz = jnp.where(j == 0, s + 1, jnp.where(s == nz // 2 - 1, 0, nz - 1 - s))
        return lax.rem(i, nx), dz

    def target(s, i):
        return ahead(*offset(s, i))

    def origin(s, i):
        return behind(*offset(s, i))

    per = 2 * nx
    stages = nz // 2
    own = (stages - 1, nx)

    cols, tok = x_hbm.shape
    hidden = wg.shape[1]
    cut = wd_hbm.shape[0] // 128 * 128
    loads = [
        pltpu.make_async_copy(wg_hbm, wg.at[pl.ds(0, cols)], wsem.at[0]),
        pltpu.make_async_copy(wu_hbm, wu.at[pl.ds(0, cols)], wsem.at[1]),
        pltpu.make_async_copy(wd_hbm.at[pl.ds(0, cut)], wd.at[pl.ds(0, cut)], wsem.at[2]),
        pltpu.make_async_copy(
            wd_hbm.at[pl.ds(cut, cols - cut)], wd.at[pl.ds(cols, cols - cut)], wsem.at[3]
        ),
    ]
    small = [
        pltpu.make_async_copy(src, dst, lsem.at[i])
        for i, (src, dst) in enumerate(
            (
                (ids_hbm, ids_ref),
                (counts_hbm, counts_ref),
                (x_hbm, x_ref),
                (g_hbm, g_ref),
                (prob_hbm, prob_ref),
                (ld_hbm, ld_ref),
                (u_hbm, u_ref),
                (b_hbm, b_ref),
                (c_hbm, c_ref),
            )
        )
    ]
    for load in small:
        load.start()
    own_w = pltpu.make_async_copy(w_hbm, w.at[z], wsem.at[4])
    own_w.start()
    for load in loads:
        load.start()
    hello_ctx(n, me)
    hello_tp((sib, up, dn))
    for load in small[0:2]:
        load.wait()

    experts = counts_ref.shape[1]
    cap = inbuf.shape[2]
    slots = experts * cap
    rest = cols - cut
    full = cut + 128
    ids = ids_ref[...]
    names = lax.broadcasted_iota(i32, (experts, tok), 0)
    m0 = ids[0:1, :] == names
    m1 = ids[1:2, :] == names
    member = jnp.where(m0, 1.0, 0.0) + jnp.where(m1, 1.0, 0.0)
    t_row = lax.broadcasted_iota(i32, (tok, tok), 0)
    t_col = lax.broadcasted_iota(i32, (tok, tok), 1)
    rank = mm(member.astype(bf16), jnp.where(t_row < t_col, 1.0, 0.0).astype(bf16))
    e_row = lax.broadcasted_iota(i32, (experts, experts), 0)
    e_col = lax.broadcasted_iota(i32, (experts, experts), 1)
    limit = jnp.sum(
        jnp.where(e_row == e_col, counts_ref[...].astype(f32), 0.0), axis=1, keepdims=True
    )
    slot = jnp.where(rank < limit, rank + (names * cap).astype(f32), -1.0)
    place = lax.broadcasted_iota(i32, (slots, tok), 0).astype(f32)
    p0 = jnp.where(place == jnp.sum(jnp.where(m0, slot, 0.0), 0, keepdims=True), 1.0, 0.0)
    p1 = jnp.where(place == jnp.sum(jnp.where(m1, slot, 0.0), 0, keepdims=True), 1.0, 0.0)
    both = (p0 + p1).astype(bf16)
    pick[...] = both

    pl.semaphore_wait(pltpu.get_barrier_semaphore(), n - 1 + 3)
    mid = w.shape[2] // 2
    last_hop = nz // 2 - 1

    def w_part(hf, j, block, upward):
        if j < last_hop:
            return w.at[block, :, pl.ds(hf * mid, mid)]
        return w.at[block, :, pl.ds(hf * mid + (0 if upward else mid // 2), mid // 2)]

    def w_copy(hf, j, upward):
        if upward:
            block, to, sem = lax.rem(z - j + nz, nz), ahead(0, 1), usem
        else:
            block, to, sem = lax.rem(z + j, nz), behind(0, 1), dsem
        at = w_part(hf, j, block, upward)
        return remote(at, at, sem.at[0, hf, j], sem.at[1, hf, j], "ctx", to)

    def w_landed(hf, j):
        for upward, sem in ((True, usem), (False, dsem)):
            block = lax.rem(z - j - 1 + nz, nz) if upward else lax.rem(z + j + 1, nz)
            at = w_part(hf, j, block, upward)
            remote(at, at, sem.at[0, hf, j], sem.at[1, hf, j], "ctx", ahead(0, 1)).wait_recv()

    def w_hop(hf, j):
        if j:
            w_landed(hf, j - 1)
        w_copy(hf, j, True).start()
        w_copy(hf, j, False).start()

    for load in small[2:]:
        load.wait()
    grad = g_ref[...].astype(f32)
    prob = prob_ref[...]
    scaled = jnp.concatenate(
        [(prob[0:1, :] * grad).astype(bf16), (prob[1:2, :] * grad).astype(bf16)], axis=1
    )
    pair = jnp.concatenate([p0.astype(bf16), p1.astype(bf16)], axis=1)
    sel_x = mm(both, x_ref[...], 1, 1)
    sel_g = mm(pair, scaled, 1, 1)
    send[:, :, 0:cut] = sel_x[:, 0:cut].astype(bf16).reshape(experts, cap, cut)
    send[:, :, cut : 2 * cut] = sel_g[:, 0:cut].astype(bf16).reshape(experts, cap, cut)
    last = jnp.concatenate(
        [sel_x[:, cut:], sel_g[:, cut:], jnp.zeros((slots, 128 - 2 * rest), f32)], axis=1
    )
    send[:, :, 2 * cut :] = last.astype(bf16).reshape(experts, cap, 128)

    def in_copy(s, j):
        to = target(s, j)
        at = 2 * s + j // (per // 2)
        return remote(send.at[to], inbuf.at[s, j], isem.at[2 * stages], isem.at[at], "ctx", to)

    def post(i, _):
        s, j = i // per, lax.rem(i, per)

        @pl.when(i != own[0] * per + own[1])
        def _():
            in_copy(s, j).start()

        return 0

    lax.fori_loop(0, per, post, 0)
    inbuf[own] = send[me]

    heads = ld_ref.shape[0]
    width = u_ref.shape[1]
    log = ld_ref[...]
    upto = jnp.where(t_row >= t_col, 1.0, 0.0)
    run = mm(upto, log, 1, 1, precision=HIGHEST)
    run_t = mm(log, upto, 1, 1, precision=HIGHEST)
    total = run[tok - 1 : tok, :]
    tail_x = spread(jnp.exp(total - run), width)
    tail_ref[...] = tail_x
    ut = (u_ref[...].astype(f32) * tail_x).astype(bf16)
    ut_ref[...] = ut
    st_send[...] = mm(ut, b_ref[...], 0, 0).astype(bf16).reshape(st_send.shape)
    tot_send[...] = jnp.broadcast_to(
        jnp.concatenate([total, jnp.zeros((1, tot_send.shape[2] - heads), f32)], axis=1)[None],
        tot_send.shape,
    )
    exchange(n, me, tot_send, tot_ref, sem_t, "start")
    tot_ref[me] = tot_send[me]

    wg[pl.ds(cols, 128 - rest), :] = jnp.zeros((128 - rest, hidden), bf16)
    wu[pl.ds(cols, 128 - rest), :] = jnp.zeros((128 - rest, hidden), bf16)
    wd[pl.ds(cut, rest), :] = jnp.zeros((rest, hidden), bf16)
    wd[pl.ds(cols + rest, 128 - 2 * rest), :] = jnp.zeros((128 - 2 * rest, hidden), bf16)
    for load in loads:
        load.wait()

    er_ref[...] = spread(jnp.exp(run), width)
    affinity = mm(c_ref[...], b_ref[...], 1, 1)
    for h in range(heads):
        gap = run[:, h : h + 1] - run_t[h : h + 1, :]
        decay = jnp.where(t_row >= t_col, jnp.exp(jnp.where(t_row >= t_col, gap, 0.0)), 0.0)
        decay_ref[h] = decay.astype(bf16)
        mix_ref[h] = (decay * affinity).astype(bf16)

    half = per // 2 * cap
    mine, other = pl.multiple_of(k * half, cap), pl.multiple_of((1 - k) * half, cap)

    def pair_copy(s, p):
        return remote(
            part.at[s, p, pl.ds(other, half)],
            precv.at[s, p],
            psem.at[0, s, p],
            psem.at[1, s, p],
            "tp",
            sib,
        )

    side = hidden // 2
    lows, highs = pl.ds(0, side), pl.ds(side, side)

    def chunk(dz):
        return pl.ds(pl.multiple_of(mine + dz * cap, cap), cap)

    def sum_copy(s, i):
        src = (
            part.at[s, :, chunk(y_op), lows],
            part.at[s, :, chunk(y_op), highs],
            part.at[s, :, chunk(y_up), highs],
            part.at[s, :, chunk(y_dn), lows],
            rsum.at[s, 6],
            rsum.at[s, 7],
        )[i]
        return remote(
            src, rsum.at[s, i], ssem.at[0, s, i], ssem.at[1, s, i], "tp", (up, dn)[i % 2]
        )

    def grads_at(s, core, dz):
        return gall.at[s, pl.ds(pl.multiple_of(core * half + dz * cap, cap), cap)]

    froms = (y_dn, y_up, y_op)

    def grad_copy(s, i, dz):
        at = gall.at[s, chunk(dz)]
        if i >= 2:
            at = gall.at[s, chunk(dz), pl.ds((i - 2) * hidden, hidden)]
        return remote(at, at, gsem.at[0, s, i], gsem.at[1, s, i], "tp", (up, dn)[i % 2])

    def fwd_copy(s, i, core, dz):
        at = grads_at(s, core, dz)
        return remote(at, at, fsem.at[0, s, i], fsem.at[1, s, i], "tp", sib)

    def landed(s, part_at, lo, count):
        remote(
            send.at[pl.ds(0, count)],
            inbuf.at[s, pl.ds(lo, count)],
            isem.at[2 * stages],
            isem.at[2 * s + part_at],
            "ctx",
            ahead(0, 1),
        ).wait_recv()

    def first(s):
        landed(s, 0, 0, nx)

        @pl.when(jnp.logical_and(s != 1, s + 1 < stages))
        def _():
            lax.fori_loop((s + 1) * per, (s + 2) * per, post, 0)

        @pl.when(s < stages - 1)
        def _():
            landed(s, 1, nx, nx)

        @pl.when(s == stages - 1)
        def _():
            landed(s, 1, nx + 1, nx - 1)

        rows = inbuf[s].reshape(per * cap, 2 * cut + 128)
        lasts = rows[:, 2 * cut :]
        for p, w in enumerate((wg, wu, wd)):
            lo = 0 if p < 2 else cut
            got = mm(rows[:, lo : lo + cut], w[0:cut, :]) + mm(lasts, w[cut:full, :])
            part[s, p] = got.astype(bf16)
            pair_copy(s, p).start()

    def second(s):
        for p in range(3):
            pair_copy(s, p).wait_recv()
            at = pl.ds(mine, half)
            part[s, p, at] = (part[s, p, at].astype(f32) + precv[s, p].astype(f32)).astype(bf16)
        for i in range(4):
            sum_copy(s, i).start()

    def relay(s):
        for i, (dz, at) in enumerate(((y_up, lows), (y_dn, highs))):
            sum_copy(s, i).wait_recv()
            rsum[s, 6 + i] = (
                part[s, :, chunk(dz), at].astype(f32) + rsum[s, i].astype(f32)
            ).astype(bf16)
            sum_copy(s, 4 + i).start()

    def third(s):
        for i in range(2, 6):
            sum_copy(s, i).wait_recv()
        for e, at, near, far in ((0, lows, 3, 4), (1, highs, 2, 5)):
            total = (
                part[s, :, chunk(y), at].astype(f32)
                + rsum[s, near].astype(f32)
                + rsum[s, far].astype(f32)
            )
            gate, upv, back = total[0], total[1], total[2]
            sigma = 1.0 / (1.0 + jnp.exp(-gate))
            lo, hi = pl.ds(e * side, side), pl.ds(hidden + e * side, side)
            gall[s, chunk(y), lo] = (back * upv * sigma * (1.0 + gate * (1.0 - sigma))).astype(bf16)
            gall[s, chunk(y), hi] = (back * gate * sigma).astype(bf16)
        for i in range(2):
            grad_copy(s, i, y).start()
        fwd_copy(s, 3, k, y).start()

    def fourth(s):
        for i in range(2):
            grad_copy(s, i, froms[i]).wait_recv()
            grad_copy(s, 2 + i, froms[i]).start()
            fwd_copy(s, i, k, froms[i]).start()

    def gathered(s):
        for i in range(2):
            grad_copy(s, 2 + i, y_op).wait_recv()
        fwd_copy(s, 2, k, y_op).start()

    def fifth(s):
        for i in range(3):
            fwd_copy(s, i, 1 - k, froms[i]).wait_recv()
        fwd_copy(s, 3, 1 - k, y).wait_recv()
        grad = mm(gall[s, :, 0:hidden], wg[0:cols, :], 1, 1) + mm(
            gall[s, :, hidden : 2 * hidden], wu[0:cols, :], 1, 1
        )
        eg[s] = grad.astype(bf16).reshape(per, cap, cols)

        def one(i, _):
            @pl.when(s * per + i != own[0] * per + own[1])
            def _():
                back_copy(s, i).start()

            return 0

        lax.fori_loop(0, per, one, 0)

    def back_copy(s, i):
        return remote(eg.at[s, i], ret.at[me], rsem.at[0], rsem.at[1], "ctx", origin(s, i))

    def stage(s, _):
        second(s)

        @pl.when(s > 0)
        def _():
            fourth(s - 1)

        @pl.when(s > 1)
        def _():
            fifth(s - 2)

        relay(s)

        @pl.when(s == 0)
        def _():
            lax.fori_loop(2 * per, 3 * per, post, 0)

        @pl.when(s > 0)
        def _():
            gathered(s - 1)

        @pl.when(s + 1 < stages)
        def _():
            first(s + 1)

        @pl.when(s == stages - 2)
        def _():
            w_hop(0, 0)

        @pl.when(s == stages - 1)
        def _():
            fifth(s - 1)
            w_hop(0, 1)

        third(s)
        return 0

    own_w.wait()
    first(0)
    lax.fori_loop(0, stages, stage, 0)
    fourth(stages - 1)
    gathered(stages - 1)
    fifth(stages - 1)
    w_hop(1, 0)
    w_hop(0, 2)
    ret[me] = eg[own]

    others = pl.ds(0, n - 1)
    returned = remote(
        ret.at[others], ret.at[others], rsem.at[0], rsem.at[1], "ctx", ahead(0, 1)
    )
    returned.wait_recv()
    entries = ret[...].reshape(slots, cols)
    input_grad = g_ref[...].astype(f32) + mm(entries, pick[...], 0, 0)
    ya[y] = input_grad.reshape(nz // 2, cols // (nz // 2), tok).astype(bf16)

    def y_copy(i, dz):
        first_half = (0, 1, 1, 0, 0, 1)[i]
        at = ya.at[dz, pl.ds(first_half * (nz // 4), nz // 4)]
        return remote(at, at, ysem.at[0, i], ysem.at[1, i], "tp", (up, dn)[i % 2])

    def x_copy(place, source):
        return remote(
            ya.at[place],
            xa.at[source, k],
            xsem.at[0, place],
            xsem.at[1, source],
            "ctx",
            place * nz + z,
        )

    def f_copy(source, core):
        at = xa.at[source, core]
        return remote(at, at, hfsem.at[0, source], hfsem.at[1, source], "tp", sib)

    def pass_on(place):
        @pl.when(place != x)
        def _():
            x_copy(place, x).start()

        @pl.when(place == x)
        def _():
            xa[x, k] = ya[place]
            f_copy(x, k).start()

    for i in range(4):
        y_copy(i, y).start()
    pass_on(y)
    out_ref[...] = input_grad.astype(bf16)
    for i in range(2):
        y_copy(i, froms[i]).wait_recv()
        y_copy(4 + i, froms[i]).start()
    w_hop(1, 1)
    for i in range(2):
        y_copy(2 + i, froms[i]).wait_recv()
        pass_on(froms[i])
    w_hop(0, 3)
    for i in range(2):
        y_copy(4 + i, y_op).wait_recv()
    pass_on(y_op)

    def x_at(d):
        return lax.rem(x + d, nx)

    wide = width // 2
    quarter = wide // 2

    def product(source, hf):
        total = jnp.zeros((tok, wide), f32)
        for b in range(nz):
            part_x = xa[source, b // (nz // 2), b % (nz // 2)]
            total = total + mm(part_x, w[b, :, pl.ds(hf * wide, wide)], 0, 0)
        return total

    x_up, x_dn, x_op = x_at(1), x_at(nx - 1), x_at(2)
    def quart(hf, q):
        return pl.ds(hf * wide + q * quarter, quarter)

    def h_copy(hf, i):
        src, q = ((0, 0), (0, 1), (1, 1), (2, 0), (1, 0), (2, 1))[i]
        return remote(
            hsend.at[src, :, quart(hf, q)],
            hrecv.at[hf, i],
            hsem.at[0, hf, i],
            hsem.at[1, hf, i],
            "ctx",
            (x_up, x_dn)[i % 2] * nz + z,
        )

    order = [2, 1, nx - 1]
    w_hop(1, 2)
    exchange(n, me, st_send, st_recv, sem_s, "start")
    st_recv[me] = st_send[me]
    for d in order:
        source = x_at(d)
        x_copy(x, source).wait_recv()
        f_copy(source, k).start()
    size = width // heads

    def h_send(hf):
        w_landed(hf, 3)
        for i, d in enumerate(order):
            source = x_at(d)
            if hf == 0:
                f_copy(source, 1 - k).wait_recv()
            hsend[i, :, pl.ds(hf * wide, wide)] = product(source, hf).astype(bf16)
            if i == 0:
                h_copy(hf, 0).start()
                h_copy(hf, 1).start()
            else:
                h_copy(hf, 1 + i).start()

    def h_relay(hf):
        for i in range(2):
            h_copy(hf, i).wait_recv()
            at = quart(hf, i)
            hsend[1 + i, :, at] = (
                hsend[1 + i, :, at].astype(f32) + hrecv[hf, i].astype(f32)
            ).astype(bf16)
            h_copy(hf, 4 + i).start()

    h_send(0)
    w_hop(1, 3)
    h_relay(0)
    f_copy(x, 1 - k).wait_recv()
    wholes = [product(x, 0)]
    exchange(n, me, tot_send, tot_ref, sem_t, "wait")
    exchange(n, me, st_send, st_recv, sem_s, "wait")
    scan_states(n, me, st_recv, back_send, tot_ref, size, 0, False)
    exchange(n, me, back_send, before_ref, sem_b, "start")
    before_ref[me] = back_send[me]
    h_send(1)

    weights = jnp.zeros((tok, tok), f32)
    some = heads // 2
    weighted = []
    for hf in range(2):
        for i in range(2, 6):
            h_copy(hf, i).wait_recv()
        grad = (
            wholes[hf]
            + jnp.concatenate(
                [
                    hrecv[hf, 4].astype(f32) + hrecv[hf, 3].astype(f32),
                    hrecv[hf, 2].astype(f32) + hrecv[hf, 5].astype(f32),
                ],
                axis=1,
            )
        ).astype(bf16)
        ge = (grad.astype(f32) * er_ref[:, hf * wide : (hf + 1) * wide]).astype(bf16)
        weighted.append(ge)
        gst_send[hf] = mm(ge, c_ref[...], 0, 0).astype(bf16).reshape(gst_send.shape[1:])
        exchange(n, me, gst_send.at[hf], gst_recv.at[hf], gsem_s.at[hf], "start")
        gst_recv[hf, me] = gst_send[hf, me]
        if hf == 0:
            h_relay(1)
            wholes.append(product(x, 1))
        for j in range(some):
            h = hf * some + j
            gh = grad[:, j * size : (j + 1) * size]
            uh = u_ref[:, h * size : (h + 1) * size]
            weights = weights + decay_ref[h].astype(f32) * mm(gh, uh, 1, 1)
            intra[:, h * size : (h + 1) * size] = mm(mix_ref[h], gh, 0, 0)
    weights = weights.astype(bf16)
    state = b_ref.shape[1]

    for hf in range(2):
        exchange(n, me, gst_send.at[hf], gst_recv.at[hf], gsem_s.at[hf], "wait")
        scan_states(
            n, me, gst_recv.at[hf], gback_send.at[hf], tot_ref, size, hf * some, True
        )
        exchange(n, me, gback_send.at[hf], after.at[hf], gsem_b.at[hf], "start")
        after[hf, me] = gback_send[hf, me]

    exchange(n, me, back_send, before_ref, sem_b, "wait")
    before = before_ref[...].reshape(-1, state)
    out_map_ref[...] = (
        mm(weights, b_ref[...])
        + mm(weighted[0], before[0 : some * size])
        + mm(weighted[1], before[some * size :])
    )
    in_part = mm(weights, c_ref[...], 0, 0)

    def settle(s, _):
        for p in range(3):
            pair_copy(s, p).wait_send()
        for i in range(6):
            sum_copy(s, i).wait_send()
        for i in range(4):
            grad_copy(s, i, y).wait_send()
        for i in range(3):
            fwd_copy(s, i, k, froms[i]).wait_send()
        fwd_copy(s, 3, k, y).wait_send()
        return 0

    lax.fori_loop(0, stages, settle, 0)

    remote(
        send.at[others],
        send.at[others],
        isem.at[2 * stages],
        isem.at[0],
        "ctx",
        ahead(0, 1),
    ).wait_send()
    returned.wait_send()
    for hf in range(2):
        for j in range(nz // 2):
            w_copy(hf, j, True).wait_send()
            w_copy(hf, j, False).wait_send()
    for i in range(6):
        y_copy(i, y).wait_send()
    for d in order:
        x_copy(x_at(d), x).wait_send()
    for hf in range(2):
        for i in range(6):
            h_copy(hf, i).wait_send()
    for d in range(nx):
        f_copy(x_at(d), k).wait_send()

    for hf in range(2):
        exchange(n, me, gback_send.at[hf], after.at[hf], gsem_b.at[hf], "wait")
        later = after[hf].reshape(-1, state)
        at = pl.ds(hf * wide, wide)
        in_part = in_part + mm(ut_ref[:, at], later)
        scan_ref[:, at] = (
            intra[:, at] + tail_ref[:, at] * mm(b_ref[...], later, 1, 1)
        ).astype(bf16)
    in_ref[...] = in_part


def layer(
    sizes, moe_t, grad_t, ids_t, prob_t, counts, ssd_input, in_map, out_map, log_t, wg, wu, wd, w
):
    nx, nz, ny = sizes
    n = nx * nz
    cols, tok = moe_t.shape
    experts = counts.shape[1]
    cap = 2 * tok * ids_t.shape[0] // experts
    heads = log_t.shape[0]
    width = ssd_input.shape[1]
    state = in_map.shape[1]
    hidden = wg.shape[1]
    part = width // n
    cut = cols // 128 * 128
    full = cut + 128
    per, stages = 2 * nx, nz // 2
    rows = per * cap
    small = jax.ShapeDtypeStruct((tok, state), f32)
    halves = pltpu.VMEM((2, n, part // 2, state), bf16)
    states = pltpu.VMEM((n, part, state), bf16)
    pair = DMA((2,))
    return pl.pallas_call(
        functools.partial(layer_kernel, nx, nz, ny),
        out_shape=(
            jax.ShapeDtypeStruct((cols, tok), bf16),
            jax.ShapeDtypeStruct((tok, width), bf16),
            small,
            small,
        ),
        in_specs=[HBM] * 13,
        out_specs=[VMEM] * 4,
        scratch_shapes=[
            pltpu.VMEM((cols, tok), bf16),
            pltpu.VMEM((cols, tok), bf16),
            pltpu.VMEM(ids_t.shape, i32),
            pltpu.VMEM(prob_t.shape, f32),
            pltpu.VMEM(counts.shape, i32),
            pltpu.VMEM((tok, width), bf16),
            pltpu.VMEM((tok, state), bf16),
            pltpu.VMEM((tok, state), bf16),
            pltpu.VMEM(log_t.shape, f32),
            pltpu.VMEM((tok, width), f32),
            pltpu.VMEM((tok, width), f32),
            pltpu.VMEM((tok, width), bf16),
            pltpu.VMEM((heads, tok, tok), bf16),
            pltpu.VMEM((heads, tok, tok), bf16),
            states,
            pltpu.VMEM((n, 1, 128), f32),
            pltpu.VMEM((full, hidden), bf16),
            pltpu.VMEM((full, hidden), bf16),
            pltpu.VMEM((full, hidden), bf16),
            pltpu.VMEM((n, cap, 2 * cut + 128), bf16),
            pltpu.VMEM((stages, per, cap, 2 * cut + 128), bf16),
            pltpu.VMEM((stages, 3, rows, hidden), bf16),
            pltpu.VMEM((stages, 3, rows // 2, hidden), bf16),
            pltpu.VMEM((stages, 8, 3, cap, hidden // 2), bf16),
            pltpu.VMEM((stages, rows, 2 * hidden), bf16),
            pltpu.VMEM((stages, per, cap, cols), bf16),
            pltpu.VMEM((n, cap, cols), bf16),
            pltpu.VMEM((experts * cap, tok), bf16),
            states,
            states,
            states,
            pltpu.VMEM((n, 1, 128), f32),
            pltpu.VMEM((nz, w.shape[0], width), bf16),
            pltpu.VMEM((ny, nz // 2, w.shape[0], tok), bf16),
            pltpu.VMEM((nx, 2, nz // 2, w.shape[0], tok), bf16),
            pltpu.VMEM((3, tok, width), bf16),
            pltpu.VMEM((2, 6, tok, width // 4), bf16),
            pltpu.VMEM((tok, width), f32),
            halves,
            halves,
            halves,
            halves,
            DMA((5,)),
            DMA((2 * stages + 1,)),
            DMA((2, stages, 3)),
            DMA((2, stages, 6)),
            DMA((2, stages, 4)),
            DMA((2, stages, 4)),
            pair,
            pair,
            pair,
            pair,
            DMA((2, 2, nz // 2)),
            DMA((2, 2, nz // 2)),
            DMA((2, 6)),
            DMA((2, nx)),
            DMA((2, nx)),
            DMA((2, 2, 6)),
            DMA((2, 2)),
            DMA((2, 2)),
            DMA((9,)),
        ],
        compiler_params=pltpu.CompilerParams(
            collective_id=0, has_side_effects=True, vmem_limit_bytes=56 * 2**20
        ),
        name="layer",
    )(moe_t, grad_t, ids_t, prob_t, counts, ssd_input, in_map, out_map, log_t, wg, wu, wd, w)


def keep_kernel(*refs):
    count = (len(refs) - 1) // 3
    given, kept, held, sems = refs[:count], refs[count : 2 * count], refs[2 * count : -1], refs[-1]
    loads = [pltpu.make_async_copy(a, b, sems.at[0, i]) for i, (a, b) in enumerate(zip(given, held))]
    stores = [pltpu.make_async_copy(a, b, sems.at[1, i]) for i, (a, b) in enumerate(zip(held, kept))]
    for load in loads:
        load.start()
    for load, store in zip(loads, stores):
        load.wait()
        store.start()
    for store in stores:
        store.wait()


def keep(arrays):
    return pl.pallas_call(
        keep_kernel,
        out_shape=tuple(jax.ShapeDtypeStruct(a.shape, a.dtype) for a in arrays),
        in_specs=[HBM] * len(arrays),
        out_specs=[HBM] * len(arrays),
        scratch_shapes=[pltpu.VMEM(a.shape, a.dtype) for a in arrays] + [DMA((2, len(arrays)))],
        compiler_params=pltpu.CompilerParams(vmem_limit_bytes=60 * 2**20),
        name="keep",
    )(*arrays)


def body(
    moe_input,
    out_grad,
    route_prob,
    route_ids,
    route_counts,
    w_gate,
    w_up,
    w_down,
    out_weight,
    ssd_input,
    input_map,
    output_map,
    log_decay,
):
    n = lax.axis_size("ctx")
    ny = lax.axis_size("tp") // 2
    nx = ny
    nz = n // nx
    outs = layer(
        (nx, nz, ny),
        moe_input.T,
        out_grad.T,
        route_ids.T,
        route_prob.T,
        route_counts,
        ssd_input,
        input_map,
        output_map,
        log_decay.T,
        w_gate[0],
        w_up[0],
        w_down[0].T,
        out_weight,
    )
    grad_t, scan_grad, in_map_grad, out_map_grad = keep(outs)
    return (grad_t.T, scan_grad, in_map_grad, out_map_grad)


def solution(mesh):
    in_specs = (
        P("ctx", "tp"),
        P("ctx", "tp"),
        P("ctx", None),
        P("ctx", None),
        P("ctx", None),
        P("ctx", "tp", None),
        P("ctx", "tp", None),
        P("ctx", None, "tp"),
        P("ctx", "tp"),
        P("ctx", "tp"),
        P("ctx", "tp"),
        P("ctx", "tp"),
        P("ctx", "tp"),
    )
    out_specs = (P("ctx", "tp"), P("ctx", "tp"), P("ctx", "tp"), P("ctx", "tp"))
    return jax.shard_map(body, mesh=mesh, in_specs=in_specs, out_specs=out_specs, check_vma=False)
```

```python
import functools

import jax
import jax.numpy as jnp
from jax import lax
from jax.experimental import pallas as pl
from jax.experimental.pallas import tpu as pltpu
from jax.sharding import PartitionSpec as P

MESH = pl.DeviceIdType.MESH
HIGHEST = lax.Precision.HIGHEST
bf16, f32, i32 = jnp.bfloat16, jnp.float32, jnp.int32
VMEM = pl.BlockSpec(memory_space=pltpu.VMEM)
HBM = pl.BlockSpec(memory_space=pltpu.HBM)
DMA = pltpu.SemaphoreType.DMA


def mm(a, b, ca=1, cb=0, precision=None):
    return lax.dot_general(
        a, b, (((ca,), (cb,)), ((), ())), precision=precision, preferred_element_type=f32
    )


def remote(src, dst, send, recv, axis, place):
    return pltpu.make_async_remote_copy(
        src_ref=src,
        dst_ref=dst,
        send_sem=send,
        recv_sem=recv,
        device_id={axis: place},
        device_id_type=MESH,
    )


def hello_ctx(n, me):
    barrier = pltpu.get_barrier_semaphore()

    def one(i, _):
        pl.semaphore_signal(
            barrier, inc=1, device_id={"ctx": lax.rem(me + i, n)}, device_id_type=MESH
        )
        return 0

    lax.fori_loop(1, n, one, 0)


def hello_tp(places):
    barrier = pltpu.get_barrier_semaphore()
    for place in places:
        pl.semaphore_signal(barrier, inc=1, device_id={"tp": place}, device_id_type=MESH)


def exchange(n, me, src, dst, sems, act):
    if act == "wait":
        copy = remote(
            src.at[pl.ds(0, n - 1)],
            dst.at[pl.ds(0, n - 1)],
            sems.at[0],
            sems.at[1],
            "ctx",
            lax.rem(me + 1, n),
        )
        copy.wait_recv()
        copy.wait_send()
        return

    def one(i, _):
        to = lax.rem(me + i, n)
        remote(src.at[to], dst.at[me], sems.at[0], sems.at[1], "ctx", to).start()
        return 0

    lax.fori_loop(1, n, one, 0)


def spread(columns, total):
    heads = columns.shape[1]
    size = total // heads
    put = lax.broadcasted_iota(i32, (heads, total), 1) // size == lax.broadcasted_iota(
        i32, (heads, total), 0
    )
    return mm(columns, put.astype(f32), precision=HIGHEST)


def scan_states(n, me, loc, out, totals, rows_per_head, first_head, backward):
    head = first_head + me * loc.shape[1] // rows_per_head
    lane = lax.broadcasted_iota(i32, totals.shape, 2)
    decay = jnp.exp(jnp.sum(jnp.where(lane == head, totals[...], 0.0), axis=2, keepdims=True))
    state = jnp.zeros(loc.shape[1:], f32)
    order = range(n - 1, -1, -1) if backward else range(n)
    for c in order:
        out[c] = state.astype(bf16)
        state = decay[c, 0:1, :] * state + loc[c].astype(f32)


def layer_kernel(
    nx,
    nz,
    ny,
    x_hbm,
    g_hbm,
    ids_hbm,
    prob_hbm,
    counts_hbm,
    u_hbm,
    b_hbm,
    c_hbm,
    ld_hbm,
    wg_hbm,
    wu_hbm,
    wd_hbm,
    w_hbm,
    out_ref,
    scan_ref,
    in_ref,
    out_map_ref,
    x_ref,
    g_ref,
    ids_ref,
    prob_ref,
    counts_ref,
    u_ref,
    b_ref,
    c_ref,
    ld_ref,
    er_ref,
    tail_ref,
    ut_ref,
    decay_ref,
    mix_ref,
    before_ref,
    tot_ref,
    wg,
    wu,
    wd,
    send,
    inbuf,
    part,
    precv,
    rsum,
    gall,
    eg,
    ret,
    pick,
    st_send,
    st_recv,
    back_send,
    tot_send,
    w,
    ya,
    xa,
    hsend,
    hrecv,
    intra,
    gst_send,
    gst_recv,
    gback_send,
    after,
    wsem,
    isem,
    psem,
    ssem,
    gsem,
    fsem,
    rsem,
    sem_s,
    sem_t,
    sem_b,
    usem,
    dsem,
    ysem,
    xsem,
    hfsem,
    hsem,
    gsem_s,
    gsem_b,
    lsem,
    osem,
):
    n = nx * nz
    me = lax.axis_index("ctx")
    x, z = me // nz, lax.rem(me, nz)
    t = lax.axis_index("tp")
    y, k = t // 2, lax.rem(t, 2)
    sib = y * 2 + (1 - k)
    y_up, y_dn, y_op = lax.rem(y + 1, ny), lax.rem(y + ny - 1, ny), lax.rem(y + 2, ny)
    up, dn = y_up * 2 + k, y_dn * 2 + k

    def ahead(dx, dz):
        return lax.rem(x + dx, nx) * nz + lax.rem(z + dz, nz)

    def behind(dx, dz):
        return lax.rem(x - dx + nx, nx) * nz + lax.rem(z - dz + nz, nz)

    def offset(s, i):
        j = i // nx
        dz = jnp.where(j == 0, s + 1, jnp.where(s == nz // 2 - 1, 0, nz - 1 - s))
        return lax.rem(i, nx), dz

    def target(s, i):
        return ahead(*offset(s, i))

    def origin(s, i):
        return behind(*offset(s, i))

    per = 2 * nx
    stages = nz // 2
    own = (stages - 1, nx)

    cols, tok = x_hbm.shape
    hidden = wg.shape[1]
    cut = wd_hbm.shape[0] // 128 * 128
    loads = [
        pltpu.make_async_copy(wg_hbm, wg.at[pl.ds(0, cols)], wsem.at[0]),
        pltpu.make_async_copy(wu_hbm, wu.at[pl.ds(0, cols)], wsem.at[1]),
        pltpu.make_async_copy(wd_hbm.at[pl.ds(0, cut)], wd.at[pl.ds(0, cut)], wsem.at[2]),
        pltpu.make_async_copy(
            wd_hbm.at[pl.ds(cut, cols - cut)], wd.at[pl.ds(cols, cols - cut)], wsem.at[3]
        ),
    ]
    small = [
        pltpu.make_async_copy(src, dst, lsem.at[i])
        for i, (src, dst) in enumerate(
            (
                (ids_hbm, ids_ref),
                (counts_hbm, counts_ref),
                (x_hbm, x_ref),
                (g_hbm, g_ref),
                (prob_hbm, prob_ref),
                (ld_hbm, ld_ref),
                (u_hbm, u_ref),
                (b_hbm, b_ref),
                (c_hbm, c_ref),
            )
        )
    ]
    for load in small:
        load.start()
    own_w = pltpu.make_async_copy(w_hbm, w.at[z], wsem.at[4])
    own_w.start()
    for load in loads:
        load.start()
    hello_ctx(n, me)
    hello_tp((sib, up, dn))
    for load in small[0:2]:
        load.wait()

    experts = counts_ref.shape[1]
    cap = inbuf.shape[2]
    slots = experts * cap
    rest = cols - cut
    full = cut + 128
    ids = ids_ref[...]
    names = lax.broadcasted_iota(i32, (experts, tok), 0)
    m0 = ids[0:1, :] == names
    m1 = ids[1:2, :] == names
    member = jnp.where(m0, 1.0, 0.0) + jnp.where(m1, 1.0, 0.0)
    t_row = lax.broadcasted_iota(i32, (tok, tok), 0)
    t_col = lax.broadcasted_iota(i32, (tok, tok), 1)
    rank = mm(member.astype(bf16), jnp.where(t_row < t_col, 1.0, 0.0).astype(bf16))
    e_row = lax.broadcasted_iota(i32, (experts, experts), 0)
    e_col = lax.broadcasted_iota(i32, (experts, experts), 1)
    limit = jnp.sum(
        jnp.where(e_row == e_col, counts_ref[...].astype(f32), 0.0), axis=1, keepdims=True
    )
    slot = jnp.where(rank < limit, rank + (names * cap).astype(f32), -1.0)
    place = lax.broadcasted_iota(i32, (slots, tok), 0).astype(f32)
    p0 = jnp.where(place == jnp.sum(jnp.where(m0, slot, 0.0), 0, keepdims=True), 1.0, 0.0)
    p1 = jnp.where(place == jnp.sum(jnp.where(m1, slot, 0.0), 0, keepdims=True), 1.0, 0.0)
    both = (p0 + p1).astype(bf16)
    pick[...] = both

    pl.semaphore_wait(pltpu.get_barrier_semaphore(), n - 1 + 3)
    mid = w.shape[2] // 2
    last_hop = nz // 2 - 1

    def w_part(hf, j, block, upward):
        if j < last_hop:
            return w.at[block, :, pl.ds(hf * mid, mid)]
        return w.at[block, :, pl.ds(hf * mid + (0 if upward else mid // 2), mid // 2)]

    def w_copy(hf, j, upward):
        if upward:
            block, to, sem = lax.rem(z - j + nz, nz), ahead(0, 1), usem
        else:
            block, to, sem = lax.rem(z + j, nz), behind(0, 1), dsem
        at = w_part(hf, j, block, upward)
        return remote(at, at, sem.at[0, hf, j], sem.at[1, hf, j], "ctx", to)

    def w_landed(hf, j):
        for upward, sem in ((True, usem), (False, dsem)):
            block = lax.rem(z - j - 1 + nz, nz) if upward else lax.rem(z + j + 1, nz)
            at = w_part(hf, j, block, upward)
            remote(at, at, sem.at[0, hf, j], sem.at[1, hf, j], "ctx", ahead(0, 1)).wait_recv()

    def w_hop(hf, j):
        if j:
            w_landed(hf, j - 1)
        w_copy(hf, j, True).start()
        w_copy(hf, j, False).start()

    for load in small[2:]:
        load.wait()
    grad = g_ref[...].astype(f32)
    prob = prob_ref[...]
    scaled = jnp.concatenate(
        [(prob[0:1, :] * grad).astype(bf16), (prob[1:2, :] * grad).astype(bf16)], axis=1
    )
    pair = jnp.concatenate([p0.astype(bf16), p1.astype(bf16)], axis=1)
    sel_x = mm(both, x_ref[...], 1, 1)
    sel_g = mm(pair, scaled, 1, 1)
    send[:, :, 0:cut] = sel_x[:, 0:cut].astype(bf16).reshape(experts, cap, cut)
    send[:, :, cut : 2 * cut] = sel_g[:, 0:cut].astype(bf16).reshape(experts, cap, cut)
    last = jnp.concatenate(
        [sel_x[:, cut:], sel_g[:, cut:], jnp.zeros((slots, 128 - 2 * rest), f32)], axis=1
    )
    send[:, :, 2 * cut :] = last.astype(bf16).reshape(experts, cap, 128)

    def in_copy(s, j):
        to = target(s, j)
        at = 2 * s + j // (per // 2)
        return remote(send.at[to], inbuf.at[s, j], isem.at[2 * stages], isem.at[at], "ctx", to)

    def post(i, _):
        s, j = i // per, lax.rem(i, per)

        @pl.when(i != own[0] * per + own[1])
        def _():
            in_copy(s, j).start()

        return 0

    lax.fori_loop(0, per, post, 0)
    inbuf[own] = send[me]

    heads = ld_ref.shape[0]
    width = u_ref.shape[1]
    log = ld_ref[...]
    upto = jnp.where(t_row >= t_col, 1.0, 0.0)
    run = mm(upto, log, 1, 1, precision=HIGHEST)
    run_t = mm(log, upto, 1, 1, precision=HIGHEST)
    total = run[tok - 1 : tok, :]
    tail_x = spread(jnp.exp(total - run), width)
    tail_ref[...] = tail_x
    ut = (u_ref[...].astype(f32) * tail_x).astype(bf16)
    ut_ref[...] = ut
    st_send[...] = mm(ut, b_ref[...], 0, 0).astype(bf16).reshape(st_send.shape)
    tot_send[...] = jnp.broadcast_to(
        jnp.concatenate([total, jnp.zeros((1, tot_send.shape[2] - heads), f32)], axis=1)[None],
        tot_send.shape,
    )
    exchange(n, me, tot_send, tot_ref, sem_t, "start")
    tot_ref[me] = tot_send[me]

    wg[pl.ds(cols, 128 - rest), :] = jnp.zeros((128 - rest, hidden), bf16)
    wu[pl.ds(cols, 128 - rest), :] = jnp.zeros((128 - rest, hidden), bf16)
    wd[pl.ds(cut, rest), :] = jnp.zeros((rest, hidden), bf16)
    wd[pl.ds(cols + rest, 128 - 2 * rest), :] = jnp.zeros((128 - 2 * rest, hidden), bf16)
    for load in loads:
        load.wait()

    er_ref[...] = spread(jnp.exp(run), width)
    affinity = mm(c_ref[...], b_ref[...], 1, 1)
    for h in range(heads):
        gap = run[:, h : h + 1] - run_t[h : h + 1, :]
        decay = jnp.where(t_row >= t_col, jnp.exp(jnp.where(t_row >= t_col, gap, 0.0)), 0.0)
        decay_ref[h] = decay.astype(bf16)
        mix_ref[h] = (decay * affinity).astype(bf16)

    half = per // 2 * cap
    mine, other = pl.multiple_of(k * half, cap), pl.multiple_of((1 - k) * half, cap)

    def pair_copy(s, p):
        return remote(
            part.at[s, p, pl.ds(other, half)],
            precv.at[s, p],
            osem.at[0],
            psem.at[s, p],
            "tp",
            sib,
        )

    side = hidden // 2
    lows, highs = pl.ds(0, side), pl.ds(side, side)

    def chunk(dz):
        return pl.ds(pl.multiple_of(mine + dz * cap, cap), cap)

    def sum_copy(s, i):
        src = (
            part.at[s, :, chunk(y_op), lows],
            part.at[s, :, chunk(y_op), highs],
            part.at[s, :, chunk(y_up), highs],
            part.at[s, :, chunk(y_dn), lows],
            rsum.at[s, 6],
            rsum.at[s, 7],
        )[i]
        return remote(
            src, rsum.at[s, i], osem.at[1], ssem.at[s, i], "tp", (up, dn)[i % 2]
        )

    def grads_at(s, core, dz):
        return gall.at[s, pl.ds(pl.multiple_of(core * half + dz * cap, cap), cap)]

    froms = (y_dn, y_up, y_op)

    def grad_copy(s, i, dz):
        at = gall.at[s, chunk(dz)]
        if i >= 2:
            at = gall.at[s, chunk(dz), pl.ds((i - 2) * hidden, hidden)]
        return remote(at, at, osem.at[2], gsem.at[s, i], "tp", (up, dn)[i % 2])

    def fwd_copy(s, i, core, dz):
        at = grads_at(s, core, dz)
        return remote(at, at, osem.at[3], fsem.at[s, i], "tp", sib)

    def landed(s, part_at, lo, count):
        remote(
            send.at[pl.ds(0, count)],
            inbuf.at[s, pl.ds(lo, count)],
            isem.at[2 * stages],
            isem.at[2 * s + part_at],
            "ctx",
            ahead(0, 1),
        ).wait_recv()

    def first(s):
        landed(s, 0, 0, nx)

        @pl.when(s == 0)
        def _():
            lax.fori_loop((s + 1) * per, (s + 2) * per, post, 0)

        @pl.when(s < stages - 1)
        def _():
            landed(s, 1, nx, nx)

        @pl.when(s == stages - 1)
        def _():
            landed(s, 1, nx + 1, nx - 1)

        rows = inbuf[s].reshape(per * cap, 2 * cut + 128)
        lasts = rows[:, 2 * cut :]
        for p, w in enumerate((wg, wu, wd)):
            lo = 0 if p < 2 else cut
            got = mm(rows[:, lo : lo + cut], w[0:cut, :]) + mm(lasts, w[cut:full, :])
            part[s, p] = got.astype(bf16)
            pair_copy(s, p).start()

    def second(s):
        for p in range(3):
            pair_copy(s, p).wait_recv()
            at = pl.ds(mine, half)
            part[s, p, at] = (part[s, p, at].astype(f32) + precv[s, p].astype(f32)).astype(bf16)
        for i in range(4):
            sum_copy(s, i).start()

    def relay(s):
        for i, (dz, at) in enumerate(((y_up, lows), (y_dn, highs))):
            sum_copy(s, i).wait_recv()
            rsum[s, 6 + i] = (
                part[s, :, chunk(dz), at].astype(f32) + rsum[s, i].astype(f32)
            ).astype(bf16)
            sum_copy(s, 4 + i).start()

    def third(s):
        for i in range(2, 6):
            sum_copy(s, i).wait_recv()
        for e, at, near, far in ((0, lows, 3, 4), (1, highs, 2, 5)):
            total = (
                part[s, :, chunk(y), at].astype(f32)
                + rsum[s, near].astype(f32)
                + rsum[s, far].astype(f32)
            )
            gate, upv, back = total[0], total[1], total[2]
            sigma = 1.0 / (1.0 + jnp.exp(-gate))
            lo, hi = pl.ds(e * side, side), pl.ds(hidden + e * side, side)
            gall[s, chunk(y), lo] = (back * upv * sigma * (1.0 + gate * (1.0 - sigma))).astype(bf16)
            gall[s, chunk(y), hi] = (back * gate * sigma).astype(bf16)
        for i in range(2):
            grad_copy(s, i, y).start()
        fwd_copy(s, 3, k, y).start()

    def fourth(s):
        for i in range(2):
            grad_copy(s, i, froms[i]).wait_recv()
            grad_copy(s, 2 + i, froms[i]).start()
            fwd_copy(s, i, k, froms[i]).start()

    def gathered(s):
        for i in range(2):
            grad_copy(s, 2 + i, y_op).wait_recv()
        fwd_copy(s, 2, k, y_op).start()

    def fifth(s):
        for i in range(3):
            fwd_copy(s, i, 1 - k, froms[i]).wait_recv()
        fwd_copy(s, 3, 1 - k, y).wait_recv()
        grad = mm(gall[s, :, 0:hidden], wg[0:cols, :], 1, 1) + mm(
            gall[s, :, hidden : 2 * hidden], wu[0:cols, :], 1, 1
        )
        eg[s] = grad.astype(bf16).reshape(per, cap, cols)

        def one(i, _):
            @pl.when(s * per + i != own[0] * per + own[1])
            def _():
                back_copy(s, i).start()

            return 0

        lax.fori_loop(0, per, one, 0)

    def back_copy(s, i):
        return remote(eg.at[s, i], ret.at[me], rsem.at[0], rsem.at[1], "ctx", origin(s, i))

    def stage(s, _):
        second(s)

        @pl.when(s > 0)
        def _():
            fourth(s - 1)

        @pl.when(s > 1)
        def _():
            fifth(s - 2)

        relay(s)

        @pl.when(s == 0)
        def _():
            lax.fori_loop(2 * per, 3 * per, post, 0)

        @pl.when(s > 0)
        def _():
            gathered(s - 1)

        @pl.when(s == 1)
        def _():
            lax.fori_loop(3 * per, 4 * per, post, 0)

        @pl.when(s + 1 < stages)
        def _():
            first(s + 1)

        @pl.when(s == stages - 2)
        def _():
            w_hop(0, 0)

        @pl.when(s == stages - 1)
        def _():
            fifth(s - 1)
            w_hop(0, 1)

        third(s)
        return 0

    own_w.wait()
    first(0)
    lax.fori_loop(0, stages, stage, 0)
    fourth(stages - 1)
    gathered(stages - 1)
    fifth(stages - 1)
    w_hop(1, 0)
    w_hop(0, 2)
    ret[me] = eg[own]

    others = pl.ds(0, n - 1)
    returned = remote(
        ret.at[others], ret.at[others], rsem.at[0], rsem.at[1], "ctx", ahead(0, 1)
    )
    returned.wait_recv()
    entries = ret[...].reshape(slots, cols)
    input_grad = g_ref[...].astype(f32) + mm(entries, pick[...], 0, 0)
    ya[y] = input_grad.reshape(nz // 2, cols // (nz // 2), tok).astype(bf16)

    def y_copy(i, dz):
        first_half = (0, 1, 1, 0, 0, 1)[i]
        at = ya.at[dz, pl.ds(first_half * (nz // 4), nz // 4)]
        return remote(at, at, ysem.at[0, i], ysem.at[1, i], "tp", (up, dn)[i % 2])

    def x_copy(place, source):
        return remote(
            ya.at[place],
            xa.at[source, k],
            xsem.at[0, place],
            xsem.at[1, source],
            "ctx",
            place * nz + z,
        )

    def f_copy(source, core):
        at = xa.at[source, core]
        return remote(at, at, hfsem.at[0, source], hfsem.at[1, source], "tp", sib)

    def pass_on(place):
        @pl.when(place != x)
        def _():
            x_copy(place, x).start()

        @pl.when(place == x)
        def _():
            xa[x, k] = ya[place]
            f_copy(x, k).start()

    for i in range(4):
        y_copy(i, y).start()
    pass_on(y)
    out_ref[...] = input_grad.astype(bf16)
    for i in range(2):
        y_copy(i, froms[i]).wait_recv()
        y_copy(4 + i, froms[i]).start()
    w_hop(1, 1)
    for i in range(2):
        y_copy(2 + i, froms[i]).wait_recv()
        pass_on(froms[i])
    w_hop(0, 3)
    for i in range(2):
        y_copy(4 + i, y_op).wait_recv()
    pass_on(y_op)

    def x_at(d):
        return lax.rem(x + d, nx)

    wide = width // 2
    quarter = wide // 2

    def product(source, hf):
        total = jnp.zeros((tok, wide), f32)
        for b in range(nz):
            part_x = xa[source, b // (nz // 2), b % (nz // 2)]
            total = total + mm(part_x, w[b, :, pl.ds(hf * wide, wide)], 0, 0)
        return total

    x_up, x_dn, x_op = x_at(1), x_at(nx - 1), x_at(2)
    def quart(hf, q):
        return pl.ds(hf * wide + q * quarter, quarter)

    def h_copy(hf, i):
        src, q = ((0, 0), (0, 1), (1, 1), (2, 0), (1, 0), (2, 1))[i]
        return remote(
            hsend.at[src, :, quart(hf, q)],
            hrecv.at[hf, i],
            hsem.at[0, hf, i],
            hsem.at[1, hf, i],
            "ctx",
            (x_up, x_dn)[i % 2] * nz + z,
        )

    order = [2, 1, nx - 1]
    w_hop(1, 2)
    exchange(n, me, st_send, st_recv, sem_s, "start")
    st_recv[me] = st_send[me]
    for d in order:
        source = x_at(d)
        x_copy(x, source).wait_recv()
        f_copy(source, k).start()
    size = width // heads

    def h_send(hf):
        w_landed(hf, 3)
        for i, d in enumerate(order):
            source = x_at(d)
            if hf == 0:
                f_copy(source, 1 - k).wait_recv()
            hsend[i, :, pl.ds(hf * wide, wide)] = product(source, hf).astype(bf16)
            if i == 0:
                h_copy(hf, 0).start()
                h_copy(hf, 1).start()
            else:
                h_copy(hf, 1 + i).start()

    def h_relay(hf):
        for i in range(2):
            h_copy(hf, i).wait_recv()
            at = quart(hf, i)
            hsend[1 + i, :, at] = (
                hsend[1 + i, :, at].astype(f32) + hrecv[hf, i].astype(f32)
            ).astype(bf16)
            h_copy(hf, 4 + i).start()

    h_send(0)
    w_hop(1, 3)
    h_relay(0)
    f_copy(x, 1 - k).wait_recv()
    wholes = [product(x, 0)]
    exchange(n, me, tot_send, tot_ref, sem_t, "wait")
    exchange(n, me, st_send, st_recv, sem_s, "wait")
    scan_states(n, me, st_recv, back_send, tot_ref, size, 0, False)
    exchange(n, me, back_send, before_ref, sem_b, "start")
    before_ref[me] = back_send[me]
    h_send(1)

    weights = jnp.zeros((tok, tok), f32)
    some = heads // 2
    weighted = []
    for hf in range(2):
        for i in range(2, 6):
            h_copy(hf, i).wait_recv()
        grad = (
            wholes[hf]
            + jnp.concatenate(
                [
                    hrecv[hf, 4].astype(f32) + hrecv[hf, 3].astype(f32),
                    hrecv[hf, 2].astype(f32) + hrecv[hf, 5].astype(f32),
                ],
                axis=1,
            )
        ).astype(bf16)
        ge = (grad.astype(f32) * er_ref[:, hf * wide : (hf + 1) * wide]).astype(bf16)
        weighted.append(ge)
        gst_send[hf] = mm(ge, c_ref[...], 0, 0).astype(bf16).reshape(gst_send.shape[1:])
        exchange(n, me, gst_send.at[hf], gst_recv.at[hf], gsem_s.at[hf], "start")
        gst_recv[hf, me] = gst_send[hf, me]
        if hf == 0:
            h_relay(1)
            wholes.append(product(x, 1))
        for j in range(some):
            h = hf * some + j
            gh = grad[:, j * size : (j + 1) * size]
            uh = u_ref[:, h * size : (h + 1) * size]
            weights = weights + decay_ref[h].astype(f32) * mm(gh, uh, 1, 1)
            intra[:, h * size : (h + 1) * size] = mm(mix_ref[h], gh, 0, 0)
    weights = weights.astype(bf16)
    state = b_ref.shape[1]

    for hf in range(2):
        exchange(n, me, gst_send.at[hf], gst_recv.at[hf], gsem_s.at[hf], "wait")
        scan_states(
            n, me, gst_recv.at[hf], gback_send.at[hf], tot_ref, size, hf * some, True
        )
        exchange(n, me, gback_send.at[hf], after.at[hf], gsem_b.at[hf], "start")
        after[hf, me] = gback_send[hf, me]

    exchange(n, me, back_send, before_ref, sem_b, "wait")
    before = before_ref[...].reshape(-1, state)
    out_map_ref[...] = (
        mm(weights, b_ref[...])
        + mm(weighted[0], before[0 : some * size])
        + mm(weighted[1], before[some * size :])
    )
    in_part = mm(weights, c_ref[...], 0, 0)

    for i, sent in enumerate(
        (
            part.at[:, :, pl.ds(other, half)],
            rsum.at[:, pl.ds(0, 6)],
            gall.at[:, pl.ds(0, 3 * cap)],
            gall.at[:, pl.ds(mine, half)],
        )
    ):
        remote(sent, sent, osem.at[i], psem.at[0, 0], "tp", sib).wait_send()

    remote(
        send.at[others],
        send.at[others],
        isem.at[2 * stages],
        isem.at[0],
        "ctx",
        ahead(0, 1),
    ).wait_send()
    returned.wait_send()
    for hf in range(2):
        for j in range(nz // 2):
            w_copy(hf, j, True).wait_send()
            w_copy(hf, j, False).wait_send()
    for i in range(6):
        y_copy(i, y).wait_send()
    for d in order:
        x_copy(x_at(d), x).wait_send()
    for hf in range(2):
        for i in range(6):
            h_copy(hf, i).wait_send()
    for d in range(nx):
        f_copy(x_at(d), k).wait_send()

    for hf in range(2):
        exchange(n, me, gback_send.at[hf], after.at[hf], gsem_b.at[hf], "wait")
        later = after[hf].reshape(-1, state)
        at = pl.ds(hf * wide, wide)
        in_part = in_part + mm(ut_ref[:, at], later)
        scan_ref[:, at] = (
            intra[:, at] + tail_ref[:, at] * mm(b_ref[...], later, 1, 1)
        ).astype(bf16)
    in_ref[...] = in_part


def layer(
    sizes, moe_t, grad_t, ids_t, prob_t, counts, ssd_input, in_map, out_map, log_t, wg, wu, wd, w
):
    nx, nz, ny = sizes
    n = nx * nz
    cols, tok = moe_t.shape
    experts = counts.shape[1]
    cap = 2 * tok * ids_t.shape[0] // experts
    heads = log_t.shape[0]
    width = ssd_input.shape[1]
    state = in_map.shape[1]
    hidden = wg.shape[1]
    part = width // n
    cut = cols // 128 * 128
    full = cut + 128
    per, stages = 2 * nx, nz // 2
    rows = per * cap
    small = jax.ShapeDtypeStruct((tok, state), f32)
    halves = pltpu.VMEM((2, n, part // 2, state), bf16)
    states = pltpu.VMEM((n, part, state), bf16)
    pair = DMA((2,))
    return pl.pallas_call(
        functools.partial(layer_kernel, nx, nz, ny),
        out_shape=(
            jax.ShapeDtypeStruct((cols, tok), bf16),
            jax.ShapeDtypeStruct((tok, width), bf16),
            small,
            small,
        ),
        in_specs=[HBM] * 13,
        out_specs=[VMEM] * 4,
        scratch_shapes=[
            pltpu.VMEM((cols, tok), bf16),
            pltpu.VMEM((cols, tok), bf16),
            pltpu.VMEM(ids_t.shape, i32),
            pltpu.VMEM(prob_t.shape, f32),
            pltpu.VMEM(counts.shape, i32),
            pltpu.VMEM((tok, width), bf16),
            pltpu.VMEM((tok, state), bf16),
            pltpu.VMEM((tok, state), bf16),
            pltpu.VMEM(log_t.shape, f32),
            pltpu.VMEM((tok, width), f32),
            pltpu.VMEM((tok, width), f32),
            pltpu.VMEM((tok, width), bf16),
            pltpu.VMEM((heads, tok, tok), bf16),
            pltpu.VMEM((heads, tok, tok), bf16),
            states,
            pltpu.VMEM((n, 1, 128), f32),
            pltpu.VMEM((full, hidden), bf16),
            pltpu.VMEM((full, hidden), bf16),
            pltpu.VMEM((full, hidden), bf16),
            pltpu.VMEM((n, cap, 2 * cut + 128), bf16),
            pltpu.VMEM((stages, per, cap, 2 * cut + 128), bf16),
            pltpu.VMEM((stages, 3, rows, hidden), bf16),
            pltpu.VMEM((stages, 3, rows // 2, hidden), bf16),
            pltpu.VMEM((stages, 8, 3, cap, hidden // 2), bf16),
            pltpu.VMEM((stages, rows, 2 * hidden), bf16),
            pltpu.VMEM((stages, per, cap, cols), bf16),
            pltpu.VMEM((n, cap, cols), bf16),
            pltpu.VMEM((experts * cap, tok), bf16),
            states,
            states,
            states,
            pltpu.VMEM((n, 1, 128), f32),
            pltpu.VMEM((nz, w.shape[0], width), bf16),
            pltpu.VMEM((ny, nz // 2, w.shape[0], tok), bf16),
            pltpu.VMEM((nx, 2, nz // 2, w.shape[0], tok), bf16),
            pltpu.VMEM((3, tok, width), bf16),
            pltpu.VMEM((2, 6, tok, width // 4), bf16),
            pltpu.VMEM((tok, width), f32),
            halves,
            halves,
            halves,
            halves,
            DMA((5,)),
            DMA((2 * stages + 1,)),
            DMA((stages, 3)),
            DMA((stages, 6)),
            DMA((stages, 4)),
            DMA((stages, 4)),
            pair,
            pair,
            pair,
            pair,
            DMA((2, 2, nz // 2)),
            DMA((2, 2, nz // 2)),
            DMA((2, 6)),
            DMA((2, nx)),
            DMA((2, nx)),
            DMA((2, 2, 6)),
            DMA((2, 2)),
            DMA((2, 2)),
            DMA((9,)),
            DMA((4,)),
        ],
        compiler_params=pltpu.CompilerParams(
            collective_id=0, has_side_effects=True, vmem_limit_bytes=56 * 2**20
        ),
        name="layer",
    )(moe_t, grad_t, ids_t, prob_t, counts, ssd_input, in_map, out_map, log_t, wg, wu, wd, w)


def keep_kernel(*refs):
    count = (len(refs) - 1) // 3
    given, kept, held, sems = refs[:count], refs[count : 2 * count], refs[2 * count : -1], refs[-1]
    loads = [pltpu.make_async_copy(a, b, sems.at[0, i]) for i, (a, b) in enumerate(zip(given, held))]
    stores = [pltpu.make_async_copy(a, b, sems.at[1, i]) for i, (a, b) in enumerate(zip(held, kept))]
    for load in loads:
        load.start()
    for load, store in zip(loads, stores):
        load.wait()
        store.start()
    for store in stores:
        store.wait()


def keep(arrays):
    return pl.pallas_call(
        keep_kernel,
        out_shape=tuple(jax.ShapeDtypeStruct(a.shape, a.dtype) for a in arrays),
        in_specs=[HBM] * len(arrays),
        out_specs=[HBM] * len(arrays),
        scratch_shapes=[pltpu.VMEM(a.shape, a.dtype) for a in arrays] + [DMA((2, len(arrays)))],
        compiler_params=pltpu.CompilerParams(vmem_limit_bytes=60 * 2**20),
        name="keep",
    )(*arrays)


def body(
    moe_input,
    out_grad,
    route_prob,
    route_ids,
    route_counts,
    w_gate,
    w_up,
    w_down,
    out_weight,
    ssd_input,
    input_map,
    output_map,
    log_decay,
):
    n = lax.axis_size("ctx")
    ny = lax.axis_size("tp") // 2
    nx = ny
    nz = n // nx
    outs = layer(
        (nx, nz, ny),
        moe_input.T,
        out_grad.T,
        route_ids.T,
        route_prob.T,
        route_counts,
        ssd_input,
        input_map,
        output_map,
        log_decay.T,
        w_gate[0],
        w_up[0],
        w_down[0].T,
        out_weight,
    )
    grad_t, scan_grad, in_map_grad, out_map_grad = keep(outs)
    return (grad_t.T, scan_grad, in_map_grad, out_map_grad)


def solution(mesh):
    in_specs = (
        P("ctx", "tp"),
        P("ctx", "tp"),
        P("ctx", None),
        P("ctx", None),
        P("ctx", None),
        P("ctx", "tp", None),
        P("ctx", "tp", None),
        P("ctx", None, "tp"),
        P("ctx", "tp"),
        P("ctx", "tp"),
        P("ctx", "tp"),
        P("ctx", "tp"),
        P("ctx", "tp"),
    )
    out_specs = (P("ctx", "tp"), P("ctx", "tp"), P("ctx", "tp"), P("ctx", "tp"))
    return jax.shard_map(body, mesh=mesh, in_specs=in_specs, out_specs=out_specs, check_vma=False)
```
